128 devices in a mesh: dp: 4 (over x_lo, core), space: 32 (over z, x_hi, y).
Axes of the slice: x: 4 (x_hi: 2, x_lo: 2; x = x_hi * 2 + x_lo), y: 4, z: 4, core: 2. Of those that a mesh axis runs over, the one named last changes fastest.
Arguments:
- volumes: bfloat16 [64, 8, 64, 512], P('space', 'dp'), may hold values from -6 to 6
- cotangent: bfloat16 [32, 8, 256, 128], P('space', 'dp'), may hold values from -0.119628906 to 0.119628906
- conv4_weight: bfloat16 [27, 128, 64], replicated, may hold values from -0.15625 to 0.15625
- conv5_weight: bfloat16 [27, 256, 128], replicated, may hold values from -0.109375 to 0.109375
Outputs:
- output5: bfloat16 [32, 8, 256, 128], P('space', 'dp')
- weight4: float32 [27, 128, 64], replicated
- weight5: float32 [27, 256, 128], P(None, None, 'space')
The draws below stay inside these ranges and needn't reach their ends.
All inputs are finite; a program needn't handle non-finite values.
Results may differ from the reference program's by a relative error of at most 0.0064.
Values may be sent and summed in bfloat16 or wider, within the bound.
No kernel may reach another device: no remote copies, remote signals or barrier semaphores. Data moves between devices by JAX's collectives and lax.ppermute only.
A program may use at most 128 MiB of HBM per device.

```python
import jax
import jax.numpy as jnp
from jax import lax

C4 = 64
F4 = 128
F5 = 256
DEPTH = 64
HEIGHT = 32
WIDTH = 16
VOLS = 8
PLANE4 = 512
PLANE5 = 128
D5 = 32


def levels(own_key, shape, cuts, smallest, top_value):
    gain, own = 1.0, jax.random.fold_in(own_key, 6)
    for dim, shards_of in cuts:
        heights = jnp.exp(jax.random.uniform(jax.random.fold_in(own, dim), (shards_of,), jnp.float32, smallest / len(cuts), top_value / len(cuts)))
        gain = gain * jnp.repeat(heights, shape[dim] // shards_of).reshape([-1 if axis == dim else 1 for axis in range(len(shape))])
    return gain


def noise(stream_key, extent, scale, reach, split=(), kind=jnp.bfloat16):
    values = scale * jax.random.normal(stream_key, extent, jnp.float32)
    if split:
        values = values * levels(stream_key, extent, split, -0.22, 0.18)
    return jnp.clip(values, -reach, reach).astype(kind)


def setup_inputs(seed: int = 0) -> dict:
    seeds = jax.random.split(jax.random.key(seed), 5)
    return {
        "volumes": noise(seeds[0], (DEPTH, VOLS, C4, PLANE4), 1.0, 6.0, ((0, 32), (1, 4))),
        "cotangent": noise(seeds[1], (D5, VOLS, F5, PLANE5), 0.02, 0.119628906, ((0, 32), (1, 4))),
        "conv4_weight": noise(seeds[2], (27, F4, C4), (27 * C4) ** -0.5, 0.15625),
        "conv5_weight": noise(seeds[3], (27, F5, F4), (27 * F4) ** -0.5, 0.109375),
    }


highest_prec = lax.Precision.HIGHEST

def plane_shift(values, b, e, row_len):
    length = values.shape[-1]
    margins = [(0, 0)] * (values.ndim - 1) + [(row_len + 1, row_len + 1)]
    padded = jnp.pad(values, margins)
    offset = row_len + 1 + b * row_len + e
    shifted = lax.slice_in_dim(padded, offset, offset + length, axis=values.ndim - 1)
    column = jnp.arange(length) % row_len
    keep_mask = ((column + e >= 0) & (column + e < row_len)).astype(values.dtype)
    return shifted * keep_mask

def plane_stack(values, row_len, chan_axis):
    return jnp.concatenate([plane_shift(values, b, e, row_len) for b in (-1, 0, 1) for e in (-1, 0, 1)], axis=chan_axis)

def arrange(weight):
    outer, inner = (weight.shape[1], weight.shape[2])
    return weight.reshape(3, 9, outer, inner).transpose(0, 2, 1, 3).reshape(3, outer, 9 * inner)

def unarrange(grad, inner):
    outer = grad.shape[1]
    return grad.reshape(3, outer, 9, inner).transpose(0, 2, 1, 3).reshape(27, outer, inner)

def flipped(weight):
    return weight[::-1].transpose(0, 2, 1)

def prepare(values, row_len):
    stacked = plane_stack(values.astype(jnp.float32), row_len, 1)
    return jnp.pad(stacked, ((1, 1), (0, 0), (0, 0)))

def convolve(stacked, arranged):
    planes = stacked.shape[0] - 2
    summed = jnp.zeros((planes, arranged.shape[1], stacked.shape[2]), jnp.float32)
    for a in range(3):
        summed = summed + jnp.einsum('fk,dkp->dfp', arranged[a], stacked[a:a + planes], precision=highest_prec)
    return summed

def weight_grad(grad, stacked, inner):
    planes = grad.shape[0]
    pieces = [jnp.einsum('dfp,dkp->fk', grad, stacked[a:a + planes], precision=highest_prec) for a in range(3)]
    return unarrange(jnp.stack(pieces), inner)

def silu_slope(values):
    sig = jax.nn.sigmoid(values)
    return sig * (1.0 + values * (1.0 - sig))

def one_volume(layer_in, cot_in, weight4, weight5):
    stacked4 = prepare(layer_in, WIDTH)
    preact4 = convolve(stacked4, arrange(weight4))
    activated = jax.nn.silu(preact4)
    planes = activated.shape[0]
    chans = activated.shape[1]
    blocks = activated.reshape(planes // 2, 2, chans, HEIGHT // 2, 2, WIDTH // 2, 2)
    inputs5 = lax.optimization_barrier(jnp.mean(blocks, axis=(1, 4, 6))).reshape(planes // 2, chans, -1)
    inputs5 = lax.optimization_barrier(inputs5.astype(jnp.bfloat16))
    stacked5 = prepare(inputs5, WIDTH // 2)
    preact5 = convolve(stacked5, arrange(weight5))
    output5 = jax.nn.silu(preact5).astype(jnp.bfloat16)
    grad_pre5 = lax.optimization_barrier((cot_in.astype(jnp.float32) * silu_slope(preact5)).astype(jnp.bfloat16))
    grad_in5 = convolve(prepare(grad_pre5, WIDTH // 2), arrange(flipped(weight5)))
    grad_in5 = lax.optimization_barrier(grad_in5.astype(jnp.bfloat16))
    spread = grad_in5.astype(jnp.float32).reshape(planes // 2, 1, chans, HEIGHT // 2, 1, WIDTH // 2, 1)
    spread = jnp.broadcast_to(spread, (planes // 2, 2, chans, HEIGHT // 2, 2, WIDTH // 2, 2)).reshape(planes, chans, -1) / 8.0
    grad_pre4 = lax.optimization_barrier((spread * silu_slope(preact4)).astype(jnp.bfloat16))
    weight4_grad = weight_grad(grad_pre4.astype(jnp.float32), stacked4, layer_in.shape[1])
    weight5_grad = weight_grad(grad_pre5.astype(jnp.float32), stacked5, chans)
    return (output5, weight4_grad, weight5_grad)

def reference(volumes, cotangent, conv4_weight, conv5_weight):
    weight4 = conv4_weight.astype(jnp.float32)
    weight5 = conv5_weight.astype(jnp.float32)

    def per_volume(slices):
        return one_volume(slices[0], slices[1], weight4, weight5)
    results = lax.map(per_volume, (jnp.moveaxis(volumes, 1, 0), jnp.moveaxis(cotangent, 1, 0)))
    output5 = jnp.moveaxis(results[0], 0, 1)
    return (output5, lax.optimization_barrier(jnp.sum(results[1], axis=0)), lax.optimization_barrier(jnp.sum(results[2], axis=0)))
```

```python
import jax
import jax.numpy as jnp
from jax import lax
from jax.experimental import pallas as pl
from jax.experimental.pallas import tpu as pltpu
from jax.sharding import PartitionSpec as P

HEIGHT = 32
WIDTH = 16
TAPS = tuple((b, e) for b in (-1, 0, 1) for e in (-1, 0, 1))
BF16 = jnp.bfloat16
F32 = jnp.float32
VMEM = pl.BlockSpec(memory_space=pltpu.VMEM)


def swap_pairs(count, phase):
    pairs = []
    for low in range(phase, count, 2):
        high = (low + 1) % count
        pairs += [(low, high), (high, low)]
    return pairs


def swapped(values, phase):
    return lax.ppermute(values, "space", swap_pairs(lax.axis_size("space"), phase))


def other_core(values):
    count = lax.axis_size("dp")
    return lax.ppermute(values, "dp", [(i, i ^ 1) for i in range(count)])


def neighbours(first, second):
    here = lax.axis_index("space")
    odd = here % 2 == 1
    below = jnp.where(odd, first, second)
    above = jnp.where(odd, second, first)
    below = jnp.where(here == 0, jnp.zeros_like(below), below)
    above = jnp.where(here == lax.axis_size("space") - 1, jnp.zeros_like(above), above)
    return below, above


def keep_mask(b, e, row_len, length):
    lane = lax.broadcasted_iota(jnp.int32, (1, length), 1)
    column = lane % row_len + e
    row = lane // row_len + b
    inside = (column >= 0) & (column < row_len) & (row >= 0) & (row < length // row_len)
    return inside.astype(F32)


def tap(values, b, e, row_len):
    length = values.shape[1]
    offset = b * row_len + e
    if offset == 0:
        return values
    return pltpu.roll(values, -offset % length, 1) * keep_mask(b, e, row_len, length)


def dot(left, right):
    return jnp.dot(left, right, preferred_element_type=F32)


def dot_rows(left, right):
    return lax.dot_general(left, right, (((1,), (1,)), ((), ())), preferred_element_type=F32)


def pool_matrix(fine_axis, shape):
    fine = lax.broadcasted_iota(jnp.int32, shape, fine_axis)
    coarse = lax.broadcasted_iota(jnp.int32, shape, 1 - fine_axis)
    owner = (fine // (2 * WIDTH)) * (WIDTH // 2) + (fine % WIDTH) // 2
    return (owner == coarse).astype(BF16)


def layer4_kernel(vol_ref, first_ref, second_ref, weight_ref, pooled_ref, slope_ref, stack_ref):
    chans, cells = vol_ref.shape[2], vol_ref.shape[3]
    rows = len(TAPS) * chans
    for n in range(2):
        below, above = neighbours(first_ref[n], second_ref[n])
        for j, plane in enumerate((below, vol_ref[0, n], vol_ref[1, n], above)):
            wide = plane.astype(F32)
            for t, (b, e) in enumerate(TAPS):
                stack_ref[pl.ds(j * rows + t * chans, chans), pl.ds(n * cells, cells)] = tap(
                    wide, b, e, WIDTH
                ).astype(BF16)
    pool = pool_matrix(0, (cells, cells // 4))
    for n in range(2):
        lanes = pl.ds(n * cells, cells)
        total = None
        for d in range(2):
            preact = dot(weight_ref[...], stack_ref[pl.ds(d * rows, 3 * rows), lanes])
            sig = jax.nn.sigmoid(preact)
            slope_ref[d, :, lanes] = sig * (1.0 + preact * (1.0 - sig)) * 0.125
            active = preact * sig
            total = active if total is None else total + active
        high = total.astype(BF16)
        low = (total - high.astype(F32)).astype(BF16)
        pooled = (dot(high, pool) + dot(low, pool)) * 0.125
        pooled_ref[:, pl.ds(n * cells // 4, cells // 4)] = pooled.astype(BF16)


def layer4(volumes, first, second, weight):
    vols, chans, cells = volumes.shape[1:]
    outer = weight.shape[0]
    return pl.pallas_call(
        layer4_kernel,
        out_shape=(
            jax.ShapeDtypeStruct((outer, vols * cells // 4), BF16),
            jax.ShapeDtypeStruct((2, outer, vols * cells), F32),
            jax.ShapeDtypeStruct((4 * len(TAPS) * chans, vols * cells), BF16),
        ),
        in_specs=[VMEM] * 4,
        out_specs=(VMEM, VMEM, VMEM),
        name="layer4",
    )(volumes, first, second, weight)


def spread_taps(planes, out_ref, row_len, cells, sign):
    chans = planes[0].shape[0]
    for j, plane in enumerate(planes):
        for n in range(plane.shape[1] // cells):
            wide = plane[:, n * cells : (n + 1) * cells].astype(F32)
            for t, (b, e) in enumerate(TAPS):
                out_ref[pl.ds((j * len(TAPS) + t) * chans, chans), pl.ds(n * cells, cells)] = tap(
                    wide, sign * b, sign * e, row_len
                ).astype(BF16)


def layer5_kernel(
    pooled_ref, first_ref, second_ref, weight_ref, cot_ref, out_ref, grad_ref, stack_ref
):
    below, above = neighbours(first_ref[...], second_ref[...])
    cells = cot_ref.shape[2]
    spread_taps((below, pooled_ref[...], above), stack_ref, WIDTH // 2, cells, 1)
    chans = pooled_ref.shape[0]
    preact = None
    for o in range(0, 27, 2):
        if o < 26:
            weight = jnp.concatenate([weight_ref[o], weight_ref[o + 1]], axis=1)
        else:
            weight = weight_ref[o]
        part = dot(weight, stack_ref[pl.ds(o * chans, weight.shape[1]), :])
        preact = part if preact is None else preact + part
    sig = jax.nn.sigmoid(preact)
    active = preact * sig
    slope = sig * (1.0 + preact * (1.0 - sig))
    for n in range(cot_ref.shape[0]):
        lanes = slice(n * cells, (n + 1) * cells)
        out_ref[n] = active[:, lanes].astype(BF16)
        grad_ref[:, lanes] = (cot_ref[n].astype(F32) * slope[:, lanes]).astype(BF16)


def layer5(pooled, first, second, weight, cot):
    vols, outer, cells = cot.shape
    return pl.pallas_call(
        layer5_kernel,
        out_shape=(
            jax.ShapeDtypeStruct((vols, outer, cells), BF16),
            jax.ShapeDtypeStruct((outer, vols * cells), BF16),
            jax.ShapeDtypeStruct((27 * pooled.shape[0], vols * cells), BF16),
        ),
        in_specs=[VMEM] * 5,
        out_specs=(VMEM, VMEM, VMEM),
        name="layer5",
    )(pooled, first, second, weight, cot)


def backward_kernel(
    grad_ref, first_ref, second_ref, back_ref, stack5_ref, stack4_ref, slope_ref,
    keep_ref, send_ref, spread_ref, acc_ref,
):
    core = lax.axis_index("dp") % 2
    grad = grad_ref[...]
    outer = grad.shape[0]
    half = outer // 2
    chans = back_ref.shape[1]
    cells = grad.shape[1] // 2
    top, bottom = grad[:half], grad[half:]
    ordered = jnp.concatenate(
        [jnp.where(core == 0, top, bottom), jnp.where(core == 0, bottom, top)], axis=0
    )
    for o in range(0, 27, 2):
        count = min(2, 27 - o)
        part = dot_rows(ordered, stack5_ref[pl.ds(o * chans, count * chans), :]).astype(BF16)
        for i in range(count):
            block = part[:, i * chans : (i + 1) * chans]
            for k in range(2):
                slot = 2 * (o + i) + k
                keep_ref[slot, pl.ds(0, 64), :] = block[k * 64 : (k + 1) * 64]
                send_ref[slot, pl.ds(0, 64), :] = block[half + k * 64 : half + (k + 1) * 64]
    below, above = neighbours(first_ref[...], second_ref[...])
    spread_taps((above, grad, below), spread_ref, WIDTH // 2, cells, -1)
    inward = None
    for o in range(27):
        part = dot(back_ref[o], spread_ref[pl.ds(o * outer, outer), :])
        inward = part if inward is None else inward + part
    inward = inward.astype(BF16)
    unpool = pool_matrix(1, (cells, 4 * cells))
    fine = jnp.concatenate(
        [dot(inward[:, n * cells : (n + 1) * cells], unpool) for n in range(2)], axis=1
    )
    grads = jnp.concatenate(
        [(fine * slope_ref[0]).astype(BF16), (fine * slope_ref[1]).astype(BF16)], axis=0
    )
    rows = stack4_ref.shape[0] // 4
    for j in range(4):
        plane = stack4_ref[pl.ds(j * rows, rows), :]
        if j == 0:
            acc_ref[pl.ds(0, rows), :] = dot_rows(plane, grads[:chans])
        elif j == 3:
            acc_ref[pl.ds(2 * rows, rows), :] += dot_rows(plane, grads[chans:])
        else:
            both = dot_rows(plane, grads)
            acc_ref[pl.ds(j * rows, rows), :] = both[:, :chans]
            acc_ref[pl.ds((j - 1) * rows, rows), :] += both[:, chans:]
    inner = rows // len(TAPS)
    quarter = inner // 4
    for o in range(27):
        for k in range(2):
            mine = pl.multiple_of(o * inner + core * (inner // 2) + k * quarter, quarter)
            theirs = pl.multiple_of(o * inner + (1 - core) * (inner // 2) + k * quarter, quarter)
            keep_ref[2 * o + k, pl.ds(64, quarter), :] = acc_ref[pl.ds(mine, quarter), :].astype(BF16)
            send_ref[2 * o + k, pl.ds(64, quarter), :] = acc_ref[pl.ds(theirs, quarter), :].astype(BF16)
    for slot in range(54, 64):
        keep_ref[slot] = jnp.zeros(keep_ref.shape[1:], BF16)
        send_ref[slot] = jnp.zeros(send_ref.shape[1:], BF16)


def backward(grad, first, second, back, stack5, stack4, slope):
    outer, lanes = grad.shape
    return pl.pallas_call(
        backward_kernel,
        out_shape=(
            jax.ShapeDtypeStruct((64, 80, 128), BF16),
            jax.ShapeDtypeStruct((64, 80, 128), BF16),
        ),
        in_specs=[VMEM] * 7,
        out_specs=(VMEM, VMEM),
        scratch_shapes=[
            pltpu.VMEM((27 * outer, lanes), BF16),
            pltpu.VMEM((3 * stack4.shape[0] // 4, back.shape[1]), F32),
        ],
        name="backward",
    )(grad, first, second, back, stack5, stack4, slope)


def per_device(volumes, cotangent, conv4_weight, conv5_weight):
    space = lax.axis_index("space")
    odd = space % 2
    first4 = swapped(lax.dynamic_index_in_dim(volumes, 1 - odd, 0, keepdims=False), 0)
    second4 = swapped(lax.dynamic_index_in_dim(volumes, odd, 0, keepdims=False), 1)
    arranged4 = conv4_weight.transpose(1, 0, 2).reshape(conv4_weight.shape[1], -1)
    back5 = conv5_weight.transpose(0, 2, 1)
    pooled, slope, stack4 = layer4(volumes, first4, second4, arranged4)
    output5, grad, stack5 = layer5(
        pooled, swapped(pooled, 0), swapped(pooled, 1), conv5_weight, cotangent[0]
    )
    keep, send = backward(grad, swapped(grad, 0), swapped(grad, 1), back5, stack5, stack4, slope)
    axes = ("dp", "space")
    spaces, groups = lax.axis_size("space"), lax.axis_size("dp")
    per_core = [
        [dp * spaces + s for dp in range(core, groups, 2) for s in range(spaces)]
        for core in range(2)
    ]

    def exchange(parts):
        return lax.all_to_all(
            parts, axes, split_axis=0, concat_axis=0, tiled=True, axis_index_groups=per_core
        )

    part = (keep.astype(F32) + other_core(send).astype(F32)).astype(BF16)
    owned = exchange(part).astype(F32).sum(axis=0).astype(BF16)
    rows5, rows4 = owned[:64], owned[64:]
    columns = jnp.pad(rows5.T.reshape(spaces, -1, 64), ((0, 0), (0, 4), (0, 64)))
    outgoing = jnp.concatenate(
        [
            jnp.broadcast_to(rows4, (64, 16, 128)),
            jnp.broadcast_to(columns, (2, spaces, 8, 128)).reshape(64, 8, 128),
        ],
        axis=1,
    )
    mine = exchange(outgoing)
    theirs = other_core(mine)
    core = lax.axis_index("dp") % 2
    zero = jnp.where(core == 0, mine, theirs)[:54]
    one = jnp.where(core == 0, theirs, mine)[:54]
    both = jnp.stack([zero, one]).reshape(2, 27, 2, 24, 128)
    weight4 = both[:, :, :, :16].transpose(1, 4, 0, 2, 3).reshape(27, 128, 64).astype(F32)
    weight5 = both[:, :, :, 16:20, :64].transpose(1, 0, 2, 4, 3).reshape(27, 256, 4).astype(F32)
    return (output5[None], weight4, weight5)


def solution(mesh):
    placed = (P("space", "dp", None, None), P("space", "dp", None, None), P(), P())
    return jax.shard_map(
        per_device,
        mesh=mesh,
        in_specs=placed,
        out_specs=(P("space", "dp", None, None), P(), P(None, None, "space")),
        check_vma=False,
    )
```

```python
import jax
import jax.numpy as jnp
from jax import lax
from jax.experimental import pallas as pl
from jax.experimental.pallas import tpu as pltpu
from jax.sharding import PartitionSpec as P

HEIGHT = 32
WIDTH = 16
TAPS = tuple((b, e) for b in (-1, 0, 1) for e in (-1, 0, 1))
BF16 = jnp.bfloat16
F32 = jnp.float32
VMEM = pl.BlockSpec(memory_space=pltpu.VMEM)


def call(kernel, name, outputs, operands, scratch=(), room=12, flops=0):
    moved = sum(x.size * x.dtype.itemsize for x in operands)
    return pl.pallas_call(
        kernel,
        out_shape=tuple(pltpu.VMEM(shape, dtype) for shape, dtype in outputs),
        in_specs=[VMEM] * len(operands),
        out_specs=tuple(VMEM for _ in outputs),
        scratch_shapes=list(scratch),
        compiler_params=pltpu.CompilerParams(vmem_limit_bytes=room * 2**20),
        cost_estimate=pl.CostEstimate(flops=flops, bytes_accessed=moved, transcendentals=0),
        name=name,
    )(*[pltpu.with_memory_space_constraint(x, pltpu.VMEM) for x in operands])


def swap_pairs(count, phase):
    pairs = []
    for low in range(phase, count, 2):
        high = (low + 1) % count
        pairs += [(low, high), (high, low)]
    return pairs


def swapped(values, phase):
    return lax.ppermute(values, "space", swap_pairs(lax.axis_size("space"), phase))


def other_core(values):
    count = lax.axis_size("dp")
    return lax.ppermute(values, "dp", [(i, i ^ 1) for i in range(count)])


def neighbours(first, second):
    here = lax.axis_index("space")
    odd = here % 2 == 1
    below = jnp.where(odd, first, second)
    above = jnp.where(odd, second, first)
    below = jnp.where(here == 0, jnp.zeros_like(below), below)
    above = jnp.where(here == lax.axis_size("space") - 1, jnp.zeros_like(above), above)
    return below, above


def keep_mask(b, e, row_len, length):
    lane = lax.broadcasted_iota(jnp.int32, (1, length), 1)
    column = lane % row_len + e
    row = lane // row_len + b
    inside = (column >= 0) & (column < row_len) & (row >= 0) & (row < length // row_len)
    return inside.astype(F32)


def tap(values, b, e, row_len):
    length = values.shape[1]
    offset = b * row_len + e
    if offset == 0:
        return values
    return pltpu.roll(values, -offset % length, 1) * keep_mask(b, e, row_len, length)


def dot(left, right):
    return jnp.dot(left, right, preferred_element_type=F32)


def dot_rows(left, right):
    return lax.dot_general(left, right, (((1,), (1,)), ((), ())), preferred_element_type=F32)


def pool_matrix(fine_axis, shape):
    fine = lax.broadcasted_iota(jnp.int32, shape, fine_axis)
    coarse = lax.broadcasted_iota(jnp.int32, shape, 1 - fine_axis)
    owner = (fine // (2 * WIDTH)) * (WIDTH // 2) + (fine % WIDTH) // 2
    return (owner == coarse).astype(BF16)


def layer4_kernel(vol_ref, first_ref, second_ref, weight_ref, pooled_ref, slope_ref, stack_ref):
    chans, cells = vol_ref.shape[2], vol_ref.shape[3]
    rows = len(TAPS) * chans
    for n in range(2):
        below, above = neighbours(first_ref[n], second_ref[n])
        for j, plane in enumerate((below, vol_ref[0, n], vol_ref[1, n], above)):
            wide = plane.astype(F32)
            for t, (b, e) in enumerate(TAPS):
                stack_ref[pl.ds(j * rows + t * chans, chans), pl.ds(n * cells, cells)] = tap(
                    wide, b, e, WIDTH
                ).astype(BF16)
    pool = pool_matrix(0, (cells, cells // 4))
    for n in range(2):
        lanes = pl.ds(n * cells, cells)
        total = None
        for d in range(2):
            preact = dot(weight_ref[...], stack_ref[pl.ds(d * rows, 3 * rows), lanes])
            sig = jax.nn.sigmoid(preact)
            slope_ref[d, :, lanes] = sig * (1.0 + preact * (1.0 - sig)) * 0.125
            active = preact * sig
            total = active if total is None else total + active
        high = total.astype(BF16)
        low = (total - high.astype(F32)).astype(BF16)
        pooled = (dot(high, pool) + dot(low, pool)) * 0.125
        pooled_ref[:, pl.ds(n * cells // 4, cells // 4)] = pooled.astype(BF16)


def layer4(volumes, first, second, weight):
    vols, chans, cells = volumes.shape[1:]
    outer = weight.shape[0]
    return call(
        layer4_kernel,
        "layer4",
        (
            ((outer, vols * cells // 4), BF16),
            ((2, outer, vols * cells), F32),
            ((4 * len(TAPS) * chans, vols * cells), BF16),
        ),
        (volumes, first, second, weight),
        flops=2 * weight.size * 2 * vols * cells,
    )


def spread_taps(planes, out_ref, row_len, cells, sign):
    chans = planes[0].shape[0]
    for j, plane in enumerate(planes):
        for n in range(plane.shape[1] // cells):
            wide = plane[:, n * cells : (n + 1) * cells].astype(F32)
            for t, (b, e) in enumerate(TAPS):
                out_ref[pl.ds((j * len(TAPS) + t) * chans, chans), pl.ds(n * cells, cells)] = tap(
                    wide, sign * b, sign * e, row_len
                ).astype(BF16)


def inward_part(weight_ref, spread_ref, a):
    outer = weight_ref.shape[1]
    total = None
    for t in range(len(TAPS)):
        part = lax.dot_general(
            weight_ref[(a + 1) * len(TAPS) + t],
            spread_ref[pl.ds(t * outer, outer), :],
            (((0,), (0,)), ((), ())),
            preferred_element_type=F32,
        )
        total = part if total is None else total + part
    return total


def layer5_kernel(
    pooled_ref, first_ref, second_ref, weight_ref, cot_ref,
    out_ref, grad_ref, stack_ref, spread_ref, to_first_ref, to_second_ref,
):
    below, above = neighbours(first_ref[...], second_ref[...])
    cells = cot_ref.shape[2]
    spread_taps((below, pooled_ref[...], above), stack_ref, WIDTH // 2, cells, 1)
    chans = pooled_ref.shape[0]
    preact = None
    for o in range(0, 27, 2):
        if o < 26:
            weight = jnp.concatenate([weight_ref[o], weight_ref[o + 1]], axis=1)
        else:
            weight = weight_ref[o]
        part = dot(weight, stack_ref[pl.ds(o * chans, weight.shape[1]), :])
        preact = part if preact is None else preact + part
    sig = jax.nn.sigmoid(preact)
    active = preact * sig
    slope = sig * (1.0 + preact * (1.0 - sig))
    for n in range(cot_ref.shape[0]):
        lanes = slice(n * cells, (n + 1) * cells)
        out_ref[n] = active[:, lanes].astype(BF16)
        grad_ref[:, lanes] = (cot_ref[n].astype(F32) * slope[:, lanes]).astype(BF16)
    spread_taps((grad_ref[...],), spread_ref, WIDTH // 2, cells, -1)
    down = inward_part(weight_ref, spread_ref, -1).astype(BF16)
    up = inward_part(weight_ref, spread_ref, 1).astype(BF16)
    odd = lax.axis_index("space") % 2 == 1
    to_first_ref[...] = jnp.where(odd, down, up)
    to_second_ref[...] = jnp.where(odd, up, down)


def layer5(pooled, first, second, weight, cot):
    vols, outer, cells = cot.shape
    chans, lanes = pooled.shape
    return call(
        layer5_kernel,
        "layer5",
        (
            ((vols, outer, cells), BF16),
            ((outer, lanes), BF16),
            ((27 * chans, lanes), BF16),
            ((len(TAPS) * outer, lanes), BF16),
            ((chans, lanes), BF16),
            ((chans, lanes), BF16),
        ),
        (pooled, first, second, weight, cot),
        flops=4 * weight.size * lanes,
    )


def own_kernel(grad_ref, stack_ref, weight_ref, spread_ref, inward_ref, keep_ref, send_ref):
    inward_ref[...] = inward_part(weight_ref, spread_ref, 0)
    core = lax.axis_index("dp") % 2
    half = grad_ref.shape[0] // 2
    chans = stack_ref.shape[0] // 27
    top, bottom = grad_ref[pl.ds(0, half), :], grad_ref[pl.ds(half, half), :]
    ordered = jnp.concatenate(
        [jnp.where(core == 0, top, bottom), jnp.where(core == 0, bottom, top)], axis=0
    )
    for o in range(0, 27, 2):
        count = min(2, 27 - o)
        part = dot_rows(ordered, stack_ref[pl.ds(o * chans, count * chans), :]).astype(BF16)
        for i in range(count):
            block = part[:, i * chans : (i + 1) * chans]
            for k in range(2):
                slot = 2 * (o + i) + k
                keep_ref[slot] = block[k * 64 : (k + 1) * 64]
                send_ref[slot] = block[half + k * 64 : half + (k + 1) * 64]


def own_parts(grad, stack, weight, spread):
    outputs = (
        ((weight.shape[2], grad.shape[1]), F32),
        ((54, 64, 128), BF16),
        ((54, 64, 128), BF16),
    )
    return call(
        own_kernel,
        "own_parts",
        outputs,
        (grad, stack, weight, spread),
        flops=2 * grad.size * stack.shape[0] + 2 * weight.size * grad.shape[1] // 3,
    )


def weight4_kernel(
    inward_ref, first_ref, second_ref, stack_ref, slope_ref, keep_ref, send_ref, acc_ref
):
    core = lax.axis_index("dp") % 2
    below, above = neighbours(first_ref[...], second_ref[...])
    inward = (inward_ref[...] + below.astype(F32) + above.astype(F32)).astype(BF16)
    chans = inward.shape[0]
    cells = inward.shape[1] // 2
    unpool = pool_matrix(1, (cells, 4 * cells))
    fine = jnp.concatenate(
        [dot(inward[:, n * cells : (n + 1) * cells], unpool) for n in range(2)], axis=1
    )
    grads = jnp.concatenate(
        [(fine * slope_ref[0]).astype(BF16), (fine * slope_ref[1]).astype(BF16)], axis=0
    )
    rows = stack_ref.shape[0] // 4
    for j in range(4):
        plane = stack_ref[pl.ds(j * rows, rows), :]
        if j == 0:
            acc_ref[pl.ds(0, rows), :] = dot_rows(plane, grads[:chans])
        elif j == 3:
            acc_ref[pl.ds(2 * rows, rows), :] += dot_rows(plane, grads[chans:])
        else:
            both = dot_rows(plane, grads)
            acc_ref[pl.ds(j * rows, rows), :] = both[:, :chans]
            acc_ref[pl.ds((j - 1) * rows, rows), :] += both[:, chans:]
    inner = rows // len(TAPS)
    share = inner // 4
    for o in range(27):
        for k in range(2):
            mine = pl.multiple_of(o * inner + core * 2 * share + k * share, share)
            theirs = pl.multiple_of(o * inner + (1 - core) * 2 * share + k * share, share)
            keep_ref[2 * o + k] = acc_ref[pl.ds(mine, share), :].astype(BF16)
            send_ref[2 * o + k] = acc_ref[pl.ds(theirs, share), :].astype(BF16)


def weight4_parts(inward, first, second, stack, slope):
    chans = inward.shape[0]
    return call(
        weight4_kernel,
        "weight4_parts",
        (((54, 16, 128), BF16), ((54, 16, 128), BF16)),
        (inward, first, second, stack, slope),
        scratch=[pltpu.VMEM((3 * stack.shape[0] // 4, chans), F32)],
        flops=3 * stack.size * chans,
    )


def pair_kernel(keep5_ref, got5_ref, keep4_ref, got4_ref, out_ref):
    rows5, rows4 = keep5_ref.shape[1], keep4_ref.shape[1]
    for keep_ref, got_ref, at, rows in (
        (keep5_ref, got5_ref, 0, rows5),
        (keep4_ref, got4_ref, rows5, rows4),
    ):

        @pl.loop(0, keep_ref.shape[0])
        def _(i, keep_ref=keep_ref, got_ref=got_ref, at=at, rows=rows):
            total = keep_ref[i].astype(F32) + got_ref[i].astype(F32)
            out_ref[i, pl.ds(at, rows), :] = total.astype(BF16)

    for slot in range(keep5_ref.shape[0], out_ref.shape[0]):
        out_ref[slot] = jnp.zeros(out_ref.shape[1:], BF16)


def paired(keep5, got5, keep4, got4):
    (out,) = call(pair_kernel, "pairs", (((64, 80, 128), BF16),), (keep5, got5, keep4, got4))
    return out


def sum_kernel(parts_ref, rows4_ref, columns5_ref):
    def step(i, acc):
        return acc + parts_ref[i].astype(F32)

    total = lax.fori_loop(1, parts_ref.shape[0], step, parts_ref[0].astype(F32), unroll=9)
    columns5_ref[...] = total[:64].T.astype(BF16)
    rows4_ref[...] = total[64:].astype(BF16)


def summed(parts):
    return call(sum_kernel, "sums", (((16, 128), BF16), ((128, 64), BF16)), (parts,))


def per_device(volumes, cotangent, conv4_weight, conv5_weight):
    odd = lax.axis_index("space") % 2
    first4 = swapped(lax.dynamic_index_in_dim(volumes, 1 - odd, 0, keepdims=False), 0)
    second4 = swapped(lax.dynamic_index_in_dim(volumes, odd, 0, keepdims=False), 1)
    arranged4 = conv4_weight.transpose(1, 0, 2).reshape(conv4_weight.shape[1], -1)
    pooled, slope, stack4 = layer4(volumes, first4, second4, arranged4)
    output5, grad, stack5, spread5, to_first, to_second = layer5(
        pooled, swapped(pooled, 0), swapped(pooled, 1), conv5_weight, cotangent[0]
    )
    first, second = swapped(to_first, 0), swapped(to_second, 1)
    inward, keep5, send5 = own_parts(grad, stack5, conv5_weight, spread5)
    keep4, send4 = weight4_parts(inward, first, second, stack4, slope)
    axes = ("dp", "space")
    spaces, groups = lax.axis_size("space"), lax.axis_size("dp")
    per_core = [
        [dp * spaces + s for dp in range(core, groups, 2) for s in range(spaces)]
        for core in range(2)
    ]

    def exchange(parts):
        return lax.all_to_all(
            parts, axes, split_axis=0, concat_axis=0, tiled=True, axis_index_groups=per_core
        )

    part = paired(keep5, other_core(send5), keep4, other_core(send4))
    rows4, columns5 = summed(exchange(part))
    columns5 = jnp.pad(columns5.reshape(spaces, -1, 64), ((0, 0), (0, 4), (0, 64)))
    outgoing = jnp.concatenate(
        [
            jnp.broadcast_to(rows4, (64, 16, 128)),
            jnp.broadcast_to(columns5, (2, spaces, 8, 128)).reshape(64, 8, 128),
        ],
        axis=1,
    )
    mine = exchange(outgoing)
    theirs = other_core(mine)
    core = lax.axis_index("dp") % 2
    zero = jnp.where(core == 0, mine, theirs)[:54]
    one = jnp.where(core == 0, theirs, mine)[:54]
    both = jnp.stack([zero, one]).reshape(2, 27, 2, 24, 128)
    weight4 = both[:, :, :, :16].transpose(1, 4, 0, 2, 3).reshape(27, 128, 64).astype(F32)
    weight5 = both[:, :, :, 16:20, :64].transpose(1, 0, 2, 4, 3).reshape(27, 256, 4).astype(F32)
    return (output5[None], weight4, weight5)


def solution(mesh):
    placed = (P("space", "dp", None, None), P("space", "dp", None, None), P(), P())
    return jax.shard_map(
        per_device,
        mesh=mesh,
        in_specs=placed,
        out_specs=(P("space", "dp", None, None), P(), P(None, None, "space")),
        check_vma=False,
    )
```

```python
import jax
import jax.numpy as jnp
from jax import lax
from jax.experimental import pallas as pl
from jax.experimental.pallas import tpu as pltpu
from jax.sharding import PartitionSpec as P

HEIGHT = 32
WIDTH = 16
TAPS = tuple((b, e) for b in (-1, 0, 1) for e in (-1, 0, 1))
BF16 = jnp.bfloat16
F32 = jnp.float32
VMEM = pl.BlockSpec(memory_space=pltpu.VMEM)


def call(kernel, name, outputs, operands, scratch=(), room=12, flops=0, aliases=None):
    moved = sum(x.size * x.dtype.itemsize for x in operands)
    return pl.pallas_call(
        kernel,
        out_shape=tuple(pltpu.VMEM(shape, dtype) for shape, dtype in outputs),
        in_specs=[VMEM] * len(operands),
        out_specs=tuple(VMEM for _ in outputs),
        scratch_shapes=list(scratch),
        input_output_aliases=aliases or {},
        compiler_params=pltpu.CompilerParams(vmem_limit_bytes=room * 2**20),
        cost_estimate=pl.CostEstimate(flops=flops, bytes_accessed=moved, transcendentals=0),
        name=name,
    )(*[pltpu.with_memory_space_constraint(x, pltpu.VMEM) for x in operands])


def swap_pairs(count, phase):
    pairs = []
    for low in range(phase, count, 2):
        high = (low + 1) % count
        pairs += [(low, high), (high, low)]
    return pairs


def swapped(values, phase):
    return lax.ppermute(values, "space", swap_pairs(lax.axis_size("space"), phase))


def other_core(values):
    count = lax.axis_size("dp")
    return lax.ppermute(values, "dp", [(i, i ^ 1) for i in range(count)])


def neighbours(first, second):
    here = lax.axis_index("space")
    odd = here % 2 == 1
    below = jnp.where(odd, first, second)
    above = jnp.where(odd, second, first)
    below = jnp.where(here == 0, jnp.zeros_like(below), below)
    above = jnp.where(here == lax.axis_size("space") - 1, jnp.zeros_like(above), above)
    return below, above


def keep_mask(b, e, row_len, length):
    lane = lax.broadcasted_iota(jnp.int32, (1, length), 1)
    column = lane % row_len + e
    row = lane // row_len + b
    inside = (column >= 0) & (column < row_len) & (row >= 0) & (row < length // row_len)
    return inside.astype(F32)


def tap(values, b, e, row_len):
    length = values.shape[1]
    offset = b * row_len + e
    if offset == 0:
        return values
    return pltpu.roll(values, -offset % length, 1) * keep_mask(b, e, row_len, length)


def dot(left, right):
    return jnp.dot(left, right, preferred_element_type=F32)


def dot_rows(left, right):
    return lax.dot_general(left, right, (((1,), (1,)), ((), ())), preferred_element_type=F32)


def pool_matrix(fine_axis, shape):
    fine = lax.broadcasted_iota(jnp.int32, shape, fine_axis)
    coarse = lax.broadcasted_iota(jnp.int32, shape, 1 - fine_axis)
    owner = (fine // (2 * WIDTH)) * (WIDTH // 2) + (fine % WIDTH) // 2
    return (owner == coarse).astype(BF16)


def stack_plane(plane, out_ref, j, n):
    chans, cells = plane.shape
    wide = plane.astype(F32)
    for t, (b, e) in enumerate(TAPS):
        out_ref[pl.ds((j * len(TAPS) + t) * chans, chans), pl.ds(n * cells, cells)] = tap(
            wide, b, e, WIDTH
        ).astype(BF16)


def own4_kernel(vol_ref, weight_ref, part_ref, stack_ref):
    rows = len(TAPS) * vol_ref.shape[2]
    for n in range(2):
        for d in range(2):
            stack_plane(vol_ref[d, n], stack_ref, 1 + d, n)
    for d in range(2):
        part_ref[d] = dot(
            weight_ref[:, (1 - d) * rows : (3 - d) * rows], stack_ref[pl.ds(rows, 2 * rows), :]
        )


def own4(volumes, weight):
    vols, chans, cells = volumes.shape[1:]
    return call(
        own4_kernel,
        "own4",
        (
            ((2, weight.shape[0], vols * cells), F32),
            ((4 * len(TAPS) * chans, vols * cells), BF16),
        ),
        (volumes, weight),
        flops=2 * weight.size * 2 * vols * cells,
    )


def layer4_kernel(
    first_ref, second_ref, weight_ref, part_ref, _, pooled_ref, slope_ref, stack_ref
):
    chans, cells = first_ref.shape[1:]
    rows = len(TAPS) * chans
    for n in range(2):
        below, above = neighbours(first_ref[n], second_ref[n])
        stack_plane(below, stack_ref, 0, n)
        stack_plane(above, stack_ref, 3, n)
    pool = pool_matrix(0, (cells, cells // 4))
    for n in range(2):
        lanes = pl.ds(n * cells, cells)
        total = None
        for d in range(2):
            preact = part_ref[d, :, lanes] + dot(
                weight_ref[:, 2 * d * rows : (2 * d + 1) * rows],
                stack_ref[pl.ds(3 * d * rows, rows), lanes],
            )
            sig = jax.nn.sigmoid(preact)
            slope_ref[d, :, lanes] = sig * (1.0 + preact * (1.0 - sig)) * 0.125
            active = preact * sig
            total = active if total is None else total + active
        high = total.astype(BF16)
        low = (total - high.astype(F32)).astype(BF16)
        pooled = (dot(high, pool) + dot(low, pool)) * 0.125
        pooled_ref[:, pl.ds(n * cells // 4, cells // 4)] = pooled.astype(BF16)


def layer4(first, second, weight, part, stack):
    lanes = stack.shape[1]
    return call(
        layer4_kernel,
        "layer4",
        (((weight.shape[0], lanes // 4), BF16), (part.shape, F32), (stack.shape, BF16)),
        (first, second, weight, part, stack),
        flops=2 * weight.size * lanes,
        aliases={3: 1, 4: 2},
    )


def spread_taps(planes, out_ref, row_len, cells, sign):
    chans = planes[0].shape[0]
    for j, plane in enumerate(planes):
        for n in range(plane.shape[1] // cells):
            wide = plane[:, n * cells : (n + 1) * cells].astype(F32)
            for t, (b, e) in enumerate(TAPS):
                out_ref[pl.ds((j * len(TAPS) + t) * chans, chans), pl.ds(n * cells, cells)] = tap(
                    wide, sign * b, sign * e, row_len
                ).astype(BF16)


def inward_part(weight_ref, spread_ref, a):
    outer = weight_ref.shape[1]
    total = None
    for t in range(len(TAPS)):
        part = lax.dot_general(
            weight_ref[(a + 1) * len(TAPS) + t],
            spread_ref[pl.ds(t * outer, outer), :],
            (((0,), (0,)), ((), ())),
            preferred_element_type=F32,
        )
        total = part if total is None else total + part
    return total


def convolved5(weight_ref, stack_ref, a):
    chans = weight_ref.shape[2]
    first = (a + 1) * len(TAPS)
    total = None
    for o in range(first, first + len(TAPS), 2):
        if o + 1 < first + len(TAPS):
            weight = jnp.concatenate([weight_ref[o], weight_ref[o + 1]], axis=1)
        else:
            weight = weight_ref[o]
        part = dot(weight, stack_ref[pl.ds(o * chans, weight.shape[1]), :])
        total = part if total is None else total + part
    return total


def own5_kernel(pooled_ref, weight_ref, part_ref, stack_ref):
    rows = len(TAPS) * pooled_ref.shape[0]
    cells = pooled_ref.shape[1] // 2
    spread_taps((pooled_ref[...],), stack_ref.at[pl.ds(rows, rows), :], WIDTH // 2, cells, 1)
    part_ref[...] = convolved5(weight_ref, stack_ref, 0)


def own5(pooled, weight):
    chans, lanes = pooled.shape
    return call(
        own5_kernel,
        "own5",
        (((weight.shape[1], lanes), F32), ((27 * chans, lanes), BF16)),
        (pooled, weight),
        flops=2 * weight.size * lanes // 3,
    )


def layer5_kernel(
    pooled_ref, first_ref, second_ref, weight_ref, cot_ref, part_ref, _,
    out_ref, grad_ref, stack_ref, spread_ref, to_first_ref, to_second_ref, share_ref,
):
    chans = pooled_ref.shape[0]
    outer = grad_ref.shape[0]
    cells = cot_ref.shape[2]
    rows = len(TAPS) * chans
    below, above = neighbours(first_ref[...], second_ref[...])
    spread_taps((below,), stack_ref.at[pl.ds(0, rows), :], WIDTH // 2, cells, 1)
    spread_taps((above,), stack_ref.at[pl.ds(2 * rows, rows), :], WIDTH // 2, cells, 1)
    preact = part_ref[...]
    preact += convolved5(weight_ref, stack_ref, -1)
    preact += convolved5(weight_ref, stack_ref, 1)
    sig = jax.nn.sigmoid(preact)
    active = preact * sig
    slope = sig * (1.0 + preact * (1.0 - sig))
    for n in range(cot_ref.shape[0]):
        lanes = slice(n * cells, (n + 1) * cells)
        out_ref[n] = active[:, lanes].astype(BF16)
        grad_ref[:, lanes] = (cot_ref[n].astype(F32) * slope[:, lanes]).astype(BF16)
    spread_taps((grad_ref[...],), spread_ref, WIDTH // 2, cells, -1)
    down = inward_part(weight_ref, spread_ref, -1).astype(BF16)
    up = inward_part(weight_ref, spread_ref, 1).astype(BF16)
    odd = lax.axis_index("space") % 2 == 1
    to_first_ref[...] = jnp.where(odd, down, up)
    to_second_ref[...] = jnp.where(odd, up, down)
    core = lax.axis_index("dp") % 2
    half = outer // 2
    share_ref[pl.ds(0, half), :] = grad_ref[pl.ds(pl.multiple_of((1 - core) * half, half), half), :]
    share_ref[pl.ds(half, chans), :] = below
    share_ref[pl.ds(half + chans, chans), :] = pooled_ref[...]
    share_ref[pl.ds(half + 2 * chans, chans), :] = above


def layer5(pooled, first, second, weight, cot, part, stack):
    vols, outer, cells = cot.shape
    chans, lanes = pooled.shape
    return call(
        layer5_kernel,
        "layer5",
        (
            ((vols, outer, cells), BF16),
            ((outer, lanes), BF16),
            (stack.shape, BF16),
            ((len(TAPS) * outer, lanes), BF16),
            ((chans, lanes), BF16),
            ((chans, lanes), BF16),
            ((outer // 2 + 3 * chans, lanes), BF16),
        ),
        (pooled, first, second, weight, cot, part, stack),
        flops=3 * weight.size * lanes,
        aliases={6: 2},
    )


def inward_kernel(weight_ref, spread_ref, inward_ref):
    inward_ref[...] = inward_part(weight_ref, spread_ref, 0)


def own_inward(weight, spread):
    (inward,) = call(
        inward_kernel,
        "own_inward",
        (((weight.shape[2], spread.shape[1]), F32),),
        (weight, spread),
        flops=2 * weight.size * spread.shape[1] // 3,
    )
    return inward


def weight5_kernel(grad_ref, stack_ref, got_ref, part_ref, other_ref):
    core = lax.axis_index("dp") % 2
    half = grad_ref.shape[0] // 2
    chans = stack_ref.shape[0] // 27
    cells = grad_ref.shape[1] // 2
    planes = tuple(got_ref[pl.ds(half + j * chans, chans), :] for j in range(3))
    spread_taps(planes, other_ref, WIDTH // 2, cells, 1)
    mine = grad_ref[pl.ds(pl.multiple_of(core * half, half), half), :]
    theirs = got_ref[pl.ds(0, half), :]
    block = part_ref.shape[1] - 16
    rows = len(TAPS) * chans
    for j in range(3):
        at = pl.ds(j * rows, rows)
        total = dot_rows(stack_ref[at, :], mine) + dot_rows(other_ref[at, :], theirs)
        total = total.astype(BF16)
        for k in range(rows // block):
            part_ref[j * (rows // block) + k, pl.ds(0, block), :] = total[k * block : (k + 1) * block]


def weight5_part(grad, stack, got):
    (part,) = call(
        weight5_kernel,
        "weight5",
        (((64, 80, 128), BF16),),
        (grad, stack, got),
        scratch=[pltpu.VMEM(stack.shape, BF16)],
        flops=2 * grad.size * stack.shape[0],
    )
    return part


def weight4_kernel(
    inward_ref, first_ref, second_ref, stack_ref, slope_ref, keep_ref, send_ref, acc_ref
):
    core = lax.axis_index("dp") % 2
    below, above = neighbours(first_ref[...], second_ref[...])
    inward = (inward_ref[...] + below.astype(F32) + above.astype(F32)).astype(BF16)
    chans = inward.shape[0]
    cells = inward.shape[1] // 2
    unpool = pool_matrix(1, (cells, 4 * cells))
    fine = jnp.concatenate(
        [dot(inward[:, n * cells : (n + 1) * cells], unpool) for n in range(2)], axis=1
    )
    grads = jnp.concatenate(
        [(fine * slope_ref[0]).astype(BF16), (fine * slope_ref[1]).astype(BF16)], axis=0
    )
    rows = stack_ref.shape[0] // 4
    for j in range(4):
        plane = stack_ref[pl.ds(j * rows, rows), :]
        if j == 0:
            acc_ref[pl.ds(0, rows), :] = dot_rows(plane, grads[:chans])
        elif j == 3:
            acc_ref[pl.ds(2 * rows, rows), :] += dot_rows(plane, grads[chans:])
        else:
            both = dot_rows(plane, grads)
            acc_ref[pl.ds(j * rows, rows), :] = both[:, :chans]
            acc_ref[pl.ds((j - 1) * rows, rows), :] += both[:, chans:]
    inner = rows // len(TAPS)
    share = inner // 4
    for o in range(27):
        for k in range(2):
            mine = pl.multiple_of(o * inner + core * 2 * share + k * share, share)
            theirs = pl.multiple_of(o * inner + (1 - core) * 2 * share + k * share, share)
            keep_ref[2 * o + k] = acc_ref[pl.ds(mine, share), :]
            send_ref[2 * o + k] = acc_ref[pl.ds(theirs, share), :].astype(BF16)


def weight4_parts(inward, first, second, stack, slope):
    chans = inward.shape[0]
    return call(
        weight4_kernel,
        "weight4_parts",
        (((54, 16, 128), F32), ((54, 16, 128), BF16)),
        (inward, first, second, stack, slope),
        scratch=[pltpu.VMEM((3 * stack.shape[0] // 4, chans), F32)],
        flops=3 * stack.size * chans,
    )


def pair_kernel(keep_ref, got_ref, _, part_ref):
    filled, rows = keep_ref.shape[:2]
    first = part_ref.shape[1] - rows
    for i in range(filled):
        part_ref[i, pl.ds(first, rows), :] = (keep_ref[i] + got_ref[i].astype(F32)).astype(BF16)
    for i in range(filled, part_ref.shape[0]):
        part_ref[i] = jnp.zeros(part_ref.shape[1:], BF16)


def paired(keep, got, part):
    (part,) = call(pair_kernel, "pairs", ((part.shape, BF16),), (keep, got, part), aliases={2: 0})
    return part


def sum_kernel(parts_ref, rows4_ref, rows5_ref):
    def step(i, acc):
        return acc + parts_ref[i].astype(F32)

    total = lax.fori_loop(1, parts_ref.shape[0], step, parts_ref[0].astype(F32), unroll=9)
    rows5_ref[...] = total[:64].astype(BF16)
    rows4_ref[...] = total[64:].astype(BF16)


def summed(parts):
    return call(sum_kernel, "sums", (((16, 128), BF16), ((64, 128), BF16)), (parts,))


def finish_kernel(mine_ref, theirs_ref, weight4_ref, weight5_ref):
    core = lax.axis_index("dp") % 2
    upper = lax.axis_index("space") // 16
    for o in range(27):
        for side, ref in ((core, mine_ref), (1 - core, theirs_ref)):
            for k in range(2):
                at = pl.multiple_of(side * 32 + k * 16, 16)
                weight4_ref[o, pl.ds(at, 16), :] = ref[2 * o + k].astype(F32)[:16]
            at = pl.multiple_of(side * 128, 128)
            weight5_ref[o, :, pl.ds(at, 128)] = ref[2 * o + upper].astype(F32)[16:20]


def finished(mine, theirs):
    weight4, weight5 = pl.pallas_call(
        finish_kernel,
        out_shape=(
            jax.ShapeDtypeStruct((27, 64, 128), F32),
            jax.ShapeDtypeStruct((27, 4, 256), F32),
        ),
        in_specs=[VMEM] * 2,
        out_specs=(VMEM, VMEM),
        name="finish",
    )(*[pltpu.with_memory_space_constraint(x, pltpu.VMEM) for x in (mine, theirs)])
    return weight4.transpose(0, 2, 1), weight5.transpose(0, 2, 1)


def per_device(volumes, cotangent, conv4_weight, conv5_weight):
    odd = lax.axis_index("space") % 2
    first4 = swapped(lax.dynamic_index_in_dim(volumes, 1 - odd, 0, keepdims=False), 0)
    second4 = swapped(lax.dynamic_index_in_dim(volumes, odd, 0, keepdims=False), 1)
    arranged4 = conv4_weight.transpose(1, 0, 2).reshape(conv4_weight.shape[1], -1)
    part4, stack4 = own4(volumes, arranged4)
    pooled, slope, stack4 = layer4(first4, second4, arranged4, part4, stack4)
    part5, stack5 = own5(pooled, conv5_weight)
    output5, grad, stack5, spread5, to_first, to_second, share = layer5(
        pooled, swapped(pooled, 0), swapped(pooled, 1), conv5_weight, cotangent[0], part5, stack5
    )
    first, second = swapped(to_first, 0), swapped(to_second, 1)
    inward = own_inward(conv5_weight, spread5)
    part = weight5_part(grad, stack5, other_core(share))
    keep, send = weight4_parts(inward, first, second, stack4, slope)
    axes = ("dp", "space")
    spaces, groups = lax.axis_size("space"), lax.axis_size("dp")
    per_core = [
        [dp * spaces + s for dp in range(core, groups, 2) for s in range(spaces)]
        for core in range(2)
    ]

    def exchange(parts):
        return lax.all_to_all(
            parts, axes, split_axis=0, concat_axis=0, tiled=True, axis_index_groups=per_core
        )

    rows4, rows5 = summed(exchange(paired(keep, other_core(send), part)))
    rows5 = jnp.pad(rows5.reshape(spaces // 2, 4, 128), ((0, 0), (0, 4), (0, 0)))
    outgoing = jnp.concatenate(
        [
            jnp.broadcast_to(rows4, (64, 16, 128)),
            jnp.broadcast_to(rows5, (4, spaces // 2, 8, 128)).reshape(64, 8, 128),
        ],
        axis=1,
    )
    mine = exchange(outgoing)
    weight4, weight5 = finished(mine, other_core(mine))
    return (output5[None], weight4, weight5)


def solution(mesh):
    placed = (P("space", "dp", None, None), P("space", "dp", None, None), P(), P())
    return jax.shard_map(
        per_device,
        mesh=mesh,
        in_specs=placed,
        out_specs=(P("space", "dp", None, None), P(), P(None, None, "space")),
        check_vma=False,
    )
```

```python
import jax
import jax.numpy as jnp
from jax import lax
from jax.experimental import pallas as pl
from jax.experimental.pallas import tpu as pltpu
from jax.sharding import PartitionSpec as P

HEIGHT = 32
WIDTH = 16
TAPS = tuple((b, e) for b in (-1, 0, 1) for e in (-1, 0, 1))
BF16 = jnp.bfloat16
F32 = jnp.float32
VMEM = pl.BlockSpec(memory_space=pltpu.VMEM)


def call(kernel, name, outputs, operands, scratch=(), room=12, flops=0, aliases=None):
    moved = sum(x.size * x.dtype.itemsize for x in operands)
    return pl.pallas_call(
        kernel,
        out_shape=tuple(pltpu.VMEM(shape, dtype) for shape, dtype in outputs),
        in_specs=[VMEM] * len(operands),
        out_specs=tuple(VMEM for _ in outputs),
        scratch_shapes=list(scratch),
        input_output_aliases=aliases or {},
        compiler_params=pltpu.CompilerParams(vmem_limit_bytes=room * 2**20),
        cost_estimate=pl.CostEstimate(flops=flops, bytes_accessed=moved, transcendentals=0),
        name=name,
    )(*[pltpu.with_memory_space_constraint(x, pltpu.VMEM) for x in operands])


def swap_pairs(count, phase):
    pairs = []
    for low in range(phase, count, 2):
        high = (low + 1) % count
        pairs += [(low, high), (high, low)]
    return pairs


def swapped(values, phase):
    return lax.ppermute(values, "space", swap_pairs(lax.axis_size("space"), phase))


def other_core(values):
    count = lax.axis_size("dp")
    return lax.ppermute(values, "dp", [(i, i ^ 1) for i in range(count)])


def other_chip(values):
    count = lax.axis_size("dp")
    return lax.ppermute(values, "dp", [(i, i ^ 2) for i in range(count)])


def neighbours(first, second):
    here = lax.axis_index("space")
    odd = here % 2 == 1
    below = jnp.where(odd, first, second)
    above = jnp.where(odd, second, first)
    below = jnp.where(here == 0, jnp.zeros_like(below), below)
    above = jnp.where(here == lax.axis_size("space") - 1, jnp.zeros_like(above), above)
    return below, above


def keep_mask(b, e, row_len, length):
    lane = lax.broadcasted_iota(jnp.int32, (1, length), 1)
    column = lane % row_len + e
    row = lane // row_len + b
    inside = (column >= 0) & (column < row_len) & (row >= 0) & (row < length // row_len)
    return inside.astype(F32)


def tap(values, b, e, row_len):
    length = values.shape[1]
    offset = b * row_len + e
    if offset == 0:
        return values
    return pltpu.roll(values, -offset % length, 1) * keep_mask(b, e, row_len, length)


def dot(left, right):
    return jnp.dot(left, right, preferred_element_type=F32)


def dot_rows(left, right):
    return lax.dot_general(left, right, (((1,), (1,)), ((), ())), preferred_element_type=F32)


def pool_matrix(fine_axis, shape):
    fine = lax.broadcasted_iota(jnp.int32, shape, fine_axis)
    coarse = lax.broadcasted_iota(jnp.int32, shape, 1 - fine_axis)
    owner = (fine // (2 * WIDTH)) * (WIDTH // 2) + (fine % WIDTH) // 2
    return (owner == coarse).astype(BF16)


def stack_plane(plane, out_ref, j, n):
    chans, cells = plane.shape
    wide = plane.astype(F32)
    for t, (b, e) in enumerate(TAPS):
        out_ref[pl.ds((j * len(TAPS) + t) * chans, chans), pl.ds(n * cells, cells)] = tap(
            wide, b, e, WIDTH
        ).astype(BF16)


def own4_kernel(vol_ref, weight_ref, part_ref, stack_ref):
    rows = len(TAPS) * vol_ref.shape[2]
    for n in range(2):
        for d in range(2):
            stack_plane(vol_ref[d, n], stack_ref, 1 + d, n)
    for d in range(2):
        part_ref[d] = dot(
            weight_ref[:, (1 - d) * rows : (3 - d) * rows], stack_ref[pl.ds(rows, 2 * rows), :]
        )


def own4(volumes, weight):
    vols, chans, cells = volumes.shape[1:]
    return call(
        own4_kernel,
        "own4",
        (
            ((2, weight.shape[0], vols * cells), F32),
            ((4 * len(TAPS) * chans, vols * cells), BF16),
        ),
        (volumes, weight),
        flops=2 * weight.size * 2 * vols * cells,
    )


def layer4_kernel(
    first_ref, second_ref, weight_ref, part_ref, _, pooled_ref, slope_ref, stack_ref
):
    chans, cells = first_ref.shape[1:]
    rows = len(TAPS) * chans
    for n in range(2):
        below, above = neighbours(first_ref[n], second_ref[n])
        stack_plane(below, stack_ref, 0, n)
        stack_plane(above, stack_ref, 3, n)
    pool = pool_matrix(0, (cells, cells // 4))
    for n in range(2):
        lanes = pl.ds(n * cells, cells)
        total = None
        for d in range(2):
            preact = part_ref[d, :, lanes] + dot(
                weight_ref[:, 2 * d * rows : (2 * d + 1) * rows],
                stack_ref[pl.ds(3 * d * rows, rows), lanes],
            )
            sig = jax.nn.sigmoid(preact)
            slope_ref[d, :, lanes] = sig * (1.0 + preact * (1.0 - sig)) * 0.125
            active = preact * sig
            total = active if total is None else total + active
        high = total.astype(BF16)
        low = (total - high.astype(F32)).astype(BF16)
        pooled = (dot(high, pool) + dot(low, pool)) * 0.125
        pooled_ref[:, pl.ds(n * cells // 4, cells // 4)] = pooled.astype(BF16)


def layer4(first, second, weight, part, stack):
    lanes = stack.shape[1]
    return call(
        layer4_kernel,
        "layer4",
        (((weight.shape[0], lanes // 4), BF16), (part.shape, F32), (stack.shape, BF16)),
        (first, second, weight, part, stack),
        flops=2 * weight.size * lanes,
        aliases={3: 1, 4: 2},
    )


def spread_taps(planes, out_ref, row_len, cells, sign):
    chans = planes[0].shape[0]
    for j, plane in enumerate(planes):
        for n in range(plane.shape[1] // cells):
            wide = plane[:, n * cells : (n + 1) * cells].astype(F32)
            for t, (b, e) in enumerate(TAPS):
                out_ref[pl.ds((j * len(TAPS) + t) * chans, chans), pl.ds(n * cells, cells)] = tap(
                    wide, sign * b, sign * e, row_len
                ).astype(BF16)


def inward_part(weight_ref, spread_ref, a):
    outer = weight_ref.shape[1]
    total = None
    for t in range(len(TAPS)):
        part = lax.dot_general(
            weight_ref[(a + 1) * len(TAPS) + t],
            spread_ref[pl.ds(t * outer, outer), :],
            (((0,), (0,)), ((), ())),
            preferred_element_type=F32,
        )
        total = part if total is None else total + part
    return total


def convolved5(weight_ref, stack_ref, a):
    chans = weight_ref.shape[2]
    taps = len(TAPS)
    first = (a + 1) * taps
    total = None
    for t in range(0, taps, 2):
        if t + 1 < taps:
            weight = jnp.concatenate([weight_ref[first + t], weight_ref[first + t + 1]], axis=1)
        else:
            weight = weight_ref[first + t]
        part = dot(weight, stack_ref[pl.ds(t * chans, weight.shape[1]), :])
        total = part if total is None else total + part
    return total


def own5_kernel(pooled_ref, weight_ref, part_ref, stack_ref):
    cells = pooled_ref.shape[1] // 2
    spread_taps((pooled_ref[...],), stack_ref, WIDTH // 2, cells, 1)
    part_ref[...] = convolved5(weight_ref, stack_ref, 0)


def own5(pooled, weight):
    chans, lanes = pooled.shape
    (part,) = call(
        own5_kernel,
        "own5",
        (((weight.shape[1], lanes), F32),),
        (pooled, weight),
        scratch=[pltpu.VMEM((len(TAPS) * chans, lanes), BF16)],
        flops=2 * weight.size * lanes // 3,
    )
    return part


def layer5_kernel(
    pooled_ref, first_ref, second_ref, weight_ref, cot_ref, part_ref,
    out_ref, spread_ref, to_first_ref, to_second_ref, mine_ref, share_ref, stack_ref,
):
    chans = pooled_ref.shape[0]
    outer = part_ref.shape[0]
    cells = cot_ref.shape[2]
    below, above = neighbours(first_ref[...], second_ref[...])
    preact = part_ref[...]
    spread_taps((below,), stack_ref.at[0], WIDTH // 2, cells, 1)
    preact += convolved5(weight_ref, stack_ref.at[0], -1)
    spread_taps((above,), stack_ref.at[1], WIDTH // 2, cells, 1)
    preact += convolved5(weight_ref, stack_ref.at[1], 1)
    sig = jax.nn.sigmoid(preact)
    active = preact * sig
    slope = sig * (1.0 + preact * (1.0 - sig))
    for n in range(cot_ref.shape[0]):
        lanes = slice(n * cells, (n + 1) * cells)
        out_ref[n] = active[:, lanes].astype(BF16)
        grad = (cot_ref[n].astype(F32) * slope[:, lanes]).astype(BF16)
        mine_ref[pl.ds(0, outer), lanes] = grad
        share_ref[pl.ds(0, outer), lanes] = grad
    spread_taps((mine_ref[pl.ds(0, outer), :],), spread_ref, WIDTH // 2, cells, -1)
    down = inward_part(weight_ref, spread_ref, -1).astype(BF16)
    up = inward_part(weight_ref, spread_ref, 1).astype(BF16)
    odd = lax.axis_index("space") % 2 == 1
    to_first_ref[...] = jnp.where(odd, down, up)
    to_second_ref[...] = jnp.where(odd, up, down)
    chip = lax.axis_index("dp") // 2
    half = chans // 2
    for j, plane in enumerate((below, pooled_ref[...], above)):
        at = pl.ds(outer + j * half, half)
        mine_ref[at, :] = jnp.where(chip == 0, plane[:half], plane[half:])
        share_ref[at, :] = jnp.where(chip == 0, plane[half:], plane[:half])


def layer5(pooled, first, second, weight, cot, part):
    vols, outer, cells = cot.shape
    chans, lanes = pooled.shape
    return call(
        layer5_kernel,
        "layer5",
        (
            ((vols, outer, cells), BF16),
            ((len(TAPS) * outer, lanes), BF16),
            ((chans, lanes), BF16),
            ((chans, lanes), BF16),
            ((outer + 3 * chans // 2, lanes), BF16),
            ((outer + 3 * chans // 2, lanes), BF16),
        ),
        (pooled, first, second, weight, cot, part),
        scratch=[pltpu.VMEM((2, len(TAPS) * chans, lanes), BF16)],
        flops=3 * weight.size * lanes,
    )


def inward_kernel(weight_ref, spread_ref, inward_ref):
    inward_ref[...] = inward_part(weight_ref, spread_ref, 0)


def own_inward(weight, spread):
    (inward,) = call(
        inward_kernel,
        "own_inward",
        (((weight.shape[2], spread.shape[1]), F32),),
        (weight, spread),
        flops=2 * weight.size * spread.shape[1] // 3,
    )
    return inward


def regroup_kernel(mine_ref, got_ref, send_ref):
    core = lax.axis_index("dp") % 2
    rows = send_ref.shape[0] // 2
    half = mine_ref.shape[0] - rows
    for i, ref in enumerate((mine_ref, got_ref)):
        start = pl.multiple_of((1 - core) * half, half)
        send_ref[pl.ds(i * rows, half), :] = ref[pl.ds(start, half), :]
        send_ref[pl.ds(i * rows + half, rows - half), :] = ref[pl.ds(2 * half, rows - half), :]


def regrouped(mine, got, outer):
    rows = mine.shape[0] - outer // 2
    (send,) = call(regroup_kernel, "regroup", (((2 * rows, mine.shape[1]), BF16),), (mine, got))
    return send


def weight5_kernel(mine_ref, chip_ref, core_ref, part_ref, stack_ref, total_ref):
    core = lax.axis_index("dp") % 2
    lanes = mine_ref.shape[1]
    rows = core_ref.shape[0] // 2
    half = mine_ref.shape[0] - rows
    own = pl.ds(pl.multiple_of(core * half, half), half)
    grads = []
    for i, (ref, at, first) in enumerate((
        (mine_ref, own, 2 * half),
        (chip_ref, own, 2 * half),
        (core_ref, pl.ds(0, half), half),
        (core_ref, pl.ds(rows, half), rows + half),
    )):
        grads.append(ref[at, :])
        chans = (rows - half) // 3
        planes = tuple(ref[pl.ds(first + j * chans, chans), :] for j in range(3))
        spread_taps(planes, stack_ref.at[:, pl.ds(i * lanes, lanes)], WIDTH // 2, lanes // 2, 1)
    grads = jnp.concatenate(grads, axis=1)
    block = stack_ref.shape[0] // 3
    for j in range(3):
        at = pl.ds(j * block, block)
        total_ref[at, :] = dot_rows(stack_ref[at, :], grads)
    total_ref[pl.ds(3 * block, 8), :] = jnp.zeros((8, half), F32)
    owners = part_ref.shape[0]
    for owner in range(owners):
        part_ref[owner, pl.ds(16, 32), :] = total_ref[
            pl.ds(owner * (3 * block // owners), 32), :
        ].astype(BF16)


def weight5_part(mine, chip, core, outer):
    lanes = mine.shape[1]
    rows = 9 * (mine.shape[0] - outer)
    (part,) = call(
        weight5_kernel,
        "weight5",
        (((64, 48, 128), BF16),),
        (mine, chip, core),
        scratch=[pltpu.VMEM((rows, 4 * lanes), BF16), pltpu.VMEM((rows + 8, outer // 2), F32)],
        flops=4 * rows * lanes * outer,
    )
    return part


def weight4_kernel(
    inward_ref, first_ref, second_ref, stack_ref, slope_ref, keep_ref, send_ref, acc_ref
):
    core = lax.axis_index("dp") % 2
    below, above = neighbours(first_ref[...], second_ref[...])
    inward = (inward_ref[...] + below.astype(F32) + above.astype(F32)).astype(BF16)
    chans = inward.shape[0]
    cells = inward.shape[1] // 2
    unpool = pool_matrix(1, (cells, 4 * cells))
    fine = jnp.concatenate(
        [dot(inward[:, n * cells : (n + 1) * cells], unpool) for n in range(2)], axis=1
    )
    grads = jnp.concatenate(
        [(fine * slope_ref[0]).astype(BF16), (fine * slope_ref[1]).astype(BF16)], axis=0
    )
    rows = stack_ref.shape[0] // 4
    for j in range(4):
        plane = stack_ref[pl.ds(j * rows, rows), :]
        if j == 0:
            acc_ref[pl.ds(0, rows), :] = dot_rows(plane, grads[:chans])
        elif j == 3:
            acc_ref[pl.ds(2 * rows, rows), :] += dot_rows(plane, grads[chans:])
        else:
            both = dot_rows(plane, grads)
            acc_ref[pl.ds(j * rows, rows), :] = both[:, :chans]
            acc_ref[pl.ds((j - 1) * rows, rows), :] += both[:, chans:]
    inner = rows // len(TAPS)
    share = inner // 4
    for o in range(27):
        for k in range(2):
            mine = pl.multiple_of(o * inner + core * 2 * share + k * share, share)
            theirs = pl.multiple_of(o * inner + (1 - core) * 2 * share + k * share, share)
            keep_ref[2 * o + k] = acc_ref[pl.ds(mine, share), :]
            send_ref[2 * o + k] = acc_ref[pl.ds(theirs, share), :].astype(BF16)


def weight4_parts(inward, first, second, stack, slope):
    chans = inward.shape[0]
    return call(
        weight4_kernel,
        "weight4_parts",
        (((54, 16, 128), F32), ((54, 16, 128), BF16)),
        (inward, first, second, stack, slope),
        scratch=[pltpu.VMEM((3 * stack.shape[0] // 4, chans), F32)],
        flops=3 * stack.size * chans,
    )


def pair_kernel(keep_ref, got_ref, _, part_ref):
    filled, rows = keep_ref.shape[:2]
    for i in range(filled):
        part_ref[i, pl.ds(0, rows), :] = (keep_ref[i] + got_ref[i].astype(F32)).astype(BF16)
    for i in range(filled, part_ref.shape[0]):
        part_ref[i, pl.ds(0, rows), :] = jnp.zeros((rows, part_ref.shape[2]), BF16)


def paired(keep, got, part):
    (part,) = call(pair_kernel, "pairs", ((part.shape, BF16),), (keep, got, part), aliases={2: 0})
    return part


def sum_kernel(parts_ref, rows4_ref, rows5_ref):
    def step(i, acc):
        return acc + parts_ref[i].astype(F32)

    owners = parts_ref.shape[0]
    sides = [
        lax.fori_loop(1, owners // 2, lambda i, acc, at=at: step(at + i, acc), parts_ref[at].astype(F32))
        for at in (0, owners // 2)
    ]
    rows4_ref[...] = (sides[0][:16] + sides[1][:16]).astype(BF16)
    half = rows5_ref.shape[0] // 2
    owner = lax.axis_index("dp") // 2 * (owners // 2) + lax.axis_index("space")
    start = owner * (27 * half // owners) % half
    empty = jnp.zeros((half + 16 - parts_ref.shape[1], parts_ref.shape[2]), F32)
    for i, side in enumerate(sides):
        rows5 = jnp.concatenate([side[16:], empty], axis=0)
        rows5_ref[pl.ds(i * half, half), :] = pltpu.roll(rows5, start, 0).astype(BF16)


def summed(parts):
    return call(sum_kernel, "sums", (((16, 128), BF16), ((128, 128), BF16)), (parts,))


def finish_kernel(mine_ref, theirs_ref, weight4_ref, weight5_ref):
    core = lax.axis_index("dp") % 2
    first = lax.axis_index("space") % 16 * 4
    share = 27 * 64 // mine_ref.shape[0]
    row = lax.broadcasted_iota(jnp.int32, (4, 128), 0)
    for o in range(27):
        for side, ref in ((core, mine_ref), (1 - core, theirs_ref)):
            for k in range(2):
                at = pl.multiple_of(side * 32 + k * 16, 16)
                weight4_ref[o, pl.ds(at, 16), :] = ref[2 * o + k].astype(F32)[:16]
            start = o * 64 + first
            owner = start // share
            low = ref[owner].astype(F32)[16:20]
            high = ref[(start + 3) // share].astype(F32)[16:20]
            at = pl.multiple_of(side * 128, 128)
            weight5_ref[o, :, pl.ds(at, 128)] = jnp.where(
                row < (owner + 1) * share - start, low, high
            )


def finished(mine, theirs):
    weight4, weight5 = pl.pallas_call(
        finish_kernel,
        out_shape=(
            jax.ShapeDtypeStruct((27, 64, 128), F32),
            jax.ShapeDtypeStruct((27, 4, 256), F32),
        ),
        in_specs=[VMEM] * 2,
        out_specs=(VMEM, VMEM),
        name="finish",
    )(*[pltpu.with_memory_space_constraint(x, pltpu.VMEM) for x in (mine, theirs)])
    return weight4.transpose(0, 2, 1), weight5.transpose(0, 2, 1)


def per_device(volumes, cotangent, conv4_weight, conv5_weight):
    odd = lax.axis_index("space") % 2
    first4 = swapped(lax.dynamic_index_in_dim(volumes, 1 - odd, 0, keepdims=False), 0)
    second4 = swapped(lax.dynamic_index_in_dim(volumes, odd, 0, keepdims=False), 1)
    arranged4 = conv4_weight.transpose(1, 0, 2).reshape(conv4_weight.shape[1], -1)
    part4, stack4 = own4(volumes, arranged4)
    pooled, slope, stack4 = layer4(first4, second4, arranged4, part4, stack4)
    part5 = own5(pooled, conv5_weight)
    output5, spread5, to_first, to_second, mine5, share5 = layer5(
        pooled, swapped(pooled, 0), swapped(pooled, 1), conv5_weight, cotangent[0], part5
    )
    first, second = swapped(to_first, 0), swapped(to_second, 1)
    inward = own_inward(conv5_weight, spread5)
    outer = conv5_weight.shape[1]
    chip5 = other_chip(share5)
    core5 = other_core(regrouped(mine5, chip5, outer))
    part = weight5_part(mine5, chip5, core5, outer)
    keep, send = weight4_parts(inward, first, second, stack4, slope)
    axes = ("dp", "space")
    spaces, groups = lax.axis_size("space"), lax.axis_size("dp")
    per_core = [
        [dp * spaces + s for dp in range(core, groups, 2) for s in range(spaces)]
        for core in range(2)
    ]

    def exchange(parts):
        return lax.all_to_all(
            parts, axes, split_axis=0, concat_axis=0, tiled=True, axis_index_groups=per_core
        )

    rows4, rows5 = summed(exchange(paired(keep, other_core(send), part)))
    rows5 = jnp.pad(rows5.reshape(spaces, 4, 128), ((0, 0), (0, 4), (0, 0)))
    outgoing = jnp.concatenate(
        [
            jnp.broadcast_to(rows4, (64, 16, 128)),
            jnp.broadcast_to(rows5, (2, spaces, 8, 128)).reshape(64, 8, 128),
        ],
        axis=1,
    )
    mine = exchange(outgoing)
    weight4, weight5 = finished(mine, other_core(mine))
    return (output5[None], weight4, weight5)


def solution(mesh):
    placed = (P("space", "dp", None, None), P("space", "dp", None, None), P(), P())
    return jax.shard_map(
        per_device,
        mesh=mesh,
        in_specs=placed,
        out_specs=(P("space", "dp", None, None), P(), P(None, None, "space")),
        check_vma=False,
    )
```

```python
import jax
import jax.numpy as jnp
from jax import lax
from jax.experimental import pallas as pl
from jax.experimental.pallas import tpu as pltpu
from jax.sharding import PartitionSpec as P

HEIGHT = 32
WIDTH = 16
TAPS = tuple((b, e) for b in (-1, 0, 1) for e in (-1, 0, 1))
BF16 = jnp.bfloat16
F32 = jnp.float32
VMEM = pl.BlockSpec(memory_space=pltpu.VMEM)


def call(kernel, name, outputs, operands, scratch=(), room=12, flops=0, aliases=None):
    moved = sum(x.size * x.dtype.itemsize for x in operands)
    return pl.pallas_call(
        kernel,
        out_shape=tuple(pltpu.VMEM(shape, dtype) for shape, dtype in outputs),
        in_specs=[VMEM] * len(operands),
        out_specs=tuple(VMEM for _ in outputs),
        scratch_shapes=list(scratch),
        input_output_aliases=aliases or {},
        compiler_params=pltpu.CompilerParams(vmem_limit_bytes=room * 2**20),
        cost_estimate=pl.CostEstimate(flops=flops, bytes_accessed=moved, transcendentals=0),
        name=name,
    )(*[pltpu.with_memory_space_constraint(x, pltpu.VMEM) for x in operands])


def swap_pairs(groups, count, phase):
    pairs = []
    for group in range(groups):
        for here in range(count):
            there = here + 1 if here % 2 == phase else here - 1
            if 0 <= there < count:
                pairs.append((group * count + here, group * count + there))
            else:
                pairs.append((group * count + here, (group ^ 1) * count + here))
    return pairs


def swapped(values, phase):
    pairs = swap_pairs(lax.axis_size("dp"), lax.axis_size("space"), phase)
    return lax.ppermute(values, ("dp", "space"), pairs)


def other_core(values):
    count = lax.axis_size("dp")
    return lax.ppermute(values, "dp", [(i, i ^ 1) for i in range(count)])


def other_chip(values):
    count = lax.axis_size("dp")
    return lax.ppermute(values, "dp", [(i, i ^ 2) for i in range(count)])


def neighbours(first, second):
    here = lax.axis_index("space")
    odd = here % 2 == 1
    below = jnp.where(odd, first, second)
    above = jnp.where(odd, second, first)
    below = jnp.where(here == 0, jnp.zeros_like(below), below)
    above = jnp.where(here == lax.axis_size("space") - 1, jnp.zeros_like(above), above)
    return below, above


def keep_mask(b, e, row_len, length):
    lane = lax.broadcasted_iota(jnp.int32, (1, length), 1)
    column = lane % row_len + e
    row = lane // row_len + b
    inside = (column >= 0) & (column < row_len) & (row >= 0) & (row < length // row_len)
    return inside.astype(F32).astype(BF16)


def tap(values, b, e, row_len):
    length = values.shape[1]
    offset = b * row_len + e
    if offset == 0:
        return values
    return pltpu.roll(values, -offset % length, 1) * keep_mask(b, e, row_len, length)


def dot(left, right):
    return jnp.dot(left, right, preferred_element_type=F32)


def dot_rows(left, right):
    return lax.dot_general(left, right, (((1,), (1,)), ((), ())), preferred_element_type=F32)


def pool_matrix(fine_axis, shape):
    fine = lax.broadcasted_iota(jnp.int32, shape, fine_axis)
    coarse = lax.broadcasted_iota(jnp.int32, shape, 1 - fine_axis)
    owner = (fine // (2 * WIDTH)) * (WIDTH // 2) + (fine % WIDTH) // 2
    return (owner == coarse).astype(BF16)


def stack_plane(plane, out_ref, j, n):
    chans, cells = plane.shape
    for t, (b, e) in enumerate(TAPS):
        out_ref[pl.ds((j * len(TAPS) + t) * chans, chans), pl.ds(n * cells, cells)] = tap(
            plane, b, e, WIDTH
        )


def own4_kernel(vol_ref, weight_ref, part_ref, stack_ref):
    rows = len(TAPS) * vol_ref.shape[2]
    for n in range(2):
        for d in range(2):
            stack_plane(vol_ref[d, n], stack_ref, 1 + d, n)
    for d in range(2):
        part_ref[d] = dot(
            weight_ref[:, (1 - d) * rows : (3 - d) * rows], stack_ref[pl.ds(rows, 2 * rows), :]
        )


def own4(volumes, weight):
    vols, chans, cells = volumes.shape[1:]
    return call(
        own4_kernel,
        "own4",
        (
            ((2, weight.shape[0], vols * cells), F32),
            ((4 * len(TAPS) * chans, vols * cells), BF16),
        ),
        (volumes, weight),
        flops=2 * weight.size * 2 * vols * cells,
    )


def layer4_kernel(
    first_ref, second_ref, weight_ref, part_ref, _, pooled_ref, slope_ref, stack_ref
):
    chans, cells = first_ref.shape[1:]
    rows = len(TAPS) * chans
    for n in range(2):
        below, above = neighbours(first_ref[n], second_ref[n])
        stack_plane(below, stack_ref, 0, n)
        stack_plane(above, stack_ref, 3, n)
    pool = pool_matrix(0, (cells, cells // 4))
    for n in range(2):
        lanes = pl.ds(n * cells, cells)
        total = None
        for d in range(2):
            preact = part_ref[d, :, lanes] + dot(
                weight_ref[:, 2 * d * rows : (2 * d + 1) * rows],
                stack_ref[pl.ds(3 * d * rows, rows), lanes],
            )
            sig = jax.nn.sigmoid(preact)
            slope_ref[d, :, lanes] = sig * (1.0 + preact * (1.0 - sig)) * 0.125
            active = preact * sig
            total = active if total is None else total + active
        high = total.astype(BF16)
        low = (total - high.astype(F32)).astype(BF16)
        pooled = (dot(high, pool) + dot(low, pool)) * 0.125
        pooled_ref[:, pl.ds(n * cells // 4, cells // 4)] = pooled.astype(BF16)


def layer4(first, second, weight, part, stack):
    lanes = stack.shape[1]
    return call(
        layer4_kernel,
        "layer4",
        (((weight.shape[0], lanes // 4), BF16), (part.shape, F32), (stack.shape, BF16)),
        (first, second, weight, part, stack),
        flops=2 * weight.size * lanes,
        aliases={3: 1, 4: 2},
    )


def spread_taps(planes, out_ref, row_len, cells, sign):
    chans = planes[0].shape[0]
    for j, plane in enumerate(planes):
        for n in range(plane.shape[1] // cells):
            part = plane[:, n * cells : (n + 1) * cells]
            for t, (b, e) in enumerate(TAPS):
                out_ref[pl.ds((j * len(TAPS) + t) * chans, chans), pl.ds(n * cells, cells)] = tap(
                    part, sign * b, sign * e, row_len
                )


def tapped(plane, row_len, cells, b, e):
    parts = [
        tap(plane[:, at : at + cells], b, e, row_len) for at in range(0, plane.shape[1], cells)
    ]
    return jnp.concatenate(parts, axis=1)


def convolved5(weight_ref, plane, cells, a):
    first = (a + 1) * len(TAPS)
    total = None
    for t in range(0, len(TAPS), 2):
        group = range(t, min(t + 2, len(TAPS)))
        weight = jnp.concatenate([weight_ref[first + i] for i in group], axis=1)
        shifts = jnp.concatenate(
            [tapped(plane, WIDTH // 2, cells, *TAPS[i]) for i in group], axis=0
        )
        part = dot(weight, shifts)
        total = part if total is None else total + part
    return total


def own5_kernel(pooled_ref, weight_ref, part_ref, back_ref):
    chans = pooled_ref.shape[0]
    cells = pooled_ref.shape[1] // 2
    part_ref[...] = convolved5(weight_ref, pooled_ref[...], cells, 0)
    for o in range(27):
        a, t = divmod(o, len(TAPS))
        back_ref[t, pl.ds(a * chans, chans), :] = weight_ref[o].T


def own5(pooled, weight):
    chans, lanes = pooled.shape
    outer = weight.shape[1]
    return call(
        own5_kernel,
        "own5",
        (((outer, lanes), F32), ((len(TAPS), 3 * chans, outer), BF16)),
        (pooled, weight),
        flops=2 * weight.size * lanes // 3,
    )


def layer5_kernel(
    pooled_ref, first_ref, second_ref, weight_ref, cot_ref, part_ref, back_ref,
    out_ref, inward_ref, to_first_ref, to_second_ref, mine_ref, share_ref,
):
    chans = pooled_ref.shape[0]
    outer = part_ref.shape[0]
    cells = cot_ref.shape[2]
    below, above = neighbours(first_ref[...], second_ref[...])
    preact = part_ref[...] + convolved5(weight_ref, below, cells, -1)
    preact += convolved5(weight_ref, above, cells, 1)
    sig = jax.nn.sigmoid(preact)
    active = preact * sig
    slope = sig * (1.0 + preact * (1.0 - sig))
    grads = []
    for n in range(cot_ref.shape[0]):
        lanes = slice(n * cells, (n + 1) * cells)
        out_ref[n] = active[:, lanes].astype(BF16)
        grads.append((cot_ref[n].astype(F32) * slope[:, lanes]).astype(BF16))
    grad = jnp.concatenate(grads, axis=1)
    mine_ref[pl.ds(0, outer), :] = grad
    share_ref[pl.ds(0, outer), :] = grad
    inward = None
    for t, (b, e) in enumerate(TAPS):
        part = dot(back_ref[t], tapped(grad, WIDTH // 2, cells, -b, -e))
        inward = part if inward is None else inward + part
    down, up = inward[:chans].astype(BF16), inward[2 * chans :].astype(BF16)
    inward_ref[...] = inward[chans : 2 * chans]
    odd = lax.axis_index("space") % 2 == 1
    to_first_ref[...] = jnp.where(odd, down, up)
    to_second_ref[...] = jnp.where(odd, up, down)
    chip = lax.axis_index("dp") // 2
    half = chans // 2
    for j, plane in enumerate((below, pooled_ref[...], above)):
        at = pl.ds(outer + j * half, half)
        mine_ref[at, :] = jnp.where(chip == 0, plane[:half], plane[half:])
        share_ref[at, :] = jnp.where(chip == 0, plane[half:], plane[:half])


def layer5(pooled, first, second, weight, cot, part, back):
    vols, outer, cells = cot.shape
    chans, lanes = pooled.shape
    return call(
        layer5_kernel,
        "layer5",
        (
            ((vols, outer, cells), BF16),
            ((chans, lanes), F32),
            ((chans, lanes), BF16),
            ((chans, lanes), BF16),
            ((outer + 3 * chans // 2, lanes), BF16),
            ((outer + 3 * chans // 2, lanes), BF16),
        ),
        (pooled, first, second, weight, cot, part, back),
        flops=3 * weight.size * lanes,
    )


def regroup_kernel(mine_ref, got_ref, send_ref):
    core = lax.axis_index("dp") % 2
    rows = send_ref.shape[0] // 2
    half = mine_ref.shape[0] - rows
    for i, ref in enumerate((mine_ref, got_ref)):
        start = pl.multiple_of((1 - core) * half, half)
        send_ref[pl.ds(i * rows, half), :] = ref[pl.ds(start, half), :]
        send_ref[pl.ds(i * rows + half, rows - half), :] = ref[pl.ds(2 * half, rows - half), :]


def regrouped(mine, got, outer):
    rows = mine.shape[0] - outer // 2
    (send,) = call(regroup_kernel, "regroup", (((2 * rows, mine.shape[1]), BF16),), (mine, got))
    return send


def weight5_kernel(mine_ref, chip_ref, core_ref, part_ref, stack_ref, total_ref):
    core = lax.axis_index("dp") % 2
    lanes = mine_ref.shape[1]
    rows = core_ref.shape[0] // 2
    half = mine_ref.shape[0] - rows
    own = pl.ds(pl.multiple_of(core * half, half), half)
    grads = []
    for i, (ref, at, first) in enumerate((
        (mine_ref, own, 2 * half),
        (chip_ref, own, 2 * half),
        (core_ref, pl.ds(0, half), half),
        (core_ref, pl.ds(rows, half), rows + half),
    )):
        grads.append(ref[at, :])
        chans = (rows - half) // 3
        planes = tuple(ref[pl.ds(first + j * chans, chans), :] for j in range(3))
        spread_taps(planes, stack_ref.at[:, pl.ds(i * lanes, lanes)], WIDTH // 2, lanes // 2, 1)
    grads = jnp.concatenate(grads, axis=1)
    block = stack_ref.shape[0] // 3
    for j in range(3):
        at = pl.ds(j * block, block)
        total_ref[at, :] = dot_rows(stack_ref[at, :], grads)
    total_ref[pl.ds(3 * block, 8), :] = jnp.zeros((8, half), F32)
    owners = part_ref.shape[0]
    for owner in range(owners):
        part_ref[owner, pl.ds(16, 32), :] = total_ref[
            pl.ds(owner * (3 * block // owners), 32), :
        ].astype(BF16)


def weight5_part(mine, chip, core, outer):
    lanes = mine.shape[1]
    rows = 9 * (mine.shape[0] - outer)
    (part,) = call(
        weight5_kernel,
        "weight5",
        (((64, 48, 128), BF16),),
        (mine, chip, core),
        scratch=[pltpu.VMEM((rows, 4 * lanes), BF16), pltpu.VMEM((rows + 8, outer // 2), F32)],
        flops=4 * rows * lanes * outer,
    )
    return part


def weight4_kernel(
    inward_ref, first_ref, second_ref, stack_ref, slope_ref, keep_ref, send_ref, acc_ref
):
    core = lax.axis_index("dp") % 2
    below, above = neighbours(first_ref[...], second_ref[...])
    inward = (inward_ref[...] + below.astype(F32) + above.astype(F32)).astype(BF16)
    chans = inward.shape[0]
    cells = inward.shape[1] // 2
    unpool = pool_matrix(1, (cells, 4 * cells))
    fine = jnp.concatenate(
        [dot(inward[:, n * cells : (n + 1) * cells], unpool) for n in range(2)], axis=1
    )
    grads = jnp.concatenate(
        [(fine * slope_ref[0]).astype(BF16), (fine * slope_ref[1]).astype(BF16)], axis=0
    )
    grads = grads.T
    rows = stack_ref.shape[0] // 4
    for j in range(4):
        plane = stack_ref[pl.ds(j * rows, rows), :]
        if j == 0:
            acc_ref[pl.ds(0, rows), :] = dot(plane, grads[:, :chans])
        elif j == 3:
            acc_ref[pl.ds(2 * rows, rows), :] += dot(plane, grads[:, chans:])
        else:
            both = dot(plane, grads)
            acc_ref[pl.ds(j * rows, rows), :] = both[:, :chans]
            acc_ref[pl.ds((j - 1) * rows, rows), :] += both[:, chans:]
    inner = rows // len(TAPS)
    share = inner // 4
    for o in range(27):
        for k in range(2):
            mine = pl.multiple_of(o * inner + core * 2 * share + k * share, share)
            theirs = pl.multiple_of(o * inner + (1 - core) * 2 * share + k * share, share)
            keep_ref[2 * o + k] = acc_ref[pl.ds(mine, share), :]
            send_ref[2 * o + k] = acc_ref[pl.ds(theirs, share), :].astype(BF16)


def weight4_parts(inward, first, second, stack, slope):
    chans = inward.shape[0]
    return call(
        weight4_kernel,
        "weight4_parts",
        (((54, 16, 128), F32), ((54, 16, 128), BF16)),
        (inward, first, second, stack, slope),
        scratch=[pltpu.VMEM((3 * stack.shape[0] // 4, chans), F32)],
        flops=3 * stack.size * chans,
    )


def pair_kernel(keep_ref, got_ref, _, part_ref):
    filled, rows = keep_ref.shape[:2]
    for i in range(filled):
        part_ref[i, pl.ds(0, rows), :] = (keep_ref[i] + got_ref[i].astype(F32)).astype(BF16)
    for i in range(filled, part_ref.shape[0]):
        part_ref[i, pl.ds(0, rows), :] = jnp.zeros((rows, part_ref.shape[2]), BF16)


def paired(keep, got, part):
    (part,) = call(pair_kernel, "pairs", ((part.shape, BF16),), (keep, got, part), aliases={2: 0})
    return part


def sum_kernel(parts_ref, rows4_ref, rows5_ref):
    def step(i, acc):
        return acc + parts_ref[i].astype(F32)

    owners = parts_ref.shape[0]
    sides = [
        lax.fori_loop(1, owners // 2, lambda i, acc, at=at: step(at + i, acc), parts_ref[at].astype(F32))
        for at in (0, owners // 2)
    ]
    rows4_ref[...] = (sides[0][:16] + sides[1][:16]).astype(BF16)
    half = rows5_ref.shape[0] // 2
    owner = lax.axis_index("dp") // 2 * (owners // 2) + lax.axis_index("space")
    start = owner * (27 * half // owners) % half
    empty = jnp.zeros((half + 16 - parts_ref.shape[1], parts_ref.shape[2]), F32)
    for i, side in enumerate(sides):
        rows5 = jnp.concatenate([side[16:], empty], axis=0)
        rows5_ref[pl.ds(i * half, half), :] = pltpu.roll(rows5, start, 0).astype(BF16)


def summed(parts):
    return call(sum_kernel, "sums", (((16, 128), BF16), ((128, 128), BF16)), (parts,))


def finish_kernel(mine_ref, theirs_ref, weight4_ref, weight5_ref):
    core = lax.axis_index("dp") % 2
    first = lax.axis_index("space") % 16 * 4
    share = 27 * 64 // mine_ref.shape[0]
    row = lax.broadcasted_iota(jnp.int32, (4, 128), 0)
    for o in range(27):
        for side, ref in ((core, mine_ref), (1 - core, theirs_ref)):
            for k in range(2):
                at = pl.multiple_of(side * 32 + k * 16, 16)
                weight4_ref[o, pl.ds(at, 16), :] = ref[2 * o + k].astype(F32)[:16]
            start = o * 64 + first
            owner = start // share
            low = ref[owner].astype(F32)[16:20]
            high = ref[(start + 3) // share].astype(F32)[16:20]
            at = pl.multiple_of(side * 128, 128)
            weight5_ref[o, :, pl.ds(at, 128)] = jnp.where(
                row < (owner + 1) * share - start, low, high
            )


def finished(mine, theirs):
    weight4, weight5 = pl.pallas_call(
        finish_kernel,
        out_shape=(
            jax.ShapeDtypeStruct((27, 64, 128), F32),
            jax.ShapeDtypeStruct((27, 4, 256), F32),
        ),
        in_specs=[VMEM] * 2,
        out_specs=(VMEM, VMEM),
        name="finish",
    )(*[pltpu.with_memory_space_constraint(x, pltpu.VMEM) for x in (mine, theirs)])
    return weight4.transpose(0, 2, 1), weight5.transpose(0, 2, 1)


def per_device(volumes, cotangent, conv4_weight, conv5_weight):
    odd = lax.axis_index("space") % 2
    first4 = swapped(lax.dynamic_index_in_dim(volumes, 1 - odd, 0, keepdims=False), 0)
    second4 = swapped(lax.dynamic_index_in_dim(volumes, odd, 0, keepdims=False), 1)
    arranged4 = conv4_weight.transpose(1, 0, 2).reshape(conv4_weight.shape[1], -1)
    part4, stack4 = own4(volumes, arranged4)
    pooled, slope, stack4 = layer4(first4, second4, arranged4, part4, stack4)
    part5, back5 = own5(pooled, conv5_weight)
    output5, inward, to_first, to_second, mine5, share5 = layer5(
        pooled, swapped(pooled, 0), swapped(pooled, 1), conv5_weight, cotangent[0], part5, back5
    )
    first, second = swapped(to_first, 0), swapped(to_second, 1)
    outer = conv5_weight.shape[1]
    chip5 = other_chip(share5)
    core5 = other_core(regrouped(mine5, chip5, outer))
    part = weight5_part(mine5, chip5, core5, outer)
    keep, send = weight4_parts(inward, first, second, stack4, slope)
    axes = ("dp", "space")
    spaces, groups = lax.axis_size("space"), lax.axis_size("dp")
    per_core = [
        [dp * spaces + s for dp in range(core, groups, 2) for s in range(spaces)]
        for core in range(2)
    ]

    def exchange(parts):
        return lax.all_to_all(
            parts, axes, split_axis=0, concat_axis=0, tiled=True, axis_index_groups=per_core
        )

    rows4, rows5 = summed(exchange(paired(keep, other_core(send), part)))
    rows5 = jnp.pad(rows5.reshape(spaces, 4, 128), ((0, 0), (0, 4), (0, 0)))
    outgoing = jnp.concatenate(
        [
            jnp.broadcast_to(rows4, (64, 16, 128)),
            jnp.broadcast_to(rows5, (2, spaces, 8, 128)).reshape(64, 8, 128),
        ],
        axis=1,
    )
    mine = exchange(outgoing)
    weight4, weight5 = finished(mine, other_core(mine))
    return (output5[None], weight4, weight5)


def solution(mesh):
    placed = (P("space", "dp", None, None), P("space", "dp", None, None), P(), P())
    return jax.shard_map(
        per_device,
        mesh=mesh,
        in_specs=placed,
        out_specs=(P("space", "dp", None, None), P(), P(None, None, "space")),
        check_vma=False,
    )
```

```python
import jax
import jax.numpy as jnp
from jax import lax
from jax.experimental import pallas as pl
from jax.experimental.pallas import tpu as pltpu
from jax.sharding import PartitionSpec as P

HEIGHT = 32
WIDTH = 16
TAPS = tuple((b, e) for b in (-1, 0, 1) for e in (-1, 0, 1))
BF16 = jnp.bfloat16
F32 = jnp.float32
VMEM = pl.BlockSpec(memory_space=pltpu.VMEM)


def call(kernel, name, outputs, operands, scratch=(), room=12, flops=0, aliases=None):
    moved = sum(x.size * x.dtype.itemsize for x in operands)
    return pl.pallas_call(
        kernel,
        out_shape=tuple(pltpu.VMEM(shape, dtype) for shape, dtype in outputs),
        in_specs=[VMEM] * len(operands),
        out_specs=tuple(VMEM for _ in outputs),
        scratch_shapes=list(scratch),
        input_output_aliases=aliases or {},
        compiler_params=pltpu.CompilerParams(vmem_limit_bytes=room * 2**20),
        cost_estimate=pl.CostEstimate(flops=flops, bytes_accessed=moved, transcendentals=0),
        name=name,
    )(*[pltpu.with_memory_space_constraint(x, pltpu.VMEM) for x in operands])


def swap_pairs(groups, count, phase):
    pairs = []
    for group in range(groups):
        for here in range(count):
            there = here + 1 if here % 2 == phase else here - 1
            if 0 <= there < count:
                pairs.append((group * count + here, group * count + there))
            else:
                pairs.append((group * count + here, (group ^ 1) * count + here))
    return pairs


def swapped(values, phase):
    pairs = swap_pairs(lax.axis_size("dp"), lax.axis_size("space"), phase)
    return lax.ppermute(values, ("dp", "space"), pairs)


def other_core(values):
    count = lax.axis_size("dp")
    return lax.ppermute(values, "dp", [(i, i ^ 1) for i in range(count)])


def other_chip(values):
    count = lax.axis_size("dp")
    return lax.ppermute(values, "dp", [(i, i ^ 2) for i in range(count)])


def neighbours(first, second):
    here = lax.axis_index("space")
    odd = here % 2 == 1
    below = jnp.where(odd, first, second)
    above = jnp.where(odd, second, first)
    below = jnp.where(here == 0, jnp.zeros_like(below), below)
    above = jnp.where(here == lax.axis_size("space") - 1, jnp.zeros_like(above), above)
    return below, above


def keep_mask(b, e, row_len, length):
    lane = lax.broadcasted_iota(jnp.int32, (1, length), 1)
    column = lane % row_len + e
    row = lane // row_len + b
    inside = (column >= 0) & (column < row_len) & (row >= 0) & (row < length // row_len)
    return inside.astype(F32).astype(BF16)


def tap(values, b, e, row_len):
    length = values.shape[1]
    offset = b * row_len + e
    if offset == 0:
        return values
    return pltpu.roll(values, -offset % length, 1) * keep_mask(b, e, row_len, length)


def dot(left, right):
    return jnp.dot(left, right, preferred_element_type=F32)


def dot_rows(left, right):
    return lax.dot_general(left, right, (((1,), (1,)), ((), ())), preferred_element_type=F32)


def pool_matrix(fine_axis, shape):
    fine = lax.broadcasted_iota(jnp.int32, shape, fine_axis)
    coarse = lax.broadcasted_iota(jnp.int32, shape, 1 - fine_axis)
    owner = (fine // (2 * WIDTH)) * (WIDTH // 2) + (fine % WIDTH) // 2
    return (owner == coarse).astype(BF16)


def stack_plane(plane, out_ref, j, n):
    chans, cells = plane.shape
    for t, (b, e) in enumerate(TAPS):
        out_ref[pl.ds((j * len(TAPS) + t) * chans, chans), pl.ds(n * cells, cells)] = tap(
            plane, b, e, WIDTH
        )


def own4_kernel(vol_ref, weight_ref, part_ref, stack_ref):
    rows = len(TAPS) * vol_ref.shape[2]
    for n in range(2):
        for d in range(2):
            stack_plane(vol_ref[d, n], stack_ref, 1 + d, n)
    for d in range(2):
        part_ref[d] = dot(
            weight_ref[:, (1 - d) * rows : (3 - d) * rows], stack_ref[pl.ds(rows, 2 * rows), :]
        )


def own4(volumes, weight):
    vols, chans, cells = volumes.shape[1:]
    return call(
        own4_kernel,
        "own4",
        (
            ((2, weight.shape[0], vols * cells), F32),
            ((4 * len(TAPS) * chans, vols * cells), BF16),
        ),
        (volumes, weight),
        flops=2 * weight.size * 2 * vols * cells,
    )


def layer4_kernel(
    first_ref, second_ref, weight_ref, part_ref, _, pooled_ref, slope_ref, stack_ref
):
    chans, cells = first_ref.shape[1:]
    rows = len(TAPS) * chans
    for n in range(2):
        below, above = neighbours(first_ref[n], second_ref[n])
        stack_plane(below, stack_ref, 0, n)
        stack_plane(above, stack_ref, 3, n)
    pool = pool_matrix(0, (cells, cells // 4))
    for n in range(2):
        lanes = pl.ds(n * cells, cells)
        total = None
        for d in range(2):
            preact = part_ref[d, :, lanes] + dot(
                weight_ref[:, 2 * d * rows : (2 * d + 1) * rows],
                stack_ref[pl.ds(3 * d * rows, rows), lanes],
            )
            sig = jax.nn.sigmoid(preact)
            slope_ref[d, :, lanes] = sig * (1.0 + preact * (1.0 - sig)) * 0.125
            active = preact * sig
            total = active if total is None else total + active
        high = total.astype(BF16)
        low = (total - high.astype(F32)).astype(BF16)
        pooled = (dot(high, pool) + dot(low, pool)) * 0.125
        pooled_ref[:, pl.ds(n * cells // 4, cells // 4)] = pooled.astype(BF16)


def layer4(first, second, weight, part, stack):
    lanes = stack.shape[1]
    return call(
        layer4_kernel,
        "layer4",
        (((weight.shape[0], lanes // 4), BF16), (part.shape, F32), (stack.shape, BF16)),
        (first, second, weight, part, stack),
        flops=2 * weight.size * lanes,
        aliases={3: 1, 4: 2},
    )


def spread_taps(planes, out_ref, row_len, cells, sign):
    chans = planes[0].shape[0]
    for j, plane in enumerate(planes):
        for n in range(plane.shape[1] // cells):
            part = plane[:, n * cells : (n + 1) * cells]
            for t, (b, e) in enumerate(TAPS):
                out_ref[pl.ds((j * len(TAPS) + t) * chans, chans), pl.ds(n * cells, cells)] = tap(
                    part, sign * b, sign * e, row_len
                )


def tapped(plane, row_len, cells, b, e):
    parts = [
        tap(plane[:, at : at + cells], b, e, row_len) for at in range(0, plane.shape[1], cells)
    ]
    return jnp.concatenate(parts, axis=1)


def convolved5(weight_ref, plane, cells, a):
    first = (a + 1) * len(TAPS)
    total = None
    for t in range(0, len(TAPS), 2):
        group = range(t, min(t + 2, len(TAPS)))
        weight = jnp.concatenate([weight_ref[first + i] for i in group], axis=1)
        shifts = jnp.concatenate(
            [tapped(plane, WIDTH // 2, cells, *TAPS[i]) for i in group], axis=0
        )
        part = dot(weight, shifts)
        total = part if total is None else total + part
    return total


def own5_kernel(pooled_ref, weight_ref, part_ref, back_ref):
    chans = pooled_ref.shape[0]
    cells = pooled_ref.shape[1] // 2
    part_ref[...] = convolved5(weight_ref, pooled_ref[...], cells, 0)
    for o in range(27):
        a, t = divmod(o, len(TAPS))
        back_ref[t, pl.ds((0, 2, 1)[a] * chans, chans), :] = weight_ref[o].T


def own5(pooled, weight):
    chans, lanes = pooled.shape
    outer = weight.shape[1]
    return call(
        own5_kernel,
        "own5",
        (((outer, lanes), F32), ((len(TAPS), 3 * chans, outer), BF16)),
        (pooled, weight),
        flops=2 * weight.size * lanes // 3,
    )


def inward_part(back_ref, grad, cells, first, rows):
    total = None
    for t, (b, e) in enumerate(TAPS):
        shifts = tapped(grad, WIDTH // 2, cells, -b, -e)
        part = dot(back_ref[t, pl.ds(first, rows), :], shifts)
        total = part if total is None else total + part
    return total


def own_inward_kernel(mine_ref, back_ref, inward_ref):
    outer = back_ref.shape[2]
    chans, lanes = inward_ref.shape
    grad = mine_ref[pl.ds(0, outer), :]
    inward_ref[...] = inward_part(back_ref, grad, lanes // 2, 2 * chans, chans)


def own_inward(mine, back):
    chans = back.shape[1] // 3
    (inward,) = call(
        own_inward_kernel,
        "own_inward",
        (((chans, mine.shape[1]), F32),),
        (mine, back),
        flops=2 * back.size * mine.shape[1] // 3,
    )
    return inward


def layer5_kernel(
    pooled_ref, first_ref, second_ref, weight_ref, cot_ref, part_ref, back_ref,
    out_ref, to_first_ref, to_second_ref, mine_ref, share_ref,
):
    chans = pooled_ref.shape[0]
    outer = part_ref.shape[0]
    cells = cot_ref.shape[2]
    below, above = neighbours(first_ref[...], second_ref[...])
    preact = part_ref[...] + convolved5(weight_ref, below, cells, -1)
    preact += convolved5(weight_ref, above, cells, 1)
    sig = jax.nn.sigmoid(preact)
    active = preact * sig
    slope = sig * (1.0 + preact * (1.0 - sig))
    grads = []
    for n in range(cot_ref.shape[0]):
        lanes = slice(n * cells, (n + 1) * cells)
        out_ref[n] = active[:, lanes].astype(BF16)
        grads.append((cot_ref[n].astype(F32) * slope[:, lanes]).astype(BF16))
    grad = jnp.concatenate(grads, axis=1)
    mine_ref[pl.ds(0, outer), :] = grad
    share_ref[pl.ds(0, outer), :] = grad
    inward = inward_part(back_ref, grad, cells, 0, 2 * chans)
    down, up = inward[:chans].astype(BF16), inward[chans:].astype(BF16)
    odd = lax.axis_index("space") % 2 == 1
    to_first_ref[...] = jnp.where(odd, down, up)
    to_second_ref[...] = jnp.where(odd, up, down)
    chip = lax.axis_index("dp") // 2
    half = chans // 2
    for j, plane in enumerate((below, pooled_ref[...], above)):
        at = pl.ds(outer + j * half, half)
        mine_ref[at, :] = jnp.where(chip == 0, plane[:half], plane[half:])
        share_ref[at, :] = jnp.where(chip == 0, plane[half:], plane[:half])


def layer5(pooled, first, second, weight, cot, part, back):
    vols, outer, cells = cot.shape
    chans, lanes = pooled.shape
    return call(
        layer5_kernel,
        "layer5",
        (
            ((vols, outer, cells), BF16),
            ((chans, lanes), BF16),
            ((chans, lanes), BF16),
            ((outer + 3 * chans // 2, lanes), BF16),
            ((outer + 3 * chans // 2, lanes), BF16),
        ),
        (pooled, first, second, weight, cot, part, back),
        flops=3 * weight.size * lanes,
    )


def stack_window(ref, first, rows, out_ref, i):
    lanes = ref.shape[1]
    chans = rows // 3
    planes = tuple(ref[pl.ds(first + j * chans, chans), :] for j in range(3))
    spread_taps(planes, out_ref.at[:, pl.ds(i * lanes, lanes)], WIDTH // 2, lanes // 2, 1)


def regroup_kernel(mine_ref, got_ref, made_ref, send_ref, stack_ref, out_ref, sem):
    copy = pltpu.make_async_copy(made_ref, out_ref, sem)
    copy.start()
    core = lax.axis_index("dp") % 2
    rows = send_ref.shape[0] // 2
    half = mine_ref.shape[0] - rows
    for i, ref in enumerate((mine_ref, got_ref)):
        start = pl.multiple_of((1 - core) * half, half)
        send_ref[pl.ds(i * rows, half), :] = ref[pl.ds(start, half), :]
        send_ref[pl.ds(i * rows + half, rows - half), :] = ref[pl.ds(2 * half, rows - half), :]
        stack_window(ref, 2 * half, rows - half, stack_ref, i)
    copy.wait()


def regrouped(mine, got, made, outer):
    rows = mine.shape[0] - outer // 2
    lanes = mine.shape[1]
    return pl.pallas_call(
        regroup_kernel,
        out_shape=(
            pltpu.VMEM((2 * rows, lanes), BF16),
            pltpu.VMEM((9 * (mine.shape[0] - outer), 4 * lanes), BF16),
            jax.ShapeDtypeStruct(made.shape, made.dtype),
        ),
        in_specs=[VMEM] * 3,
        out_specs=(VMEM, VMEM, pl.BlockSpec(memory_space=pl.ANY)),
        scratch_shapes=[pltpu.SemaphoreType.DMA],
        compiler_params=pltpu.CompilerParams(vmem_limit_bytes=12 * 2**20),
        name="regroup",
    )(*[pltpu.with_memory_space_constraint(x, pltpu.VMEM) for x in (mine, got, made)])


def weight5_kernel(mine_ref, chip_ref, core_ref, _, part_ref, stack_ref, total_ref):
    core = lax.axis_index("dp") % 2
    rows = core_ref.shape[0] // 2
    half = mine_ref.shape[0] - rows
    own = pl.ds(pl.multiple_of(core * half, half), half)
    for i in range(2):
        stack_window(core_ref, i * rows + half, rows - half, stack_ref, 2 + i)
    grads = (mine_ref[own, :], chip_ref[own, :], core_ref[pl.ds(0, half), :], core_ref[pl.ds(rows, half), :])
    grads = jnp.concatenate(grads, axis=1)
    block = stack_ref.shape[0] // 3
    for j in range(3):
        at = pl.ds(j * block, block)
        total_ref[at, :] = dot_rows(stack_ref[at, :], grads)
    total_ref[pl.ds(3 * block, 8), :] = jnp.zeros((8, half), F32)
    owners = part_ref.shape[0]
    for owner in range(owners):
        part_ref[owner, pl.ds(16, 32), :] = total_ref[
            pl.ds(owner * (3 * block // owners), 32), :
        ].astype(BF16)


def weight5_part(mine, chip, core, stack, outer):
    part, _ = call(
        weight5_kernel,
        "weight5",
        (((64, 48, 128), BF16), (stack.shape, BF16)),
        (mine, chip, core, stack),
        scratch=[pltpu.VMEM((stack.shape[0] + 8, outer // 2), F32)],
        flops=stack.size * outer,
        aliases={3: 1},
    )
    return part


def weight4_kernel(
    inward_ref, first_ref, second_ref, stack_ref, slope_ref, keep_ref, send_ref, acc_ref
):
    core = lax.axis_index("dp") % 2
    below, above = neighbours(first_ref[...], second_ref[...])
    inward = (inward_ref[...] + below.astype(F32) + above.astype(F32)).astype(BF16)
    chans = inward.shape[0]
    cells = inward.shape[1] // 2
    unpool = pool_matrix(1, (cells, 4 * cells))
    fine = jnp.concatenate(
        [dot(inward[:, n * cells : (n + 1) * cells], unpool) for n in range(2)], axis=1
    )
    grads = jnp.concatenate(
        [(fine * slope_ref[0]).astype(BF16), (fine * slope_ref[1]).astype(BF16)], axis=0
    )
    grads = grads.T
    rows = stack_ref.shape[0] // 4
    for j in range(4):
        plane = stack_ref[pl.ds(j * rows, rows), :]
        if j == 0:
            acc_ref[pl.ds(0, rows), :] = dot(plane, grads[:, :chans])
        elif j == 3:
            acc_ref[pl.ds(2 * rows, rows), :] += dot(plane, grads[:, chans:])
        else:
            both = dot(plane, grads)
            acc_ref[pl.ds(j * rows, rows), :] = both[:, :chans]
            acc_ref[pl.ds((j - 1) * rows, rows), :] += both[:, chans:]
    inner = rows // len(TAPS)
    share = inner // 4
    for o in range(27):
        for k in range(2):
            mine = pl.multiple_of(o * inner + core * 2 * share + k * share, share)
            theirs = pl.multiple_of(o * inner + (1 - core) * 2 * share + k * share, share)
            keep_ref[2 * o + k] = acc_ref[pl.ds(mine, share), :]
            send_ref[2 * o + k] = acc_ref[pl.ds(theirs, share), :].astype(BF16)


def weight4_parts(inward, first, second, stack, slope):
    chans = inward.shape[0]
    return call(
        weight4_kernel,
        "weight4_parts",
        (((54, 16, 128), F32), ((54, 16, 128), BF16)),
        (inward, first, second, stack, slope),
        scratch=[pltpu.VMEM((3 * stack.shape[0] // 4, chans), F32)],
        flops=3 * stack.size * chans,
    )


def pair_kernel(keep_ref, got_ref, _, part_ref):
    filled, rows = keep_ref.shape[:2]
    for i in range(filled):
        part_ref[i, pl.ds(0, rows), :] = (keep_ref[i] + got_ref[i].astype(F32)).astype(BF16)
    for i in range(filled, part_ref.shape[0]):
        part_ref[i, pl.ds(0, rows), :] = jnp.zeros((rows, part_ref.shape[2]), BF16)


def paired(keep, got, part):
    (part,) = call(pair_kernel, "pairs", ((part.shape, BF16),), (keep, got, part), aliases={2: 0})
    return part


def sum_kernel(parts_ref, rows4_ref, rows5_ref):
    owners = parts_ref.shape[0]
    sides = []
    for side in range(2):
        total = parts_ref[side * owners // 2].astype(F32)
        for i in range(1, owners // 2):
            total += parts_ref[side * owners // 2 + i].astype(F32)
        sides.append(total)
    rows4_ref[...] = (sides[0][:16] + sides[1][:16]).astype(BF16)
    half = rows5_ref.shape[0] // 2
    owner = lax.axis_index("dp") // 2 * (owners // 2) + lax.axis_index("space")
    start = owner * (27 * half // owners) % half
    empty = jnp.zeros((half + 16 - parts_ref.shape[1], parts_ref.shape[2]), F32)
    for i, side in enumerate(sides):
        rows5 = jnp.concatenate([side[16:], empty], axis=0)
        rows5_ref[pl.ds(i * half, half), :] = pltpu.roll(rows5, start, 0).astype(BF16)


def summed(parts):
    return call(sum_kernel, "sums", (((16, 128), BF16), ((128, 128), BF16)), (parts,))


def place_rows(rows_ref, weight4_ref, weight5_ref, side, half4_ref, half5_ref, sems):
    first = lax.axis_index("space") % 16 * 4
    share = 27 * 64 // rows_ref.shape[0]
    row = lax.broadcasted_iota(jnp.int32, (4, 128), 0)
    for o in range(27):
        for k in range(2):
            half4_ref[o, pl.ds(k * 16, 16), :] = rows_ref[2 * o + k].astype(F32)[:16]
    at = pl.multiple_of(side * 32, 32)
    copy4 = pltpu.make_async_copy(half4_ref, weight4_ref.at[:, pl.ds(at, 32), :], sems.at[0])
    copy4.start()
    for o in range(27):
        start = o * 64 + first
        owner = start // share
        low = rows_ref[owner].astype(F32)[16:20]
        high = rows_ref[(start + 3) // share].astype(F32)[16:20]
        half5_ref[o] = jnp.where(row < (owner + 1) * share - start, low, high)
    at = pl.multiple_of(side * 128, 128)
    copy5 = pltpu.make_async_copy(half5_ref, weight5_ref.at[:, :, pl.ds(at, 128)], sems.at[1])
    copy5.start()
    copy4.wait()
    copy5.wait()


def first_half_kernel(rows_ref, weight4_ref, weight5_ref, *scratch):
    place_rows(rows_ref, weight4_ref, weight5_ref, lax.axis_index("dp") % 2, *scratch)


def second_half_kernel(rows_ref, _, __, weight4_ref, weight5_ref, *scratch):
    place_rows(rows_ref, weight4_ref, weight5_ref, 1 - lax.axis_index("dp") % 2, *scratch)


def placed_half(kernel, name, rows, *halves):
    anywhere = pl.BlockSpec(memory_space=pl.ANY)
    return pl.pallas_call(
        kernel,
        out_shape=(
            jax.ShapeDtypeStruct((27, 64, 128), F32),
            jax.ShapeDtypeStruct((27, 4, 256), F32),
        ),
        in_specs=[VMEM] + [anywhere] * len(halves),
        out_specs=(anywhere, anywhere),
        scratch_shapes=[
            pltpu.VMEM((27, 32, 128), F32),
            pltpu.VMEM((27, 4, 128), F32),
            pltpu.SemaphoreType.DMA((2,)),
        ],
        input_output_aliases={i + 1: i for i in range(len(halves))},
        name=name,
    )(pltpu.with_memory_space_constraint(rows, pltpu.VMEM), *halves)


def per_device(volumes, cotangent, conv4_weight, conv5_weight):
    odd = lax.axis_index("space") % 2
    first4 = swapped(lax.dynamic_index_in_dim(volumes, 1 - odd, 0, keepdims=False), 0)
    second4 = swapped(lax.dynamic_index_in_dim(volumes, odd, 0, keepdims=False), 1)
    arranged4 = conv4_weight.transpose(1, 0, 2).reshape(conv4_weight.shape[1], -1)
    part4, stack4 = own4(volumes, arranged4)
    pooled, slope, stack4 = layer4(first4, second4, arranged4, part4, stack4)
    part5, back5 = own5(pooled, conv5_weight)
    output5, to_first, to_second, mine5, share5 = layer5(
        pooled, swapped(pooled, 0), swapped(pooled, 1), conv5_weight, cotangent[0], part5, back5
    )
    first, second = swapped(to_first, 0), swapped(to_second, 1)
    inward = own_inward(mine5, back5)
    outer = conv5_weight.shape[1]
    chip5 = other_chip(share5)
    send5, chips5, output5 = regrouped(mine5, chip5, output5, outer)
    part = weight5_part(mine5, chip5, other_core(send5), chips5, outer)
    keep, send = weight4_parts(inward, first, second, stack4, slope)
    axes = ("dp", "space")
    spaces, groups = lax.axis_size("space"), lax.axis_size("dp")
    per_core = [
        [dp * spaces + s for dp in range(core, groups, 2) for s in range(spaces)]
        for core in range(2)
    ]

    def exchange(parts):
        return lax.all_to_all(
            parts, axes, split_axis=0, concat_axis=0, tiled=True, axis_index_groups=per_core
        )

    rows4, rows5 = summed(exchange(paired(keep, other_core(send), part)))
    rows5 = jnp.pad(rows5.reshape(spaces, 4, 128), ((0, 0), (0, 4), (0, 0)))
    outgoing = jnp.concatenate(
        [
            jnp.broadcast_to(rows4, (64, 16, 128)),
            jnp.broadcast_to(rows5, (2, spaces, 8, 128)).reshape(64, 8, 128),
        ],
        axis=1,
    )
    mine = exchange(outgoing)
    halves = placed_half(first_half_kernel, "first_half", mine)
    weight4, weight5 = placed_half(second_half_kernel, "second_half", other_core(mine), *halves)
    return (output5[None], weight4.transpose(0, 2, 1), weight5.transpose(0, 2, 1))


def solution(mesh):
    placed = (P("space", "dp", None, None), P("space", "dp", None, None), P(), P())
    return jax.shard_map(
        per_device,
        mesh=mesh,
        in_specs=placed,
        out_specs=(P("space", "dp", None, None), P(), P(None, None, "space")),
        check_vma=False,
    )
```

```python
import jax
import jax.numpy as jnp
from jax import lax
from jax.experimental import pallas as pl
from jax.experimental.pallas import tpu as pltpu
from jax.sharding import PartitionSpec as P

HEIGHT = 32
WIDTH = 16
TAPS = tuple((b, e) for b in (-1, 0, 1) for e in (-1, 0, 1))
BF16 = jnp.bfloat16
F32 = jnp.float32
VMEM = pl.BlockSpec(memory_space=pltpu.VMEM)


def call(kernel, name, outputs, operands, scratch=(), room=12, flops=0, aliases=None):
    moved = sum(x.size * x.dtype.itemsize for x in operands)
    return pl.pallas_call(
        kernel,
        out_shape=tuple(pltpu.VMEM(shape, dtype) for shape, dtype in outputs),
        in_specs=[VMEM] * len(operands),
        out_specs=tuple(VMEM for _ in outputs),
        scratch_shapes=list(scratch),
        input_output_aliases=aliases or {},
        compiler_params=pltpu.CompilerParams(vmem_limit_bytes=room * 2**20),
        cost_estimate=pl.CostEstimate(flops=flops, bytes_accessed=moved, transcendentals=0),
        name=name,
    )(*[pltpu.with_memory_space_constraint(x, pltpu.VMEM) for x in operands])


def swap_pairs(groups, count, phase):
    pairs = []
    for group in range(groups):
        for here in range(count):
            there = here + 1 if here % 2 == phase else here - 1
            if 0 <= there < count:
                pairs.append((group * count + here, group * count + there))
            else:
                pairs.append((group * count + here, (group ^ 1) * count + here))
    return pairs


def swapped(values, phase):
    pairs = swap_pairs(lax.axis_size("dp"), lax.axis_size("space"), phase)
    return lax.ppermute(values, ("dp", "space"), pairs)


def other_core(values):
    count = lax.axis_size("dp")
    return lax.ppermute(values, "dp", [(i, i ^ 1) for i in range(count)])


def other_chip(values):
    count = lax.axis_size("dp")
    return lax.ppermute(values, "dp", [(i, i ^ 2) for i in range(count)])


def neighbours(first, second):
    here = lax.axis_index("space")
    odd = here % 2 == 1
    below = jnp.where(odd, first, second)
    above = jnp.where(odd, second, first)
    below = jnp.where(here == 0, jnp.zeros_like(below), below)
    above = jnp.where(here == lax.axis_size("space") - 1, jnp.zeros_like(above), above)
    return below, above


def keep_mask(b, e, row_len, length):
    lane = lax.broadcasted_iota(jnp.int32, (1, length), 1)
    column = lane % row_len + e
    row = lane // row_len + b
    inside = (column >= 0) & (column < row_len) & (row >= 0) & (row < length // row_len)
    return inside.astype(F32).astype(BF16)


def tap(values, b, e, row_len):
    length = values.shape[1]
    offset = b * row_len + e
    if offset == 0:
        return values
    return pltpu.roll(values, -offset % length, 1) * keep_mask(b, e, row_len, length)


def dot(left, right):
    return jnp.dot(left, right, preferred_element_type=F32)


def dot_rows(left, right):
    return lax.dot_general(left, right, (((1,), (1,)), ((), ())), preferred_element_type=F32)


def pool_matrix(fine_axis, shape):
    fine = lax.broadcasted_iota(jnp.int32, shape, fine_axis)
    coarse = lax.broadcasted_iota(jnp.int32, shape, 1 - fine_axis)
    owner = (fine // (2 * WIDTH)) * (WIDTH // 2) + (fine % WIDTH) // 2
    return (owner == coarse).astype(BF16)


def stack_plane(plane, out_ref, j, n):
    chans, cells = plane.shape
    for t, (b, e) in enumerate(TAPS):
        out_ref[pl.ds((j * len(TAPS) + t) * chans, chans), pl.ds(n * cells, cells)] = tap(
            plane, b, e, WIDTH
        )


def own4_kernel(vol_ref, weight_ref, part_ref, stack_ref):
    rows = len(TAPS) * vol_ref.shape[2]
    for n in range(2):
        for d in range(2):
            stack_plane(vol_ref[d, n], stack_ref, 1 + d, n)
    for d in range(2):
        part_ref[d] = dot(
            weight_ref[:, (1 - d) * rows : (3 - d) * rows], stack_ref[pl.ds(rows, 2 * rows), :]
        )


def own4(volumes, weight):
    vols, chans, cells = volumes.shape[1:]
    return call(
        own4_kernel,
        "own4",
        (
            ((2, weight.shape[0], vols * cells), F32),
            ((4 * len(TAPS) * chans, vols * cells), BF16),
        ),
        (volumes, weight),
        flops=2 * weight.size * 2 * vols * cells,
    )


def layer4_kernel(
    first_ref, second_ref, weight_ref, part_ref, _, pooled_ref, slope_ref, stack_ref
):
    chans, cells = first_ref.shape[1:]
    rows = len(TAPS) * chans
    for n in range(2):
        below, above = neighbours(first_ref[n], second_ref[n])
        stack_plane(below, stack_ref, 0, n)
        stack_plane(above, stack_ref, 3, n)
    pool = pool_matrix(0, (cells, cells // 4))
    for n in range(2):
        lanes = pl.ds(n * cells, cells)
        total = None
        for d in range(2):
            preact = part_ref[d, :, lanes] + dot(
                weight_ref[:, 2 * d * rows : (2 * d + 1) * rows],
                stack_ref[pl.ds(3 * d * rows, rows), lanes],
            )
            sig = jax.nn.sigmoid(preact)
            slope_ref[d, :, lanes] = sig * (1.0 + preact * (1.0 - sig)) * 0.125
            active = preact * sig
            total = active if total is None else total + active
        high = total.astype(BF16)
        low = (total - high.astype(F32)).astype(BF16)
        pooled = (dot(high, pool) + dot(low, pool)) * 0.125
        pooled_ref[:, pl.ds(n * cells // 4, cells // 4)] = pooled.astype(BF16)


def layer4(first, second, weight, part, stack):
    lanes = stack.shape[1]
    return call(
        layer4_kernel,
        "layer4",
        (((weight.shape[0], lanes // 4), BF16), (part.shape, F32), (stack.shape, BF16)),
        (first, second, weight, part, stack),
        flops=2 * weight.size * lanes,
        aliases={3: 1, 4: 2},
    )


def spread_taps(planes, out_ref, row_len, cells, sign):
    chans = planes[0].shape[0]
    for j, plane in enumerate(planes):
        for n in range(plane.shape[1] // cells):
            part = plane[:, n * cells : (n + 1) * cells]
            for t, (b, e) in enumerate(TAPS):
                out_ref[pl.ds((j * len(TAPS) + t) * chans, chans), pl.ds(n * cells, cells)] = tap(
                    part, sign * b, sign * e, row_len
                )


def tapped(plane, row_len, cells, b, e):
    parts = [
        tap(plane[:, at : at + cells], b, e, row_len) for at in range(0, plane.shape[1], cells)
    ]
    return jnp.concatenate(parts, axis=1)


def convolved5(weight_ref, plane, cells, a):
    first = (a + 1) * len(TAPS)
    total = None
    for t in range(0, len(TAPS), 2):
        group = range(t, min(t + 2, len(TAPS)))
        weight = jnp.concatenate([weight_ref[first + i] for i in group], axis=1)
        shifts = jnp.concatenate(
            [tapped(plane, WIDTH // 2, cells, *TAPS[i]) for i in group], axis=0
        )
        part = dot(weight, shifts)
        total = part if total is None else total + part
    return total


def own5_kernel(pooled_ref, weight_ref, part_ref, back_ref):
    chans = pooled_ref.shape[0]
    cells = pooled_ref.shape[1] // 2
    part_ref[...] = convolved5(weight_ref, pooled_ref[...], cells, 0)
    for o in range(27):
        a, t = divmod(o, len(TAPS))
        back_ref[t, pl.ds((0, 2, 1)[a] * chans, chans), :] = weight_ref[o].T


def own5(pooled, weight):
    chans, lanes = pooled.shape
    outer = weight.shape[1]
    return call(
        own5_kernel,
        "own5",
        (((outer, lanes), F32), ((len(TAPS), 3 * chans, outer), BF16)),
        (pooled, weight),
        flops=2 * weight.size * lanes // 3,
    )


def inward_part(back_ref, grad, cells, first, rows):
    total = None
    for t, (b, e) in enumerate(TAPS):
        shifts = tapped(grad, WIDTH // 2, cells, -b, -e)
        part = dot(back_ref[t, pl.ds(first, rows), :], shifts)
        total = part if total is None else total + part
    return total


def own_inward_kernel(mine_ref, back_ref, inward_ref):
    outer = back_ref.shape[2]
    chans, lanes = inward_ref.shape
    grad = mine_ref[pl.ds(0, outer), :]
    inward_ref[...] = inward_part(back_ref, grad, lanes // 2, 2 * chans, chans)


def own_inward(mine, back):
    chans = back.shape[1] // 3
    (inward,) = call(
        own_inward_kernel,
        "own_inward",
        (((chans, mine.shape[1]), F32),),
        (mine, back),
        flops=2 * back.size * mine.shape[1] // 3,
    )
    return inward


def layer5_kernel(
    pooled_ref, first_ref, second_ref, weight_ref, cot_ref, part_ref, back_ref,
    out_ref, to_first_ref, to_second_ref, mine_ref, share_ref,
):
    chans = pooled_ref.shape[0]
    outer = part_ref.shape[0]
    cells = cot_ref.shape[2]
    below, above = neighbours(first_ref[...], second_ref[...])
    preact = part_ref[...] + convolved5(weight_ref, below, cells, -1)
    preact += convolved5(weight_ref, above, cells, 1)
    sig = jax.nn.sigmoid(preact)
    active = preact * sig
    slope = sig * (1.0 + preact * (1.0 - sig))
    grads = []
    for n in range(cot_ref.shape[0]):
        lanes = slice(n * cells, (n + 1) * cells)
        out_ref[n] = active[:, lanes].astype(BF16)
        grads.append((cot_ref[n].astype(F32) * slope[:, lanes]).astype(BF16))
    grad = jnp.concatenate(grads, axis=1)
    mine_ref[pl.ds(0, outer), :] = grad
    share_ref[pl.ds(0, outer), :] = grad
    inward = inward_part(back_ref, grad, cells, 0, 2 * chans)
    down, up = inward[:chans].astype(BF16), inward[chans:].astype(BF16)
    odd = lax.axis_index("space") % 2 == 1
    to_first_ref[...] = jnp.where(odd, down, up)
    to_second_ref[...] = jnp.where(odd, up, down)
    chip = lax.axis_index("dp") // 2
    half = chans // 2
    for j, plane in enumerate((below, pooled_ref[...], above)):
        at = pl.ds(outer + j * half, half)
        mine_ref[at, :] = jnp.where(chip == 0, plane[:half], plane[half:])
        share_ref[at, :] = jnp.where(chip == 0, plane[half:], plane[:half])


def layer5(pooled, first, second, weight, cot, part, back):
    vols, outer, cells = cot.shape
    chans, lanes = pooled.shape
    return call(
        layer5_kernel,
        "layer5",
        (
            ((vols, outer, cells), BF16),
            ((chans, lanes), BF16),
            ((chans, lanes), BF16),
            ((outer + 3 * chans // 2, lanes), BF16),
            ((outer + 3 * chans // 2, lanes), BF16),
        ),
        (pooled, first, second, weight, cot, part, back),
        flops=3 * weight.size * lanes,
    )


def stack_window(ref, first, rows, out_ref, i):
    lanes = ref.shape[1]
    chans = rows // 3
    planes = tuple(ref[pl.ds(first + j * chans, chans), :] for j in range(3))
    spread_taps(planes, out_ref.at[:, pl.ds(i * lanes, lanes)], WIDTH // 2, lanes // 2, 1)


def regroup_kernel(mine_ref, got_ref, made_ref, send_ref, stack_ref, out_ref, sem):
    copy = pltpu.make_async_copy(made_ref, out_ref, sem)
    copy.start()
    core = lax.axis_index("dp") % 2
    rows = send_ref.shape[0] // 2
    half = mine_ref.shape[0] - rows
    for i, ref in enumerate((mine_ref, got_ref)):
        start = pl.multiple_of((1 - core) * half, half)
        send_ref[pl.ds(i * rows, half), :] = ref[pl.ds(start, half), :]
        send_ref[pl.ds(i * rows + half, rows - half), :] = ref[pl.ds(2 * half, rows - half), :]
        stack_window(ref, 2 * half, rows - half, stack_ref, i)
    copy.wait()


def regrouped(mine, got, made, outer):
    rows = mine.shape[0] - outer // 2
    lanes = mine.shape[1]
    return pl.pallas_call(
        regroup_kernel,
        out_shape=(
            pltpu.VMEM((2 * rows, lanes), BF16),
            pltpu.VMEM((9 * (mine.shape[0] - outer), 4 * lanes), BF16),
            jax.ShapeDtypeStruct(made.shape, made.dtype),
        ),
        in_specs=[VMEM] * 3,
        out_specs=(VMEM, VMEM, pl.BlockSpec(memory_space=pl.ANY)),
        scratch_shapes=[pltpu.SemaphoreType.DMA],
        compiler_params=pltpu.CompilerParams(vmem_limit_bytes=12 * 2**20),
        name="regroup",
    )(*[pltpu.with_memory_space_constraint(x, pltpu.VMEM) for x in (mine, got, made)])


def weight5_kernel(mine_ref, chip_ref, core_ref, _, part_ref, stack_ref, total_ref):
    core = lax.axis_index("dp") % 2
    rows = core_ref.shape[0] // 2
    half = mine_ref.shape[0] - rows
    own = pl.ds(pl.multiple_of(core * half, half), half)
    for i in range(2):
        stack_window(core_ref, i * rows + half, rows - half, stack_ref, 2 + i)
    grads = (mine_ref[own, :], chip_ref[own, :], core_ref[pl.ds(0, half), :], core_ref[pl.ds(rows, half), :])
    grads = jnp.concatenate(grads, axis=1)
    block = stack_ref.shape[0] // 3
    for j in range(3):
        at = pl.ds(j * block, block)
        total_ref[at, :] = dot_rows(stack_ref[at, :], grads)
    total_ref[pl.ds(3 * block, 8), :] = jnp.zeros((8, half), F32)
    owners = part_ref.shape[0]
    for owner in range(owners):
        part_ref[owner, pl.ds(16, 32), :] = total_ref[
            pl.ds(owner * (3 * block // owners), 32), :
        ].astype(BF16)


def weight5_part(mine, chip, core, stack, outer):
    part, _ = call(
        weight5_kernel,
        "weight5",
        (((64, 48, 128), BF16), (stack.shape, BF16)),
        (mine, chip, core, stack),
        scratch=[pltpu.VMEM((stack.shape[0] + 8, outer // 2), F32)],
        flops=stack.size * outer,
        aliases={3: 1},
    )
    return part


def weight4_kernel(
    inward_ref, first_ref, second_ref, stack_ref, slope_ref, keep_ref, send_ref, acc_ref
):
    core = lax.axis_index("dp") % 2
    below, above = neighbours(first_ref[...], second_ref[...])
    inward = (inward_ref[...] + below.astype(F32) + above.astype(F32)).astype(BF16)
    chans = inward.shape[0]
    cells = inward.shape[1] // 2
    unpool = pool_matrix(1, (cells, 4 * cells))
    fine = jnp.concatenate(
        [dot(inward[:, n * cells : (n + 1) * cells], unpool) for n in range(2)], axis=1
    )
    grads = jnp.concatenate(
        [(fine * slope_ref[0]).astype(BF16), (fine * slope_ref[1]).astype(BF16)], axis=0
    )
    grads = grads.T
    rows = stack_ref.shape[0] // 4
    for j in range(4):
        plane = stack_ref[pl.ds(j * rows, rows), :]
        if j == 0:
            acc_ref[pl.ds(0, rows), :] = dot(plane, grads[:, :chans])
        elif j == 3:
            acc_ref[pl.ds(2 * rows, rows), :] += dot(plane, grads[:, chans:])
        else:
            both = dot(plane, grads)
            acc_ref[pl.ds(j * rows, rows), :] = both[:, :chans]
            acc_ref[pl.ds((j - 1) * rows, rows), :] += both[:, chans:]
    inner = rows // len(TAPS)
    share = inner // 4
    for o in range(27):
        for k in range(2):
            mine = pl.multiple_of(o * inner + core * 2 * share + k * share, share)
            theirs = pl.multiple_of(o * inner + (1 - core) * 2 * share + k * share, share)
            keep_ref[2 * o + k] = acc_ref[pl.ds(mine, share), :]
            send_ref[2 * o + k] = acc_ref[pl.ds(theirs, share), :].astype(BF16)


def weight4_parts(inward, first, second, stack, slope):
    chans = inward.shape[0]
    return call(
        weight4_kernel,
        "weight4_parts",
        (((54, 16, 128), F32), ((54, 16, 128), BF16)),
        (inward, first, second, stack, slope),
        scratch=[pltpu.VMEM((3 * stack.shape[0] // 4, chans), F32)],
        flops=3 * stack.size * chans,
    )


def pair_kernel(keep_ref, got_ref, _, part_ref):
    filled, rows = keep_ref.shape[:2]
    for i in range(filled):
        part_ref[i, pl.ds(0, rows), :] = (keep_ref[i] + got_ref[i].astype(F32)).astype(BF16)
    for i in range(filled, part_ref.shape[0]):
        part_ref[i, pl.ds(0, rows), :] = jnp.zeros((rows, part_ref.shape[2]), BF16)


def paired(keep, got, part):
    (part,) = call(pair_kernel, "pairs", ((part.shape, BF16),), (keep, got, part), aliases={2: 0})
    return part


def sum_kernel(parts_ref, rows4_ref, rows5_ref):
    owners = parts_ref.shape[0]
    sides = []
    for side in range(2):
        total = parts_ref[side * owners // 2].astype(F32)
        for i in range(1, owners // 2):
            total += parts_ref[side * owners // 2 + i].astype(F32)
        sides.append(total)
    rows4_ref[...] = (sides[0][:16] + sides[1][:16]).astype(BF16)
    half = rows5_ref.shape[0] // 2
    owner = lax.axis_index("dp") // 2 * (owners // 2) + lax.axis_index("space")
    start = owner * (27 * half // owners) % half
    empty = jnp.zeros((half + 16 - parts_ref.shape[1], parts_ref.shape[2]), F32)
    for i, side in enumerate(sides):
        rows5 = jnp.concatenate([side[16:], empty], axis=0)
        rows5_ref[pl.ds(i * half, half), :] = pltpu.roll(rows5, start, 0).astype(BF16)


def summed(parts):
    return call(sum_kernel, "sums", (((16, 128), BF16), ((128, 128), BF16)), (parts,))


def place_rows(rows4_ref, rows5_ref, weight4_ref, weight5_ref, side, half4_ref, half5_ref, sems):
    first = lax.axis_index("space") % 16 * 4
    share = 27 * 64 // rows4_ref.shape[0]
    row = lax.broadcasted_iota(jnp.int32, (8, 128), 0)
    for o in range(27):
        for k in range(2):
            half4_ref[o, pl.ds(k * 16, 16), :] = rows4_ref[2 * o + k].astype(F32)
    at = pl.multiple_of(side * 32, 32)
    copy4 = pltpu.make_async_copy(half4_ref, weight4_ref.at[:, pl.ds(at, 32), :], sems.at[0])
    copy4.start()
    for o in range(27):
        start = o * 64 + first
        owner = start // share
        low, high = rows5_ref[owner], rows5_ref[(start + 3) // share]
        half5_ref[o] = jnp.where(row < (owner + 1) * share - start, low, high)[:4]
    at = pl.multiple_of(side * 128, 128)
    copy5 = pltpu.make_async_copy(
        half5_ref.at[pl.ds(0, 27)], weight5_ref.at[:, :, pl.ds(at, 128)], sems.at[1]
    )
    copy5.start()
    copy4.wait()
    copy5.wait()


def first_half_kernel(rows4_ref, rows5_ref, weight4_ref, weight5_ref, *scratch):
    place_rows(rows4_ref, rows5_ref, weight4_ref, weight5_ref, lax.axis_index("dp") % 2, *scratch)


def second_half_kernel(rows4_ref, rows5_ref, _, __, weight4_ref, weight5_ref, *scratch):
    place_rows(rows4_ref, rows5_ref, weight4_ref, weight5_ref, 1 - lax.axis_index("dp") % 2, *scratch)


def placed_half(kernel, name, rows, *halves):
    anywhere = pl.BlockSpec(memory_space=pl.ANY)
    near = [rows[:, :16], rows[:, 16:].astype(F32)]
    return pl.pallas_call(
        kernel,
        out_shape=(
            jax.ShapeDtypeStruct((27, 64, 128), F32),
            jax.ShapeDtypeStruct((27, 4, 256), F32),
        ),
        in_specs=[VMEM] * 2 + [anywhere] * len(halves),
        out_specs=(anywhere, anywhere),
        scratch_shapes=[
            pltpu.VMEM((27, 32, 128), F32),
            pltpu.VMEM((32, 4, 128), F32),
            pltpu.SemaphoreType.DMA((2,)),
        ],
        input_output_aliases={i + 2: i for i in range(len(halves))},
        name=name,
    )(*[pltpu.with_memory_space_constraint(x, pltpu.VMEM) for x in near], *halves)


def per_device(volumes, cotangent, conv4_weight, conv5_weight):
    odd = lax.axis_index("space") % 2
    first4 = swapped(lax.dynamic_index_in_dim(volumes, 1 - odd, 0, keepdims=False), 0)
    second4 = swapped(lax.dynamic_index_in_dim(volumes, odd, 0, keepdims=False), 1)
    arranged4 = conv4_weight.transpose(1, 0, 2).reshape(conv4_weight.shape[1], -1)
    part4, stack4 = own4(volumes, arranged4)
    pooled, slope, stack4 = layer4(first4, second4, arranged4, part4, stack4)
    part5, back5 = own5(pooled, conv5_weight)
    output5, to_first, to_second, mine5, share5 = layer5(
        pooled, swapped(pooled, 0), swapped(pooled, 1), conv5_weight, cotangent[0], part5, back5
    )
    first, second = swapped(to_first, 0), swapped(to_second, 1)
    inward = own_inward(mine5, back5)
    outer = conv5_weight.shape[1]
    chip5 = other_chip(share5)
    send5, chips5, output5 = regrouped(mine5, chip5, output5, outer)
    part = weight5_part(mine5, chip5, other_core(send5), chips5, outer)
    keep, send = weight4_parts(inward, first, second, stack4, slope)
    axes = ("dp", "space")
    spaces, groups = lax.axis_size("space"), lax.axis_size("dp")
    per_core = [
        [dp * spaces + s for dp in range(core, groups, 2) for s in range(spaces)]
        for core in range(2)
    ]

    def exchange(parts):
        return lax.all_to_all(
            parts, axes, split_axis=0, concat_axis=0, tiled=True, axis_index_groups=per_core
        )

    rows4, rows5 = summed(exchange(paired(keep, other_core(send), part)))
    rows5 = jnp.pad(rows5.reshape(spaces, 4, 128), ((0, 0), (0, 4), (0, 0)))
    outgoing = jnp.concatenate(
        [
            jnp.broadcast_to(rows4, (64, 16, 128)),
            jnp.broadcast_to(rows5, (2, spaces, 8, 128)).reshape(64, 8, 128),
        ],
        axis=1,
    )
    mine = exchange(outgoing)
    halves = placed_half(first_half_kernel, "first_half", mine)
    weight4, weight5 = placed_half(second_half_kernel, "second_half", other_core(mine), *halves)
    return (output5[None], weight4.transpose(0, 2, 1), weight5.transpose(0, 2, 1))


def solution(mesh):
    placed = (P("space", "dp", None, None), P("space", "dp", None, None), P(), P())
    return jax.shard_map(
        per_device,
        mesh=mesh,
        in_specs=placed,
        out_specs=(P("space", "dp", None, None), P(), P(None, None, "space")),
        check_vma=False,
    )
```

```python
import jax
import jax.numpy as jnp
from jax import lax
from jax.experimental import pallas as pl
from jax.experimental.pallas import tpu as pltpu
from jax.sharding import PartitionSpec as P

HEIGHT = 32
WIDTH = 16
TAPS = tuple((b, e) for b in (-1, 0, 1) for e in (-1, 0, 1))
BF16 = jnp.bfloat16
F32 = jnp.float32
VMEM = pl.BlockSpec(memory_space=pltpu.VMEM)


def call(kernel, name, outputs, operands, scratch=(), room=12, flops=0, aliases=None):
    moved = sum(x.size * x.dtype.itemsize for x in operands)
    return pl.pallas_call(
        kernel,
        out_shape=tuple(pltpu.VMEM(shape, dtype) for shape, dtype in outputs),
        in_specs=[VMEM] * len(operands),
        out_specs=tuple(VMEM for _ in outputs),
        scratch_shapes=list(scratch),
        input_output_aliases=aliases or {},
        compiler_params=pltpu.CompilerParams(vmem_limit_bytes=room * 2**20),
        cost_estimate=pl.CostEstimate(flops=flops, bytes_accessed=moved, transcendentals=0),
        name=name,
    )(*[pltpu.with_memory_space_constraint(x, pltpu.VMEM) for x in operands])


def swap_pairs(groups, count, phase):
    pairs = []
    for group in range(groups):
        for here in range(count):
            there = here + 1 if here % 2 == phase else here - 1
            if 0 <= there < count:
                pairs.append((group * count + here, group * count + there))
            else:
                pairs.append((group * count + here, (group ^ 1) * count + here))
    return pairs


def swapped(values, phase):
    pairs = swap_pairs(lax.axis_size("dp"), lax.axis_size("space"), phase)
    return lax.ppermute(values, ("dp", "space"), pairs)


def other_core(values):
    count = lax.axis_size("dp")
    return lax.ppermute(values, "dp", [(i, i ^ 1) for i in range(count)])


def other_chip(values):
    count = lax.axis_size("dp")
    return lax.ppermute(values, "dp", [(i, i ^ 2) for i in range(count)])


def neighbours(first, second):
    here = lax.axis_index("space")
    odd = here % 2 == 1
    below = jnp.where(odd, first, second)
    above = jnp.where(odd, second, first)
    below = jnp.where(here == 0, jnp.zeros_like(below), below)
    above = jnp.where(here == lax.axis_size("space") - 1, jnp.zeros_like(above), above)
    return below, above


def keep_mask(b, e, row_len, length):
    lane = lax.broadcasted_iota(jnp.int32, (1, length), 1)
    column = lane % row_len + e
    row = lane // row_len + b
    inside = (column >= 0) & (column < row_len) & (row >= 0) & (row < length // row_len)
    return inside.astype(F32).astype(BF16)


def tap(values, b, e, row_len):
    length = values.shape[1]
    offset = b * row_len + e
    if offset == 0:
        return values
    return pltpu.roll(values, -offset % length, 1) * keep_mask(b, e, row_len, length)


def dot(left, right):
    return jnp.dot(left, right, preferred_element_type=F32)


def dot_rows(left, right):
    return lax.dot_general(left, right, (((1,), (1,)), ((), ())), preferred_element_type=F32)


def pool_matrix(fine_axis, shape):
    fine = lax.broadcasted_iota(jnp.int32, shape, fine_axis)
    coarse = lax.broadcasted_iota(jnp.int32, shape, 1 - fine_axis)
    owner = (fine // (2 * WIDTH)) * (WIDTH // 2) + (fine % WIDTH) // 2
    return (owner == coarse).astype(BF16)


def stack_plane(plane, out_ref, j, n):
    chans, cells = plane.shape
    for t, (b, e) in enumerate(TAPS):
        out_ref[pl.ds((j * len(TAPS) + t) * chans, chans), pl.ds(n * cells, cells)] = tap(
            plane, b, e, WIDTH
        )


def own4_kernel(vol_ref, weight_ref, part_ref, stack_ref):
    rows = len(TAPS) * vol_ref.shape[2]
    for n in range(2):
        for d in range(2):
            stack_plane(vol_ref[d, n], stack_ref, 1 + d, n)
    for d in range(2):
        part_ref[d] = dot(
            weight_ref[:, (1 - d) * rows : (3 - d) * rows], stack_ref[pl.ds(rows, 2 * rows), :]
        )


def own4(volumes, weight):
    vols, chans, cells = volumes.shape[1:]
    return call(
        own4_kernel,
        "own4",
        (
            ((2, weight.shape[0], vols * cells), F32),
            ((4 * len(TAPS) * chans, vols * cells), BF16),
        ),
        (volumes, weight),
        flops=2 * weight.size * 2 * vols * cells,
    )


def layer4_kernel(
    first_ref, second_ref, weight_ref, part_ref, _, pooled_ref, preact_ref, stack_ref
):
    chans, cells = first_ref.shape[1:]
    rows = len(TAPS) * chans
    for n in range(2):
        below, above = neighbours(first_ref[n], second_ref[n])
        stack_plane(below, stack_ref, 0, n)
        stack_plane(above, stack_ref, 3, n)
    pool = pool_matrix(0, (cells, cells // 4))
    for n in range(2):
        lanes = pl.ds(n * cells, cells)
        total = None
        for d in range(2):
            preact = part_ref[d, :, lanes] + dot(
                weight_ref[:, 2 * d * rows : (2 * d + 1) * rows],
                stack_ref[pl.ds(3 * d * rows, rows), lanes],
            )
            preact_ref[d, :, lanes] = preact
            active = preact * jax.nn.sigmoid(preact)
            total = active if total is None else total + active
        high = total.astype(BF16)
        low = (total - high.astype(F32)).astype(BF16)
        pooled = (dot(high, pool) + dot(low, pool)) * 0.125
        pooled_ref[:, pl.ds(n * cells // 4, cells // 4)] = pooled.astype(BF16)


def layer4(first, second, weight, part, stack):
    lanes = stack.shape[1]
    return call(
        layer4_kernel,
        "layer4",
        (((weight.shape[0], lanes // 4), BF16), (part.shape, F32), (stack.shape, BF16)),
        (first, second, weight, part, stack),
        flops=2 * weight.size * lanes,
        aliases={3: 1, 4: 2},
    )


def spread_taps(planes, out_ref, row_len, cells, sign):
    chans = planes[0].shape[0]
    for j, plane in enumerate(planes):
        for n in range(plane.shape[1] // cells):
            part = plane[:, n * cells : (n + 1) * cells]
            for t, (b, e) in enumerate(TAPS):
                out_ref[pl.ds((j * len(TAPS) + t) * chans, chans), pl.ds(n * cells, cells)] = tap(
                    part, sign * b, sign * e, row_len
                )


def tapped(plane, row_len, cells, b, e):
    parts = [
        tap(plane[:, at : at + cells], b, e, row_len) for at in range(0, plane.shape[1], cells)
    ]
    return jnp.concatenate(parts, axis=1)


def convolved5(weight_ref, plane, cells, a):
    first = (a + 1) * len(TAPS)
    total = None
    for t in range(0, len(TAPS), 2):
        group = range(t, min(t + 2, len(TAPS)))
        weight = jnp.concatenate([weight_ref[first + i] for i in group], axis=1)
        shifts = jnp.concatenate(
            [tapped(plane, WIDTH // 2, cells, *TAPS[i]) for i in group], axis=0
        )
        part = dot(weight, shifts)
        total = part if total is None else total + part
    return total


def own5_kernel(pooled_ref, weight_ref, preact4_ref, part_ref, back_ref, slope_ref):
    for d in range(2):
        preact = preact4_ref[d]
        sig = jax.nn.sigmoid(preact)
        slope_ref[d] = sig * (1.0 + preact * (1.0 - sig)) * 0.125
    chans = pooled_ref.shape[0]
    cells = pooled_ref.shape[1] // 2
    part_ref[...] = convolved5(weight_ref, pooled_ref[...], cells, 0)
    for o in range(27):
        a, t = divmod(o, len(TAPS))
        back_ref[t, pl.ds((0, 2, 1)[a] * chans, chans), :] = weight_ref[o].T


def own5(pooled, weight, preact4):
    chans, lanes = pooled.shape
    outer = weight.shape[1]
    return call(
        own5_kernel,
        "own5",
        (((outer, lanes), F32), ((len(TAPS), 3 * chans, outer), BF16), (preact4.shape, F32)),
        (pooled, weight, preact4),
        aliases={2: 2},
        flops=2 * weight.size * lanes // 3,
    )


def inward_part(back_ref, grad, cells, first, rows):
    total = None
    for t, (b, e) in enumerate(TAPS):
        shifts = tapped(grad, WIDTH // 2, cells, -b, -e)
        part = dot(back_ref[t, pl.ds(first, rows), :], shifts)
        total = part if total is None else total + part
    return total


def layer5_kernel(
    pooled_ref, first_ref, second_ref, weight_ref, cot_ref, part_ref, back_ref,
    out_ref, to_first_ref, to_second_ref, mine_ref, share_ref,
):
    chans = pooled_ref.shape[0]
    outer = part_ref.shape[0]
    cells = cot_ref.shape[2]
    below, above = neighbours(first_ref[...], second_ref[...])
    preact = part_ref[...] + convolved5(weight_ref, below, cells, -1)
    preact += convolved5(weight_ref, above, cells, 1)
    sig = jax.nn.sigmoid(preact)
    active = preact * sig
    slope = sig * (1.0 + preact * (1.0 - sig))
    grads = []
    for n in range(cot_ref.shape[0]):
        lanes = slice(n * cells, (n + 1) * cells)
        out_ref[n] = active[:, lanes].astype(BF16)
        grads.append((cot_ref[n].astype(F32) * slope[:, lanes]).astype(BF16))
    grad = jnp.concatenate(grads, axis=1)
    mine_ref[pl.ds(0, outer), :] = grad
    share_ref[pl.ds(0, outer), :] = grad
    inward = inward_part(back_ref, grad, cells, 0, 2 * chans)
    down, up = inward[:chans].astype(BF16), inward[chans:].astype(BF16)
    odd = lax.axis_index("space") % 2 == 1
    to_first_ref[...] = jnp.where(odd, down, up)
    to_second_ref[...] = jnp.where(odd, up, down)
    chip = lax.axis_index("dp") // 2
    half = chans // 2
    for j, plane in enumerate((below, pooled_ref[...], above)):
        at = pl.ds(outer + j * half, half)
        mine_ref[at, :] = jnp.where(chip == 0, plane[:half], plane[half:])
        share_ref[at, :] = jnp.where(chip == 0, plane[half:], plane[:half])


def layer5(pooled, first, second, weight, cot, part, back):
    vols, outer, cells = cot.shape
    chans, lanes = pooled.shape
    return call(
        layer5_kernel,
        "layer5",
        (
            ((vols, outer, cells), BF16),
            ((chans, lanes), BF16),
            ((chans, lanes), BF16),
            ((outer + 3 * chans // 2, lanes), BF16),
            ((outer + 3 * chans // 2, lanes), BF16),
        ),
        (pooled, first, second, weight, cot, part, back),
        flops=3 * weight.size * lanes,
    )


def stack_window(ref, first, rows, out_ref, i):
    lanes = ref.shape[1]
    chans = rows // 3
    planes = tuple(ref[pl.ds(first + j * chans, chans), :] for j in range(3))
    spread_taps(planes, out_ref.at[:, pl.ds(i * lanes, lanes)], WIDTH // 2, lanes // 2, 1)


def regroup_kernel(mine_ref, got_ref, made_ref, send_ref, out_ref, sem):
    copy = pltpu.make_async_copy(made_ref, out_ref, sem)
    copy.start()
    core = lax.axis_index("dp") % 2
    rows = send_ref.shape[0] // 2
    half = mine_ref.shape[0] - rows
    for i, ref in enumerate((mine_ref, got_ref)):
        start = pl.multiple_of((1 - core) * half, half)
        send_ref[pl.ds(i * rows, half), :] = ref[pl.ds(start, half), :]
        send_ref[pl.ds(i * rows + half, rows - half), :] = ref[pl.ds(2 * half, rows - half), :]
    copy.wait()


def regrouped(mine, got, made, outer):
    rows = mine.shape[0] - outer // 2
    lanes = mine.shape[1]
    return pl.pallas_call(
        regroup_kernel,
        out_shape=(
            pltpu.VMEM((2 * rows, lanes), BF16),
            jax.ShapeDtypeStruct(made.shape, made.dtype),
        ),
        in_specs=[VMEM] * 3,
        out_specs=(VMEM, pl.BlockSpec(memory_space=pl.ANY)),
        scratch_shapes=[pltpu.SemaphoreType.DMA],
        compiler_params=pltpu.CompilerParams(vmem_limit_bytes=12 * 2**20),
        name="regroup",
    )(*[pltpu.with_memory_space_constraint(x, pltpu.VMEM) for x in (mine, got, made)])


def weight5_sums(sources, stack_ref, total_ref):
    for i, (_, ref, first, rows) in enumerate(sources):
        stack_window(ref, first, rows, stack_ref, i)
    grads = jnp.concatenate([grad for grad, *_ in sources], axis=1)
    block = stack_ref.shape[0] // 3
    for j in range(3):
        at = pl.ds(j * block, block)
        total_ref[at, :] = dot_rows(stack_ref[at, :], grads)


def own_kernel(mine_ref, chip_ref, back_ref, inward_ref, total_ref, stack_ref):
    core = lax.axis_index("dp") % 2
    outer = back_ref.shape[2]
    chans, lanes = inward_ref.shape
    grad = mine_ref[pl.ds(0, outer), :]
    inward_ref[...] = inward_part(back_ref, grad, lanes // 2, 2 * chans, chans)
    own = pl.ds(pl.multiple_of(core * (outer // 2), outer // 2), outer // 2)
    rows = mine_ref.shape[0] - outer
    weight5_sums([(ref[own, :], ref, outer, rows) for ref in (mine_ref, chip_ref)], stack_ref, total_ref)


def own_parts(mine, chip, back):
    lanes = mine.shape[1]
    chans, outer = back.shape[1] // 3, back.shape[2]
    rows = 9 * (mine.shape[0] - outer)
    return call(
        own_kernel,
        "own_parts",
        (((chans, lanes), F32), ((rows, outer // 2), F32)),
        (mine, chip, back),
        scratch=[pltpu.VMEM((rows, 2 * lanes), BF16)],
        flops=2 * back.size * lanes // 3 + 2 * rows * lanes * outer,
    )


def weight5_kernel(core_ref, first_ref, part_ref, stack_ref, total_ref):
    rows, half = core_ref.shape[0] // 2, total_ref.shape[1]
    sources = [
        (core_ref[pl.ds(i * rows, half), :], core_ref, i * rows + half, rows - half)
        for i in range(2)
    ]
    weight5_sums(sources, stack_ref, total_ref)
    filled = first_ref.shape[0]
    total_ref[pl.ds(0, filled), :] += first_ref[...]
    total_ref[pl.ds(filled, 8), :] = jnp.zeros((8, half), F32)
    owners = part_ref.shape[0]
    for owner in range(owners):
        part_ref[owner, pl.ds(16, 32), :] = total_ref[pl.ds(owner * (filled // owners), 32), :].astype(
            BF16
        )


def weight5_part(core, first):
    rows, half = first.shape
    (part,) = call(
        weight5_kernel,
        "weight5",
        (((64, 48, 128), BF16),),
        (core, first),
        scratch=[pltpu.VMEM((rows, 2 * core.shape[1]), BF16), pltpu.VMEM((rows + 8, half), F32)],
        flops=4 * rows * core.shape[1] * half,
    )
    return part


def weight4_kernel(
    inward_ref, first_ref, second_ref, stack_ref, slope_ref, keep_ref, send_ref, acc_ref
):
    core = lax.axis_index("dp") % 2
    below, above = neighbours(first_ref[...], second_ref[...])
    inward = (inward_ref[...] + below.astype(F32) + above.astype(F32)).astype(BF16)
    chans = inward.shape[0]
    cells = inward.shape[1] // 2
    unpool = pool_matrix(1, (cells, 4 * cells))
    fine = jnp.concatenate(
        [dot(inward[:, n * cells : (n + 1) * cells], unpool) for n in range(2)], axis=1
    )
    grads = jnp.concatenate(
        [(fine * slope_ref[0]).astype(BF16), (fine * slope_ref[1]).astype(BF16)], axis=0
    )
    grads = grads.T
    rows = stack_ref.shape[0] // 4
    for j in range(4):
        plane = stack_ref[pl.ds(j * rows, rows), :]
        if j == 0:
            acc_ref[pl.ds(0, rows), :] = dot(plane, grads[:, :chans])
        elif j == 3:
            acc_ref[pl.ds(2 * rows, rows), :] += dot(plane, grads[:, chans:])
        else:
            both = dot(plane, grads)
            acc_ref[pl.ds(j * rows, rows), :] = both[:, :chans]
            acc_ref[pl.ds((j - 1) * rows, rows), :] += both[:, chans:]
    inner = rows // len(TAPS)
    share = inner // 4
    for o in range(27):
        for k in range(2):
            mine = pl.multiple_of(o * inner + core * 2 * share + k * share, share)
            theirs = pl.multiple_of(o * inner + (1 - core) * 2 * share + k * share, share)
            keep_ref[2 * o + k] = acc_ref[pl.ds(mine, share), :]
            send_ref[2 * o + k] = acc_ref[pl.ds(theirs, share), :].astype(BF16)


def weight4_parts(inward, first, second, stack, slope):
    chans = inward.shape[0]
    return call(
        weight4_kernel,
        "weight4_parts",
        (((54, 16, 128), F32), ((54, 16, 128), BF16)),
        (inward, first, second, stack, slope),
        scratch=[pltpu.VMEM((3 * stack.shape[0] // 4, chans), F32)],
        flops=3 * stack.size * chans,
    )


def pair_kernel(keep_ref, got_ref, _, part_ref):
    filled, rows = keep_ref.shape[:2]
    for i in range(filled):
        part_ref[i, pl.ds(0, rows), :] = (keep_ref[i] + got_ref[i].astype(F32)).astype(BF16)
    for i in range(filled, part_ref.shape[0]):
        part_ref[i, pl.ds(0, rows), :] = jnp.zeros((rows, part_ref.shape[2]), BF16)


def paired(keep, got, part):
    (part,) = call(pair_kernel, "pairs", ((part.shape, BF16),), (keep, got, part), aliases={2: 0})
    return part


def sum_kernel(parts_ref, rows4_ref, rows5_ref):
    owners = parts_ref.shape[0]
    sides = []
    for side in range(2):
        total = parts_ref[side * owners // 2].astype(F32)
        for i in range(1, owners // 2):
            total += parts_ref[side * owners // 2 + i].astype(F32)
        sides.append(total)
    rows4_ref[...] = (sides[0][:16] + sides[1][:16]).astype(BF16)
    half = rows5_ref.shape[0] // 2
    owner = lax.axis_index("dp") // 2 * (owners // 2) + lax.axis_index("space")
    start = owner * (27 * half // owners) % half
    empty = jnp.zeros((half + 16 - parts_ref.shape[1], parts_ref.shape[2]), F32)
    for i, side in enumerate(sides):
        rows5 = jnp.concatenate([side[16:], empty], axis=0)
        rows5_ref[pl.ds(i * half, half), :] = pltpu.roll(rows5, start, 0).astype(BF16)


def summed(parts):
    return call(sum_kernel, "sums", (((16, 128), BF16), ((128, 128), BF16)), (parts,))


def place_rows(rows4_ref, rows5_ref, weight4_ref, weight5_ref, side, half4_ref, half5_ref, sems):
    first = lax.axis_index("space") % 16 * 4
    share = 27 * 64 // rows4_ref.shape[0]
    row = lax.broadcasted_iota(jnp.int32, (8, 128), 0)
    for o in range(27):
        for k in range(2):
            half4_ref[o, pl.ds(k * 16, 16), :] = rows4_ref[2 * o + k].astype(F32)
    at = pl.multiple_of(side * 32, 32)
    copy4 = pltpu.make_async_copy(half4_ref, weight4_ref.at[:, pl.ds(at, 32), :], sems.at[0])
    copy4.start()
    for o in range(27):
        start = o * 64 + first
        owner = start // share
        low, high = rows5_ref[owner], rows5_ref[(start + 3) // share]
        half5_ref[o] = jnp.where(row < (owner + 1) * share - start, low, high)[:4]
    at = pl.multiple_of(side * 128, 128)
    copy5 = pltpu.make_async_copy(
        half5_ref.at[pl.ds(0, 27)], weight5_ref.at[:, :, pl.ds(at, 128)], sems.at[1]
    )
    copy5.start()
    copy4.wait()
    copy5.wait()


def first_half_kernel(rows4_ref, rows5_ref, weight4_ref, weight5_ref, *scratch):
    place_rows(rows4_ref, rows5_ref, weight4_ref, weight5_ref, lax.axis_index("dp") % 2, *scratch)


def second_half_kernel(rows4_ref, rows5_ref, _, __, weight4_ref, weight5_ref, *scratch):
    place_rows(rows4_ref, rows5_ref, weight4_ref, weight5_ref, 1 - lax.axis_index("dp") % 2, *scratch)


def placed_half(kernel, name, rows, *halves):
    anywhere = pl.BlockSpec(memory_space=pl.ANY)
    near = [rows[:, :16], rows[:, 16:].astype(F32)]
    return pl.pallas_call(
        kernel,
        out_shape=(
            jax.ShapeDtypeStruct((27, 64, 128), F32),
            jax.ShapeDtypeStruct((27, 4, 256), F32),
        ),
        in_specs=[VMEM] * 2 + [anywhere] * len(halves),
        out_specs=(anywhere, anywhere),
        scratch_shapes=[
            pltpu.VMEM((27, 32, 128), F32),
            pltpu.VMEM((32, 4, 128), F32),
            pltpu.SemaphoreType.DMA((2,)),
        ],
        input_output_aliases={i + 2: i for i in range(len(halves))},
        name=name,
    )(*[pltpu.with_memory_space_constraint(x, pltpu.VMEM) for x in near], *halves)


def per_device(volumes, cotangent, conv4_weight, conv5_weight):
    odd = lax.axis_index("space") % 2
    first4 = swapped(lax.dynamic_index_in_dim(volumes, 1 - odd, 0, keepdims=False), 0)
    second4 = swapped(lax.dynamic_index_in_dim(volumes, odd, 0, keepdims=False), 1)
    arranged4 = conv4_weight.transpose(1, 0, 2).reshape(conv4_weight.shape[1], -1)
    part4, stack4 = own4(volumes, arranged4)
    pooled, preact4, stack4 = layer4(first4, second4, arranged4, part4, stack4)
    part5, back5, slope = own5(pooled, conv5_weight, preact4)
    output5, to_first, to_second, mine5, share5 = layer5(
        pooled, swapped(pooled, 0), swapped(pooled, 1), conv5_weight, cotangent[0], part5, back5
    )
    first, second = swapped(to_first, 0), swapped(to_second, 1)
    chip5 = other_chip(share5)
    send5, output5 = regrouped(mine5, chip5, output5, conv5_weight.shape[1])
    inward, chips5 = own_parts(mine5, chip5, back5)
    part = weight5_part(other_core(send5), chips5)
    keep, send = weight4_parts(inward, first, second, stack4, slope)
    axes = ("dp", "space")
    spaces, groups = lax.axis_size("space"), lax.axis_size("dp")
    per_core = [
        [dp * spaces + s for dp in range(core, groups, 2) for s in range(spaces)]
        for core in range(2)
    ]

    def exchange(parts):
        return lax.all_to_all(
            parts, axes, split_axis=0, concat_axis=0, tiled=True, axis_index_groups=per_core
        )

    rows4, rows5 = summed(exchange(paired(keep, other_core(send), part)))
    rows5 = jnp.pad(rows5.reshape(spaces, 4, 128), ((0, 0), (0, 4), (0, 0)))
    outgoing = jnp.concatenate(
        [
            jnp.broadcast_to(rows4, (64, 16, 128)),
            jnp.broadcast_to(rows5, (2, spaces, 8, 128)).reshape(64, 8, 128),
        ],
        axis=1,
    )
    mine = exchange(outgoing)
    halves = placed_half(first_half_kernel, "first_half", mine)
    weight4, weight5 = placed_half(second_half_kernel, "second_half", other_core(mine), *halves)
    return (output5[None], weight4.transpose(0, 2, 1), weight5.transpose(0, 2, 1))


def solution(mesh):
    placed = (P("space", "dp", None, None), P("space", "dp", None, None), P(), P())
    return jax.shard_map(
        per_device,
        mesh=mesh,
        in_specs=placed,
        out_specs=(P("space", "dp", None, None), P(), P(None, None, "space")),
        check_vma=False,
    )
```

```python
import jax
import jax.numpy as jnp
from jax import lax
from jax.experimental import pallas as pl
from jax.experimental.pallas import tpu as pltpu
from jax.sharding import PartitionSpec as P

HEIGHT = 32
WIDTH = 16
TAPS = tuple((b, e) for b in (-1, 0, 1) for e in (-1, 0, 1))
BF16 = jnp.bfloat16
F32 = jnp.float32
VMEM = pl.BlockSpec(memory_space=pltpu.VMEM)


def call(kernel, name, outputs, operands, scratch=(), room=12, flops=0, aliases=None):
    moved = sum(x.size * x.dtype.itemsize for x in operands)
    return pl.pallas_call(
        kernel,
        out_shape=tuple(pltpu.VMEM(shape, dtype) for shape, dtype in outputs),
        in_specs=[VMEM] * len(operands),
        out_specs=tuple(VMEM for _ in outputs),
        scratch_shapes=list(scratch),
        input_output_aliases=aliases or {},
        compiler_params=pltpu.CompilerParams(vmem_limit_bytes=room * 2**20),
        cost_estimate=pl.CostEstimate(flops=flops, bytes_accessed=moved, transcendentals=0),
        name=name,
    )(*[pltpu.with_memory_space_constraint(x, pltpu.VMEM) for x in operands])


def swap_pairs(groups, count, phase):
    pairs = []
    for group in range(groups):
        for here in range(count):
            there = here + 1 if here % 2 == phase else here - 1
            if 0 <= there < count:
                pairs.append((group * count + here, group * count + there))
            else:
                pairs.append((group * count + here, (group ^ 1) * count + here))
    return pairs


def swapped(values, phase):
    pairs = swap_pairs(lax.axis_size("dp"), lax.axis_size("space"), phase)
    return lax.ppermute(values, ("dp", "space"), pairs)


def other_core(values):
    count = lax.axis_size("dp")
    return lax.ppermute(values, "dp", [(i, i ^ 1) for i in range(count)])


def other_chip(values):
    count = lax.axis_size("dp")
    return lax.ppermute(values, "dp", [(i, i ^ 2) for i in range(count)])


def neighbours(first, second):
    here = lax.axis_index("space")
    odd = here % 2 == 1
    below = jnp.where(odd, first, second)
    above = jnp.where(odd, second, first)
    below = jnp.where(here == 0, jnp.zeros_like(below), below)
    above = jnp.where(here == lax.axis_size("space") - 1, jnp.zeros_like(above), above)
    return below, above


def keep_mask(b, e, row_len, length):
    lane = lax.broadcasted_iota(jnp.int32, (1, length), 1)
    column = lane % row_len + e
    row = lane // row_len + b
    inside = (column >= 0) & (column < row_len) & (row >= 0) & (row < length // row_len)
    return inside.astype(F32).astype(BF16)


def tap(values, b, e, row_len):
    length = values.shape[1]
    offset = b * row_len + e
    if offset == 0:
        return values
    return pltpu.roll(values, -offset % length, 1) * keep_mask(b, e, row_len, length)


def dot(left, right):
    return jnp.dot(left, right, preferred_element_type=F32)


def dot_rows(left, right):
    return lax.dot_general(left, right, (((1,), (1,)), ((), ())), preferred_element_type=F32)


def pool_matrix(fine_axis, shape):
    fine = lax.broadcasted_iota(jnp.int32, shape, fine_axis)
    coarse = lax.broadcasted_iota(jnp.int32, shape, 1 - fine_axis)
    owner = (fine // (2 * WIDTH)) * (WIDTH // 2) + (fine % WIDTH) // 2
    return (owner == coarse).astype(BF16)


def stack_plane(plane, out_ref, j, n):
    chans, cells = plane.shape
    for t, (b, e) in enumerate(TAPS):
        out_ref[pl.ds((j * len(TAPS) + t) * chans, chans), pl.ds(n * cells, cells)] = tap(
            plane, b, e, WIDTH
        )


def own4_kernel(vol_ref, weight_ref, part_ref, stack_ref):
    rows = len(TAPS) * vol_ref.shape[2]
    for n in range(2):
        for d in range(2):
            stack_plane(vol_ref[d, n], stack_ref, 1 + d, n)
    for d in range(2):
        part_ref[d] = dot(
            weight_ref[:, (1 - d) * rows : (3 - d) * rows], stack_ref[pl.ds(rows, 2 * rows), :]
        )


def own4(volumes, weight):
    vols, chans, cells = volumes.shape[1:]
    return call(
        own4_kernel,
        "own4",
        (
            ((2, weight.shape[0], vols * cells), F32),
            ((4 * len(TAPS) * chans, vols * cells), BF16),
        ),
        (volumes, weight),
        flops=2 * weight.size * 2 * vols * cells,
    )


def layer4_kernel(
    first_ref, second_ref, weight_ref, part_ref, _, pooled_ref, preact_ref, stack_ref
):
    chans, cells = first_ref.shape[1:]
    rows = len(TAPS) * chans
    for n in range(2):
        below, above = neighbours(first_ref[n], second_ref[n])
        stack_plane(below, stack_ref, 0, n)
        stack_plane(above, stack_ref, 3, n)
    pool = pool_matrix(0, (cells, cells // 4))
    for n in range(2):
        lanes = pl.ds(n * cells, cells)
        total = None
        for d in range(2):
            preact = part_ref[d, :, lanes] + dot(
                weight_ref[:, 2 * d * rows : (2 * d + 1) * rows],
                stack_ref[pl.ds(3 * d * rows, rows), lanes],
            )
            preact_ref[d, :, lanes] = preact
            active = preact * jax.nn.sigmoid(preact)
            total = active if total is None else total + active
        high = total.astype(BF16)
        low = (total - high.astype(F32)).astype(BF16)
        pooled = (dot(high, pool) + dot(low, pool)) * 0.125
        pooled_ref[:, pl.ds(n * cells // 4, cells // 4)] = pooled.astype(BF16)


def layer4(first, second, weight, part, stack):
    lanes = stack.shape[1]
    return call(
        layer4_kernel,
        "layer4",
        (((weight.shape[0], lanes // 4), BF16), (part.shape, F32), (stack.shape, BF16)),
        (first, second, weight, part, stack),
        flops=2 * weight.size * lanes,
        aliases={3: 1, 4: 2},
    )


def spread_taps(planes, out_ref, row_len, cells, sign):
    chans = planes[0].shape[0]
    for j, plane in enumerate(planes):
        for n in range(plane.shape[1] // cells):
            part = plane[:, n * cells : (n + 1) * cells]
            for t, (b, e) in enumerate(TAPS):
                out_ref[pl.ds((j * len(TAPS) + t) * chans, chans), pl.ds(n * cells, cells)] = tap(
                    part, sign * b, sign * e, row_len
                )


def tapped(plane, row_len, cells, b, e):
    parts = [
        tap(plane[:, at : at + cells], b, e, row_len) for at in range(0, plane.shape[1], cells)
    ]
    return jnp.concatenate(parts, axis=1)


def convolved5(weight_ref, plane, cells, a):
    first = (a + 1) * len(TAPS)
    total = None
    for t in range(0, len(TAPS), 2):
        group = range(t, min(t + 2, len(TAPS)))
        weight = jnp.concatenate([weight_ref[first + i] for i in group], axis=1)
        shifts = jnp.concatenate(
            [tapped(plane, WIDTH // 2, cells, *TAPS[i]) for i in group], axis=0
        )
        part = dot(weight, shifts)
        total = part if total is None else total + part
    return total


def own5_kernel(pooled_ref, weight_ref, preact4_ref, part_ref, back_ref, slope_ref):
    for d in range(2):
        preact = preact4_ref[d]
        sig = jax.nn.sigmoid(preact)
        slope_ref[d] = sig * (1.0 + preact * (1.0 - sig)) * 0.125
    chans = pooled_ref.shape[0]
    cells = pooled_ref.shape[1] // 2
    part_ref[...] = convolved5(weight_ref, pooled_ref[...], cells, 0)
    for o in range(27):
        a, t = divmod(o, len(TAPS))
        back_ref[t, pl.ds((0, 2, 1)[a] * chans, chans), :] = weight_ref[o].T


def own5(pooled, weight, preact4):
    chans, lanes = pooled.shape
    outer = weight.shape[1]
    return call(
        own5_kernel,
        "own5",
        (((outer, lanes), F32), ((len(TAPS), 3 * chans, outer), BF16), (preact4.shape, F32)),
        (pooled, weight, preact4),
        aliases={2: 2},
        flops=2 * weight.size * lanes // 3,
    )


def inward_part(back_ref, grad, cells, first, rows):
    total = None
    for t, (b, e) in enumerate(TAPS):
        shifts = tapped(grad, WIDTH // 2, cells, -b, -e)
        part = dot(back_ref[t, pl.ds(first, rows), :], shifts)
        total = part if total is None else total + part
    return total


def layer5_kernel(
    pooled_ref, first_ref, second_ref, weight_ref, cot_ref, part_ref, back_ref,
    out_ref, to_first_ref, to_second_ref, mine_ref, share_ref,
):
    chans = pooled_ref.shape[0]
    outer = part_ref.shape[0]
    cells = cot_ref.shape[2]
    below, above = neighbours(first_ref[...], second_ref[...])
    preact = part_ref[...] + convolved5(weight_ref, below, cells, -1)
    preact += convolved5(weight_ref, above, cells, 1)
    sig = jax.nn.sigmoid(preact)
    active = preact * sig
    slope = sig * (1.0 + preact * (1.0 - sig))
    grads = []
    for n in range(cot_ref.shape[0]):
        lanes = slice(n * cells, (n + 1) * cells)
        out_ref[n] = active[:, lanes].astype(BF16)
        grads.append((cot_ref[n].astype(F32) * slope[:, lanes]).astype(BF16))
    grad = jnp.concatenate(grads, axis=1)
    mine_ref[pl.ds(0, outer), :] = grad
    share_ref[pl.ds(0, outer), :] = grad
    inward = inward_part(back_ref, grad, cells, 0, 2 * chans)
    down, up = inward[:chans].astype(BF16), inward[chans:].astype(BF16)
    odd = lax.axis_index("space") % 2 == 1
    to_first_ref[...] = jnp.where(odd, down, up)
    to_second_ref[...] = jnp.where(odd, up, down)
    chip = lax.axis_index("dp") // 2
    half = chans // 2
    for j, plane in enumerate((below, pooled_ref[...], above)):
        at = pl.ds(outer + j * half, half)
        mine_ref[at, :] = jnp.where(chip == 0, plane[:half], plane[half:])
        share_ref[at, :] = jnp.where(chip == 0, plane[half:], plane[:half])


def layer5(pooled, first, second, weight, cot, part, back):
    vols, outer, cells = cot.shape
    chans, lanes = pooled.shape
    return call(
        layer5_kernel,
        "layer5",
        (
            ((vols, outer, cells), BF16),
            ((chans, lanes), BF16),
            ((chans, lanes), BF16),
            ((outer + 3 * chans // 2, lanes), BF16),
            ((outer + 3 * chans // 2, lanes), BF16),
        ),
        (pooled, first, second, weight, cot, part, back),
        flops=3 * weight.size * lanes,
    )


def stack_window(ref, first, rows, out_ref, i):
    lanes = ref.shape[1]
    chans = rows // 3
    planes = tuple(ref[pl.ds(first + j * chans, chans), :] for j in range(3))
    spread_taps(planes, out_ref.at[:, pl.ds(i * lanes, lanes)], WIDTH // 2, lanes // 2, 1)


def regroup_kernel(mine_ref, got_ref, send_ref):
    core = lax.axis_index("dp") % 2
    rows = send_ref.shape[0] // 2
    half = mine_ref.shape[0] - rows
    for i, ref in enumerate((mine_ref, got_ref)):
        start = pl.multiple_of((1 - core) * half, half)
        send_ref[pl.ds(i * rows, half), :] = ref[pl.ds(start, half), :]
        send_ref[pl.ds(i * rows + half, rows - half), :] = ref[pl.ds(2 * half, rows - half), :]


def regrouped(mine, got, outer):
    rows = mine.shape[0] - outer // 2
    (send,) = call(regroup_kernel, "regroup", (((2 * rows, mine.shape[1]), BF16),), (mine, got))
    return send


def weight5_sums(sources, stack_ref, total_ref):
    for i, (_, ref, first, rows) in enumerate(sources):
        stack_window(ref, first, rows, stack_ref, i)
    grads = jnp.concatenate([grad for grad, *_ in sources], axis=1)
    block = stack_ref.shape[0] // 3
    for j in range(3):
        at = pl.ds(j * block, block)
        total_ref[at, :] = dot_rows(stack_ref[at, :], grads)


def own_kernel(mine_ref, back_ref, made_ref, inward_ref, total_ref, out_ref, stack_ref, sem):
    copy = pltpu.make_async_copy(made_ref, out_ref, sem)
    copy.start()
    core = lax.axis_index("dp") % 2
    outer = back_ref.shape[2]
    chans, lanes = inward_ref.shape
    grad = mine_ref[pl.ds(0, outer), :]
    inward_ref[...] = inward_part(back_ref, grad, lanes // 2, 2 * chans, chans)
    own = pl.ds(pl.multiple_of(core * (outer // 2), outer // 2), outer // 2)
    rows = mine_ref.shape[0] - outer
    weight5_sums([(mine_ref[own, :], mine_ref, outer, rows)], stack_ref, total_ref)
    copy.wait()


def own_parts(mine, back, made):
    lanes = mine.shape[1]
    chans, outer = back.shape[1] // 3, back.shape[2]
    rows = 9 * (mine.shape[0] - outer)
    return pl.pallas_call(
        own_kernel,
        out_shape=(
            pltpu.VMEM((chans, lanes), F32),
            pltpu.VMEM((rows, outer // 2), F32),
            jax.ShapeDtypeStruct(made.shape, made.dtype),
        ),
        in_specs=[VMEM] * 3,
        out_specs=(VMEM, VMEM, pl.BlockSpec(memory_space=pl.ANY)),
        scratch_shapes=[pltpu.VMEM((rows, lanes), BF16), pltpu.SemaphoreType.DMA],
        compiler_params=pltpu.CompilerParams(vmem_limit_bytes=12 * 2**20),
        cost_estimate=pl.CostEstimate(
            flops=2 * back.size * lanes // 3 + 2 * rows * lanes * outer,
            bytes_accessed=2 * back.size,
            transcendentals=0,
        ),
        name="own_parts",
    )(*[pltpu.with_memory_space_constraint(x, pltpu.VMEM) for x in (mine, back, made)])


def weight5_kernel(chip_ref, core_ref, first_ref, part_ref, stack_ref, total_ref):
    rows, half = core_ref.shape[0] // 2, total_ref.shape[1]
    own = pl.multiple_of(lax.axis_index("dp") % 2 * half, half)
    sources = [(chip_ref[pl.ds(own, half), :], chip_ref, 2 * half, rows - half)] + [
        (core_ref[pl.ds(i * rows, half), :], core_ref, i * rows + half, rows - half)
        for i in range(2)
    ]
    weight5_sums(sources, stack_ref, total_ref)
    filled = first_ref.shape[0]
    total_ref[pl.ds(0, filled), :] += first_ref[...]
    total_ref[pl.ds(filled, 8), :] = jnp.zeros((8, half), F32)
    owners = part_ref.shape[0]
    for owner in range(owners):
        part_ref[owner, pl.ds(16, 32), :] = total_ref[pl.ds(owner * (filled // owners), 32), :].astype(
            BF16
        )


def weight5_part(chip, core, first):
    rows, half = first.shape
    (part,) = call(
        weight5_kernel,
        "weight5",
        (((64, 48, 128), BF16),),
        (chip, core, first),
        scratch=[pltpu.VMEM((rows, 3 * core.shape[1]), BF16), pltpu.VMEM((rows + 8, half), F32)],
        flops=4 * rows * core.shape[1] * half,
    )
    return part


def halo_kernel(inward_ref, first_ref, second_ref, sum_ref):
    below, above = neighbours(first_ref[...], second_ref[...])
    sum_ref[...] = (inward_ref[...] + below.astype(F32) + above.astype(F32)).astype(BF16)


def halo_sum(inward, first, second):
    (total,) = call(
        halo_kernel, "halo_sum", ((first.shape, BF16),), (inward, first, second), flops=8 * 10**9
    )
    return total


def weight4_kernel(inward_ref, stack_ref, slope_ref, keep_ref, send_ref, acc_ref):
    core = lax.axis_index("dp") % 2
    inward = inward_ref[...]
    chans = inward.shape[0]
    cells = inward.shape[1] // 2
    unpool = pool_matrix(1, (cells, 4 * cells))
    fine = jnp.concatenate(
        [dot(inward[:, n * cells : (n + 1) * cells], unpool) for n in range(2)], axis=1
    )
    grads = jnp.concatenate(
        [(fine * slope_ref[0]).astype(BF16), (fine * slope_ref[1]).astype(BF16)], axis=0
    )
    grads = grads.T
    rows = stack_ref.shape[0] // 4
    for j in range(4):
        plane = stack_ref[pl.ds(j * rows, rows), :]
        if j == 0:
            acc_ref[pl.ds(0, rows), :] = dot(plane, grads[:, :chans])
        elif j == 3:
            acc_ref[pl.ds(2 * rows, rows), :] += dot(plane, grads[:, chans:])
        else:
            both = dot(plane, grads)
            acc_ref[pl.ds(j * rows, rows), :] = both[:, :chans]
            acc_ref[pl.ds((j - 1) * rows, rows), :] += both[:, chans:]
    inner = rows // len(TAPS)
    share = inner // 4
    for o in range(27):
        for k in range(2):
            mine = pl.multiple_of(o * inner + core * 2 * share + k * share, share)
            theirs = pl.multiple_of(o * inner + (1 - core) * 2 * share + k * share, share)
            keep_ref[2 * o + k] = acc_ref[pl.ds(mine, share), :]
            send_ref[2 * o + k] = acc_ref[pl.ds(theirs, share), :].astype(BF16)


def weight4_parts(inward, stack, slope):
    chans = inward.shape[0]
    return call(
        weight4_kernel,
        "weight4_parts",
        (((54, 16, 128), F32), ((54, 16, 128), BF16)),
        (inward, stack, slope),
        scratch=[pltpu.VMEM((3 * stack.shape[0] // 4, chans), F32)],
        flops=3 * stack.size * chans,
    )


def pair_kernel(keep_ref, got_ref, _, part_ref):
    filled, rows = keep_ref.shape[:2]
    for i in range(filled):
        part_ref[i, pl.ds(0, rows), :] = (keep_ref[i] + got_ref[i].astype(F32)).astype(BF16)
    for i in range(filled, part_ref.shape[0]):
        part_ref[i, pl.ds(0, rows), :] = jnp.zeros((rows, part_ref.shape[2]), BF16)


def paired(keep, got, part):
    (part,) = call(pair_kernel, "pairs", ((part.shape, BF16),), (keep, got, part), aliases={2: 0})
    return part


def sum_kernel(parts_ref, rows4_ref, rows5_ref):
    owners = parts_ref.shape[0]
    sides = []
    for side in range(2):
        total = parts_ref[side * owners // 2].astype(F32)
        for i in range(1, owners // 2):
            total += parts_ref[side * owners // 2 + i].astype(F32)
        sides.append(total)
    rows4_ref[...] = (sides[0][:16] + sides[1][:16]).astype(BF16)
    half = rows5_ref.shape[0] // 2
    owner = lax.axis_index("dp") // 2 * (owners // 2) + lax.axis_index("space")
    start = owner * (27 * half // owners) % half
    empty = jnp.zeros((half + 16 - parts_ref.shape[1], parts_ref.shape[2]), F32)
    for i, side in enumerate(sides):
        rows5 = jnp.concatenate([side[16:], empty], axis=0)
        rows5_ref[pl.ds(i * half, half), :] = pltpu.roll(rows5, start, 0).astype(BF16)


def summed(parts):
    return call(sum_kernel, "sums", (((16, 128), BF16), ((128, 128), BF16)), (parts,))


def place_rows(rows4_ref, rows5_ref, weight4_ref, weight5_ref, side, half4_ref, half5_ref, sems):
    first = lax.axis_index("space") % 16 * 4
    share = 27 * 64 // rows4_ref.shape[0]
    row = lax.broadcasted_iota(jnp.int32, (8, 128), 0)
    for o in range(27):
        for k in range(2):
            half4_ref[o, pl.ds(k * 16, 16), :] = rows4_ref[2 * o + k].astype(F32)
    at = pl.multiple_of(side * 32, 32)
    copy4 = pltpu.make_async_copy(half4_ref, weight4_ref.at[:, pl.ds(at, 32), :], sems.at[0])
    copy4.start()
    for o in range(27):
        start = o * 64 + first
        owner = start // share
        low, high = rows5_ref[owner], rows5_ref[(start + 3) // share]
        half5_ref[o] = jnp.where(row < (owner + 1) * share - start, low, high)[:4]
    at = pl.multiple_of(side * 128, 128)
    copy5 = pltpu.make_async_copy(
        half5_ref.at[pl.ds(0, 27)], weight5_ref.at[:, :, pl.ds(at, 128)], sems.at[1]
    )
    copy5.start()
    copy4.wait()
    copy5.wait()


def first_half_kernel(rows4_ref, rows5_ref, weight4_ref, weight5_ref, *scratch):
    place_rows(rows4_ref, rows5_ref, weight4_ref, weight5_ref, lax.axis_index("dp") % 2, *scratch)


def second_half_kernel(rows4_ref, rows5_ref, _, __, weight4_ref, weight5_ref, *scratch):
    place_rows(rows4_ref, rows5_ref, weight4_ref, weight5_ref, 1 - lax.axis_index("dp") % 2, *scratch)


def placed_half(kernel, name, rows, *halves):
    anywhere = pl.BlockSpec(memory_space=pl.ANY)
    near = [rows[:, :16], rows[:, 16:].astype(F32)]
    return pl.pallas_call(
        kernel,
        out_shape=(
            jax.ShapeDtypeStruct((27, 64, 128), F32),
            jax.ShapeDtypeStruct((27, 4, 256), F32),
        ),
        in_specs=[VMEM] * 2 + [anywhere] * len(halves),
        out_specs=(anywhere, anywhere),
        scratch_shapes=[
            pltpu.VMEM((27, 32, 128), F32),
            pltpu.VMEM((32, 4, 128), F32),
            pltpu.SemaphoreType.DMA((2,)),
        ],
        input_output_aliases={i + 2: i for i in range(len(halves))},
        name=name,
    )(*[pltpu.with_memory_space_constraint(x, pltpu.VMEM) for x in near], *halves)


def per_device(volumes, cotangent, conv4_weight, conv5_weight):
    odd = lax.axis_index("space") % 2
    first4 = swapped(lax.dynamic_index_in_dim(volumes, 1 - odd, 0, keepdims=False), 0)
    second4 = swapped(lax.dynamic_index_in_dim(volumes, odd, 0, keepdims=False), 1)
    arranged4 = conv4_weight.transpose(1, 0, 2).reshape(conv4_weight.shape[1], -1)
    part4, stack4 = own4(volumes, arranged4)
    pooled, preact4, stack4 = layer4(first4, second4, arranged4, part4, stack4)
    part5, back5, slope = own5(pooled, conv5_weight, preact4)
    output5, to_first, to_second, mine5, share5 = layer5(
        pooled, swapped(pooled, 0), swapped(pooled, 1), conv5_weight, cotangent[0], part5, back5
    )
    first, second = swapped(to_first, 0), swapped(to_second, 1)
    chip5 = other_chip(share5)
    inward, chips5, output5 = own_parts(mine5, back5, output5)
    inward, after = lax.optimization_barrier((halo_sum(inward, first, second), chip5))
    send5 = regrouped(mine5, after, conv5_weight.shape[1])
    part = weight5_part(chip5, other_core(send5), chips5)
    keep, send = weight4_parts(inward, stack4, slope)
    axes = ("dp", "space")
    spaces, groups = lax.axis_size("space"), lax.axis_size("dp")
    per_core = [
        [dp * spaces + s for dp in range(core, groups, 2) for s in range(spaces)]
        for core in range(2)
    ]

    def exchange(parts):
        return lax.all_to_all(
            parts, axes, split_axis=0, concat_axis=0, tiled=True, axis_index_groups=per_core
        )

    rows4, rows5 = summed(exchange(paired(keep, other_core(send), part)))
    rows5 = jnp.pad(rows5.reshape(spaces, 4, 128), ((0, 0), (0, 4), (0, 0)))
    outgoing = jnp.concatenate(
        [
            jnp.broadcast_to(rows4, (64, 16, 128)),
            jnp.broadcast_to(rows5, (2, spaces, 8, 128)).reshape(64, 8, 128),
        ],
        axis=1,
    )
    mine = exchange(outgoing)
    halves = placed_half(first_half_kernel, "first_half", mine)
    weight4, weight5 = placed_half(second_half_kernel, "second_half", other_core(mine), *halves)
    return (output5[None], weight4.transpose(0, 2, 1), weight5.transpose(0, 2, 1))


def solution(mesh):
    placed = (P("space", "dp", None, None), P("space", "dp", None, None), P(), P())
    return jax.shard_map(
        per_device,
        mesh=mesh,
        in_specs=placed,
        out_specs=(P("space", "dp", None, None), P(), P(None, None, "space")),
        check_vma=False,
    )
```

```python
import jax
import jax.numpy as jnp
from jax import lax
from jax.experimental import pallas as pl
from jax.experimental.pallas import tpu as pltpu
from jax.sharding import PartitionSpec as P

HEIGHT = 32
WIDTH = 16
TAPS = tuple((b, e) for b in (-1, 0, 1) for e in (-1, 0, 1))
BF16 = jnp.bfloat16
F32 = jnp.float32
VMEM = pl.BlockSpec(memory_space=pltpu.VMEM)


def call(kernel, name, outputs, operands, scratch=(), room=12, flops=0, aliases=None):
    moved = sum(x.size * x.dtype.itemsize for x in operands)
    return pl.pallas_call(
        kernel,
        out_shape=tuple(pltpu.VMEM(shape, dtype) for shape, dtype in outputs),
        in_specs=[VMEM] * len(operands),
        out_specs=tuple(VMEM for _ in outputs),
        scratch_shapes=list(scratch),
        input_output_aliases=aliases or {},
        compiler_params=pltpu.CompilerParams(vmem_limit_bytes=room * 2**20),
        cost_estimate=pl.CostEstimate(flops=flops, bytes_accessed=moved, transcendentals=0),
        name=name,
    )(*[pltpu.with_memory_space_constraint(x, pltpu.VMEM) for x in operands])


def swap_pairs(groups, count, phase):
    pairs = []
    for group in range(groups):
        for here in range(count):
            there = here + 1 if here % 2 == phase else here - 1
            if 0 <= there < count:
                pairs.append((group * count + here, group * count + there))
            else:
                pairs.append((group * count + here, (group ^ 1) * count + here))
    return pairs


def swapped(values, phase):
    pairs = swap_pairs(lax.axis_size("dp"), lax.axis_size("space"), phase)
    return lax.ppermute(values, ("dp", "space"), pairs)


def other_core(values):
    count = lax.axis_size("dp")
    return lax.ppermute(values, "dp", [(i, i ^ 1) for i in range(count)])


def other_chip(values):
    count = lax.axis_size("dp")
    return lax.ppermute(values, "dp", [(i, i ^ 2) for i in range(count)])


def neighbours(first, second):
    here = lax.axis_index("space")
    odd = here % 2 == 1
    below = jnp.where(odd, first, second)
    above = jnp.where(odd, second, first)
    below = jnp.where(here == 0, jnp.zeros_like(below), below)
    above = jnp.where(here == lax.axis_size("space") - 1, jnp.zeros_like(above), above)
    return below, above


def keep_mask(b, e, row_len, length):
    lane = lax.broadcasted_iota(jnp.int32, (1, length), 1)
    column = lane % row_len + e
    row = lane // row_len + b
    inside = (column >= 0) & (column < row_len) & (row >= 0) & (row < length // row_len)
    return inside.astype(F32).astype(BF16)


def tap(values, b, e, row_len):
    length = values.shape[1]
    offset = b * row_len + e
    if offset == 0:
        return values
    return pltpu.roll(values, -offset % length, 1) * keep_mask(b, e, row_len, length)


def dot(left, right):
    return jnp.dot(left, right, preferred_element_type=F32)


def dot_rows(left, right):
    return lax.dot_general(left, right, (((1,), (1,)), ((), ())), preferred_element_type=F32)


def pool_matrix(fine_axis, shape):
    fine = lax.broadcasted_iota(jnp.int32, shape, fine_axis)
    coarse = lax.broadcasted_iota(jnp.int32, shape, 1 - fine_axis)
    owner = (fine // (2 * WIDTH)) * (WIDTH // 2) + (fine % WIDTH) // 2
    return (owner == coarse).astype(BF16)


def stack_plane(plane, out_ref, j, n):
    chans, cells = plane.shape
    for t, (b, e) in enumerate(TAPS):
        out_ref[pl.ds((j * len(TAPS) + t) * chans, chans), pl.ds(n * cells, cells)] = tap(
            plane, b, e, WIDTH
        )


def own4_kernel(vol_ref, weight_ref, part_ref, stack_ref):
    rows = len(TAPS) * vol_ref.shape[2]
    for n in range(2):
        for d in range(2):
            stack_plane(vol_ref[d, n], stack_ref, 1 + d, n)
    for d in range(2):
        part_ref[d] = dot(
            weight_ref[:, (1 - d) * rows : (3 - d) * rows], stack_ref[pl.ds(rows, 2 * rows), :]
        )


def own4(volumes, weight):
    vols, chans, cells = volumes.shape[1:]
    return call(
        own4_kernel,
        "own4",
        (
            ((2, weight.shape[0], vols * cells), F32),
            ((4 * len(TAPS) * chans, vols * cells), BF16),
        ),
        (volumes, weight),
        flops=2 * weight.size * 2 * vols * cells,
    )


def layer4_kernel(
    first_ref, second_ref, weight_ref, part_ref, _, pooled_ref, preact_ref, stack_ref
):
    chans, cells = first_ref.shape[1:]
    rows = len(TAPS) * chans
    for n in range(2):
        below, above = neighbours(first_ref[n], second_ref[n])
        stack_plane(below, stack_ref, 0, n)
        stack_plane(above, stack_ref, 3, n)
    pool = pool_matrix(0, (cells, cells // 4))
    for n in range(2):
        lanes = pl.ds(n * cells, cells)
        total = None
        for d in range(2):
            preact = part_ref[d, :, lanes] + dot(
                weight_ref[:, 2 * d * rows : (2 * d + 1) * rows],
                stack_ref[pl.ds(3 * d * rows, rows), lanes],
            )
            preact_ref[d, :, lanes] = preact
            active = preact * jax.nn.sigmoid(preact)
            total = active if total is None else total + active
        high = total.astype(BF16)
        low = (total - high.astype(F32)).astype(BF16)
        pooled = (dot(high, pool) + dot(low, pool)) * 0.125
        pooled_ref[:, pl.ds(n * cells // 4, cells // 4)] = pooled.astype(BF16)


def layer4(first, second, weight, part, stack):
    lanes = stack.shape[1]
    return call(
        layer4_kernel,
        "layer4",
        (((weight.shape[0], lanes // 4), BF16), (part.shape, F32), (stack.shape, BF16)),
        (first, second, weight, part, stack),
        flops=2 * weight.size * lanes,
        aliases={3: 1, 4: 2},
    )


def spread_taps(planes, out_ref, row_len, cells, sign):
    chans = planes[0].shape[0]
    for j, plane in enumerate(planes):
        for n in range(plane.shape[1] // cells):
            part = plane[:, n * cells : (n + 1) * cells]
            for t, (b, e) in enumerate(TAPS):
                out_ref[pl.ds((j * len(TAPS) + t) * chans, chans), pl.ds(n * cells, cells)] = tap(
                    part, sign * b, sign * e, row_len
                )


def tapped(plane, row_len, cells, b, e):
    parts = [
        tap(plane[:, at : at + cells], b, e, row_len) for at in range(0, plane.shape[1], cells)
    ]
    return jnp.concatenate(parts, axis=1)


def convolved5(weight_ref, plane, cells, a):
    first = (a + 1) * len(TAPS)
    total = None
    for t in range(0, len(TAPS), 2):
        group = range(t, min(t + 2, len(TAPS)))
        weight = jnp.concatenate([weight_ref[first + i] for i in group], axis=1)
        shifts = jnp.concatenate(
            [tapped(plane, WIDTH // 2, cells, *TAPS[i]) for i in group], axis=0
        )
        part = dot(weight, shifts)
        total = part if total is None else total + part
    return total


def own5_kernel(pooled_ref, weight_ref, preact4_ref, part_ref, back_ref, slope_ref):
    for d in range(2):
        preact = preact4_ref[d]
        sig = jax.nn.sigmoid(preact)
        slope_ref[d] = sig * (1.0 + preact * (1.0 - sig)) * 0.125
    chans = pooled_ref.shape[0]
    cells = pooled_ref.shape[1] // 2
    part_ref[...] = convolved5(weight_ref, pooled_ref[...], cells, 0)
    for o in range(27):
        a, t = divmod(o, len(TAPS))
        back_ref[t, pl.ds((0, 2, 1)[a] * chans, chans), :] = weight_ref[o].T


def own5(pooled, weight, preact4):
    chans, lanes = pooled.shape
    outer = weight.shape[1]
    return call(
        own5_kernel,
        "own5",
        (((outer, lanes), F32), ((len(TAPS), 3 * chans, outer), BF16), (preact4.shape, F32)),
        (pooled, weight, preact4),
        aliases={2: 2},
        flops=2 * weight.size * lanes // 3,
    )


def inward_part(back_ref, grad, cells, first, rows):
    total = None
    for t, (b, e) in enumerate(TAPS):
        shifts = tapped(grad, WIDTH // 2, cells, -b, -e)
        part = dot(back_ref[t, pl.ds(first, rows), :], shifts)
        total = part if total is None else total + part
    return total


def layer5_kernel(
    pooled_ref, first_ref, second_ref, weight_ref, cot_ref, part_ref, back_ref,
    out_ref, to_first_ref, to_second_ref, mine_ref, share_ref,
):
    chans = pooled_ref.shape[0]
    outer = part_ref.shape[0]
    cells = cot_ref.shape[2]
    below, above = neighbours(first_ref[...], second_ref[...])
    preact = part_ref[...] + convolved5(weight_ref, below, cells, -1)
    preact += convolved5(weight_ref, above, cells, 1)
    sig = jax.nn.sigmoid(preact)
    active = preact * sig
    slope = sig * (1.0 + preact * (1.0 - sig))
    grads = []
    for n in range(cot_ref.shape[0]):
        lanes = slice(n * cells, (n + 1) * cells)
        out_ref[n] = active[:, lanes].astype(BF16)
        grads.append((cot_ref[n].astype(F32) * slope[:, lanes]).astype(BF16))
    grad = jnp.concatenate(grads, axis=1)
    mine_ref[pl.ds(0, outer), :] = grad
    share_ref[pl.ds(0, outer), :] = grad
    inward = inward_part(back_ref, grad, cells, 0, 2 * chans)
    down, up = inward[:chans].astype(BF16), inward[chans:].astype(BF16)
    odd = lax.axis_index("space") % 2 == 1
    to_first_ref[...] = jnp.where(odd, down, up)
    to_second_ref[...] = jnp.where(odd, up, down)
    chip = lax.axis_index("dp") // 2
    half = chans // 2
    for j, plane in enumerate((below, pooled_ref[...], above)):
        at = pl.ds(outer + j * half, half)
        mine_ref[at, :] = jnp.where(chip == 0, plane[:half], plane[half:])
        share_ref[at, :] = jnp.where(chip == 0, plane[half:], plane[:half])


def layer5(pooled, first, second, weight, cot, part, back):
    vols, outer, cells = cot.shape
    chans, lanes = pooled.shape
    return call(
        layer5_kernel,
        "layer5",
        (
            ((vols, outer, cells), BF16),
            ((chans, lanes), BF16),
            ((chans, lanes), BF16),
            ((outer + 3 * chans // 2, lanes), BF16),
            ((outer + 3 * chans // 2, lanes), BF16),
        ),
        (pooled, first, second, weight, cot, part, back),
        flops=3 * weight.size * lanes,
    )


def stack_window(ref, first, rows, out_ref, i):
    lanes = ref.shape[1]
    chans = rows // 3
    planes = tuple(ref[pl.ds(first + j * chans, chans), :] for j in range(3))
    spread_taps(planes, out_ref.at[:, pl.ds(i * lanes, lanes)], WIDTH // 2, lanes // 2, 1)


def regroup_kernel(mine_ref, got_ref, send_ref):
    core = lax.axis_index("dp") % 2
    rows = send_ref.shape[0] // 2
    half = mine_ref.shape[0] - rows
    for i, ref in enumerate((mine_ref, got_ref)):
        start = pl.multiple_of((1 - core) * half, half)
        send_ref[pl.ds(i * rows, half), :] = ref[pl.ds(start, half), :]
        send_ref[pl.ds(i * rows + half, rows - half), :] = ref[pl.ds(2 * half, rows - half), :]


def regrouped(mine, got, outer):
    rows = mine.shape[0] - outer // 2
    (send,) = call(regroup_kernel, "regroup", (((2 * rows, mine.shape[1]), BF16),), (mine, got))
    return send


def weight5_sums(sources, stack_ref, total_ref):
    for i, (_, ref, first, rows) in enumerate(sources):
        stack_window(ref, first, rows, stack_ref, i)
    grads = jnp.concatenate([grad for grad, *_ in sources], axis=1)
    total_ref[pl.ds(0, stack_ref.shape[0]), :] = dot_rows(stack_ref[...], grads)


def own_kernel(mine_ref, back_ref, made_ref, inward_ref, total_ref, out_ref, stack_ref, sem):
    copy = pltpu.make_async_copy(made_ref, out_ref, sem)
    copy.start()
    core = lax.axis_index("dp") % 2
    outer = back_ref.shape[2]
    chans, lanes = inward_ref.shape
    grad = mine_ref[pl.ds(0, outer), :]
    inward_ref[...] = inward_part(back_ref, grad, lanes // 2, 2 * chans, chans)
    own = pl.ds(pl.multiple_of(core * (outer // 2), outer // 2), outer // 2)
    rows = mine_ref.shape[0] - outer
    weight5_sums([(mine_ref[own, :], mine_ref, outer, rows)], stack_ref, total_ref)
    copy.wait()


def own_parts(mine, back, made):
    lanes = mine.shape[1]
    chans, outer = back.shape[1] // 3, back.shape[2]
    rows = 9 * (mine.shape[0] - outer)
    return pl.pallas_call(
        own_kernel,
        out_shape=(
            pltpu.VMEM((chans, lanes), F32),
            pltpu.VMEM((rows, outer // 2), F32),
            jax.ShapeDtypeStruct(made.shape, made.dtype),
        ),
        in_specs=[VMEM] * 3,
        out_specs=(VMEM, VMEM, pl.BlockSpec(memory_space=pl.ANY)),
        scratch_shapes=[pltpu.VMEM((rows, lanes), BF16), pltpu.SemaphoreType.DMA],
        compiler_params=pltpu.CompilerParams(vmem_limit_bytes=12 * 2**20),
        cost_estimate=pl.CostEstimate(
            flops=2 * back.size * lanes // 3 + 2 * rows * lanes * outer,
            bytes_accessed=2 * back.size,
            transcendentals=0,
        ),
        name="own_parts",
    )(*[pltpu.with_memory_space_constraint(x, pltpu.VMEM) for x in (mine, back, made)])


def weight5_kernel(chip_ref, core_ref, first_ref, part_ref, stack_ref, total_ref):
    rows, half = core_ref.shape[0] // 2, total_ref.shape[1]
    own = pl.multiple_of(lax.axis_index("dp") % 2 * half, half)
    sources = [(chip_ref[pl.ds(own, half), :], chip_ref, 2 * half, rows - half)] + [
        (core_ref[pl.ds(i * rows, half), :], core_ref, i * rows + half, rows - half)
        for i in range(2)
    ]
    weight5_sums(sources, stack_ref, total_ref)
    filled = first_ref.shape[0]
    total_ref[pl.ds(0, filled), :] += first_ref[...]
    total_ref[pl.ds(filled, 8), :] = jnp.zeros((8, half), F32)
    owners = part_ref.shape[0]
    for owner in range(owners):
        part_ref[owner, pl.ds(16, 32), :] = total_ref[pl.ds(owner * (filled // owners), 32), :].astype(
            BF16
        )


def weight5_part(chip, core, first):
    rows, half = first.shape
    (part,) = call(
        weight5_kernel,
        "weight5",
        (((64, 48, 128), BF16),),
        (chip, core, first),
        scratch=[pltpu.VMEM((rows, 3 * core.shape[1]), BF16), pltpu.VMEM((rows + 8, half), F32)],
        flops=4 * rows * core.shape[1] * half,
    )
    return part


def halo_kernel(inward_ref, first_ref, second_ref, sum_ref):
    below, above = neighbours(first_ref[...], second_ref[...])
    sum_ref[...] = (inward_ref[...] + below.astype(F32) + above.astype(F32)).astype(BF16)


def halo_sum(inward, first, second):
    (total,) = call(
        halo_kernel, "halo_sum", ((first.shape, BF16),), (inward, first, second), flops=8 * 10**9
    )
    return total


def weight4_kernel(inward_ref, stack_ref, slope_ref, keep_ref, send_ref, acc_ref):
    core = lax.axis_index("dp") % 2
    inward = inward_ref[...]
    chans = inward.shape[0]
    cells = inward.shape[1] // 2
    unpool = pool_matrix(1, (cells, 4 * cells))
    fine = jnp.concatenate(
        [dot(inward[:, n * cells : (n + 1) * cells], unpool) for n in range(2)], axis=1
    )
    grads = jnp.concatenate(
        [(fine * slope_ref[0]).astype(BF16), (fine * slope_ref[1]).astype(BF16)], axis=0
    )
    grads = grads.T
    rows = stack_ref.shape[0] // 4
    for j in range(4):
        plane = stack_ref[pl.ds(j * rows, rows), :]
        if j == 0:
            acc_ref[pl.ds(0, rows), :] = dot(plane, grads[:, :chans])
        elif j == 3:
            acc_ref[pl.ds(2 * rows, rows), :] += dot(plane, grads[:, chans:])
        else:
            both = dot(plane, grads)
            acc_ref[pl.ds(j * rows, rows), :] = both[:, :chans]
            acc_ref[pl.ds((j - 1) * rows, rows), :] += both[:, chans:]
    inner = rows // len(TAPS)
    share = inner // 4
    for o in range(27):
        for k in range(2):
            mine = pl.multiple_of(o * inner + core * 2 * share + k * share, share)
            theirs = pl.multiple_of(o * inner + (1 - core) * 2 * share + k * share, share)
            keep_ref[2 * o + k] = acc_ref[pl.ds(mine, share), :]
            send_ref[2 * o + k] = acc_ref[pl.ds(theirs, share), :].astype(BF16)


def weight4_parts(inward, stack, slope):
    chans = inward.shape[0]
    return call(
        weight4_kernel,
        "weight4_parts",
        (((54, 16, 128), F32), ((54, 16, 128), BF16)),
        (inward, stack, slope),
        scratch=[pltpu.VMEM((3 * stack.shape[0] // 4, chans), F32)],
        flops=3 * stack.size * chans,
    )


def pair_kernel(keep_ref, got_ref, _, part_ref):
    filled, rows = keep_ref.shape[:2]
    for i in range(filled):
        part_ref[i, pl.ds(0, rows), :] = (keep_ref[i] + got_ref[i].astype(F32)).astype(BF16)
    for i in range(filled, part_ref.shape[0]):
        part_ref[i, pl.ds(0, rows), :] = jnp.zeros((rows, part_ref.shape[2]), BF16)


def paired(keep, got, part):
    (part,) = call(pair_kernel, "pairs", ((part.shape, BF16),), (keep, got, part), aliases={2: 0})
    return part


def sum_kernel(parts_ref, rows4_ref, rows5_ref):
    owners = parts_ref.shape[0]
    sides = []
    for side in range(2):
        total = parts_ref[side * owners // 2].astype(F32)
        for i in range(1, owners // 2):
            total += parts_ref[side * owners // 2 + i].astype(F32)
        sides.append(total)
    rows4_ref[...] = (sides[0][:16] + sides[1][:16]).astype(BF16)
    half = rows5_ref.shape[0] // 2
    owner = lax.axis_index("dp") // 2 * (owners // 2) + lax.axis_index("space")
    start = owner * (27 * half // owners) % half
    empty = jnp.zeros((half + 16 - parts_ref.shape[1], parts_ref.shape[2]), F32)
    for i, side in enumerate(sides):
        rows5 = jnp.concatenate([side[16:], empty], axis=0)
        rows5_ref[pl.ds(i * half, half), :] = pltpu.roll(rows5, start, 0).astype(BF16)


def summed(parts):
    return call(sum_kernel, "sums", (((16, 128), BF16), ((128, 128), BF16)), (parts,))


def place_rows(rows4_ref, rows5_ref, weight4_ref, weight5_ref, side, half4_ref, half5_ref, sems):
    first = lax.axis_index("space") % 16 * 4
    share = 27 * 64 // rows4_ref.shape[0]
    row = lax.broadcasted_iota(jnp.int32, (8, 128), 0)
    for o in range(27):
        for k in range(2):
            half4_ref[o, pl.ds(k * 16, 16), :] = rows4_ref[2 * o + k].astype(F32)
    at = pl.multiple_of(side * 32, 32)
    copy4 = pltpu.make_async_copy(half4_ref, weight4_ref.at[:, pl.ds(at, 32), :], sems.at[0])
    copy4.start()
    for o in range(27):
        start = o * 64 + first
        owner = start // share
        low, high = rows5_ref[owner], rows5_ref[(start + 3) // share]
        half5_ref[o] = jnp.where(row < (owner + 1) * share - start, low, high)[:4]
    at = pl.multiple_of(side * 128, 128)
    copy5 = pltpu.make_async_copy(
        half5_ref.at[pl.ds(0, 27)], weight5_ref.at[:, :, pl.ds(at, 128)], sems.at[1]
    )
    copy5.start()
    copy4.wait()
    copy5.wait()


def first_half_kernel(rows4_ref, rows5_ref, weight4_ref, weight5_ref, *scratch):
    place_rows(rows4_ref, rows5_ref, weight4_ref, weight5_ref, lax.axis_index("dp") % 2, *scratch)


def second_half_kernel(rows4_ref, rows5_ref, _, __, weight4_ref, weight5_ref, *scratch):
    place_rows(rows4_ref, rows5_ref, weight4_ref, weight5_ref, 1 - lax.axis_index("dp") % 2, *scratch)


def placed_half(kernel, name, rows, *halves):
    anywhere = pl.BlockSpec(memory_space=pl.ANY)
    near = [rows[:, :16], rows[:, 16:].astype(F32)]
    return pl.pallas_call(
        kernel,
        out_shape=(
            jax.ShapeDtypeStruct((27, 64, 128), F32),
            jax.ShapeDtypeStruct((27, 4, 256), F32),
        ),
        in_specs=[VMEM] * 2 + [anywhere] * len(halves),
        out_specs=(anywhere, anywhere),
        scratch_shapes=[
            pltpu.VMEM((27, 32, 128), F32),
            pltpu.VMEM((32, 4, 128), F32),
            pltpu.SemaphoreType.DMA((2,)),
        ],
        input_output_aliases={i + 2: i for i in range(len(halves))},
        name=name,
    )(*[pltpu.with_memory_space_constraint(x, pltpu.VMEM) for x in near], *halves)


def per_device(volumes, cotangent, conv4_weight, conv5_weight):
    odd = lax.axis_index("space") % 2
    first4 = swapped(lax.dynamic_index_in_dim(volumes, 1 - odd, 0, keepdims=False), 0)
    second4 = swapped(lax.dynamic_index_in_dim(volumes, odd, 0, keepdims=False), 1)
    arranged4 = conv4_weight.transpose(1, 0, 2).reshape(conv4_weight.shape[1], -1)
    part4, stack4 = own4(volumes, arranged4)
    pooled, preact4, stack4 = layer4(first4, second4, arranged4, part4, stack4)
    part5, back5, slope = own5(pooled, conv5_weight, preact4)
    output5, to_first, to_second, mine5, share5 = layer5(
        pooled, swapped(pooled, 0), swapped(pooled, 1), conv5_weight, cotangent[0], part5, back5
    )
    first, second = swapped(to_first, 0), swapped(to_second, 1)
    chip5 = other_chip(share5)
    inward, chips5, output5 = own_parts(mine5, back5, output5)
    inward, after = lax.optimization_barrier((halo_sum(inward, first, second), chip5))
    send5 = regrouped(mine5, after, conv5_weight.shape[1])
    part = weight5_part(chip5, other_core(send5), chips5)
    keep, send = weight4_parts(inward, stack4, slope)
    axes = ("dp", "space")
    spaces, groups = lax.axis_size("space"), lax.axis_size("dp")
    per_core = [
        [dp * spaces + s for dp in range(core, groups, 2) for s in range(spaces)]
        for core in range(2)
    ]

    def exchange(parts):
        return lax.all_to_all(
            parts, axes, split_axis=0, concat_axis=0, tiled=True, axis_index_groups=per_core
        )

    rows4, rows5 = summed(exchange(paired(keep, other_core(send), part)))
    rows5 = jnp.pad(rows5.reshape(spaces, 4, 128), ((0, 0), (0, 4), (0, 0)))
    outgoing = jnp.concatenate(
        [
            jnp.broadcast_to(rows4, (64, 16, 128)),
            jnp.broadcast_to(rows5, (2, spaces, 8, 128)).reshape(64, 8, 128),
        ],
        axis=1,
    )
    mine = exchange(outgoing)
    halves = placed_half(first_half_kernel, "first_half", mine)
    weight4, weight5 = placed_half(second_half_kernel, "second_half", other_core(mine), *halves)
    return (output5[None], weight4.transpose(0, 2, 1), weight5.transpose(0, 2, 1))


def solution(mesh):
    placed = (P("space", "dp", None, None), P("space", "dp", None, None), P(), P())
    return jax.shard_map(
        per_device,
        mesh=mesh,
        in_specs=placed,
        out_specs=(P("space", "dp", None, None), P(), P(None, None, "space")),
        check_vma=False,
    )
```
